256 devices in a mesh: ta: 4 (over x), ha: 8 (over y, core), wa: 8 (over z).
Axes of the slice: x: 4, y: 4, z: 8, core: 2. Of those that a mesh axis runs over, the one named last changes fastest.
Arguments:
- latent: bfloat16 [4, 64, 64, 512], P('ta', 'ha', 'wa'), may hold values from -20 to 20, as said below
- norm1_gain: float32 [512], replicated, may hold values from 0.1 to 1.9
- norm1_shift: float32 [512], replicated, may hold values from -3 to 3
- conv1_kernel: bfloat16 [27, 512, 512], P(None, None, 'ta'), may hold values from -0.0546875 to 0.0546875
- conv1_shift: float32 [512], P('ta'), may hold values from -3 to 3
- norm2_gain: float32 [512], replicated, may hold values from 0.1 to 1.9
- norm2_shift: float32 [512], replicated, may hold values from -3 to 3
- conv2_kernel: bfloat16 [27, 512, 512], P(None, None, 'ta'), may hold values from -0.0546875 to 0.0546875
- conv2_shift: float32 [512], P('ta'), may hold values from -3 to 3
- norm3_gain: float32 [512], replicated, may hold values from 0.1 to 1.9
- norm3_shift: float32 [512], replicated, may hold values from -3 to 3
- query_weight: bfloat16 [512, 512], replicated, may hold values from -0.32 to 0.32, as said below
- query_shift: float32 [512], replicated, may hold values from -3 to 3
- key_weight: bfloat16 [512, 512], replicated, may hold values from -0.32 to 0.32, as said below
- value_weight: bfloat16 [512, 512], replicated, may hold values from -0.25 to 0.25
- value_shift: float32 [512], replicated, may hold values from -3 to 3
- output_weight: bfloat16 [512, 512], replicated, may hold values from -0.25 to 0.25
- output_shift: float32 [512], replicated, may hold values from -3 to 3
Outputs:
- block_out: bfloat16 [4, 64, 64, 512], P('ta', 'ha', 'wa')
The draws below stay inside these ranges and needn't reach their ends.
Inputs may be any that keep to these rules, and one draw needn't show every extreme that they name: `latent`: features of order one. `query_weight`: entries of order 512 ** -0.5. `key_weight`: entries of order 512 ** -0.5.
All inputs are finite; a program needn't handle non-finite values.
Results may differ from the reference program's by a relative error of at most 0.017.
Values may be sent and summed in bfloat16 or wider, within the bound.
No kernel may reach another device: no remote copies, remote signals or barrier semaphores. Data moves between devices by JAX's collectives and lax.ppermute only.
A program may use at most 64 MiB of HBM per device.

```python
import math
import jax
import jax.numpy as jnp
from jax import lax

CH = 512
GROUPS = 32
NT = 4
NH = 64
NW = 64


def draw_latent(key, part):
    key = jax.random.fold_in(key, 3)
    noise_key, mean_key, scale_key, offset_key = jax.random.split(key, 4)
    frame_pos = jnp.arange(NT, dtype=jnp.float32) / max(NT - 1, 1)
    row_pos = jnp.arange(NH, dtype=jnp.float32) / max(NH - 1, 1)
    column_pos = jnp.arange(NW, dtype=jnp.float32) / max(NW - 1, 1)
    ramp = frame_pos[:, None, None, None] + row_pos[None, :, None, None] + column_pos[None, None, :, None]
    channel_scale = jnp.exp(jax.random.uniform(scale_key, (CH,), jnp.float32, math.log(0.5), math.log(2.0)))
    channel_mean = jnp.clip(0.5 * jax.random.normal(mean_key, (CH,), jnp.float32), -1.0, 1.0)
    group_offset = jax.random.uniform(offset_key, (GROUPS,), jnp.float32, 0.5, 1.5)
    channel_mean = channel_mean + jnp.repeat(group_offset, CH // GROUPS)
    noise = jnp.clip(jax.random.normal(noise_key, (NT, NH, NW, CH), jnp.float32), -4.0, 4.0)
    level = 0.4 * 3.0 ** (0.5 * ramp)
    values = (noise * channel_scale + channel_mean) * level
    return jnp.clip(values, -19.5, 19.5).astype(jnp.bfloat16)


def draw_query_weight(key, part):
    key = jax.random.fold_in(key, 5)
    fresh = jnp.clip(jax.random.normal(key, (CH, CH), jnp.float32), -4.0, 4.0)
    matrix = fresh / math.sqrt(CH)
    return jnp.clip(matrix, -0.318, 0.318).astype(jnp.bfloat16)


def draw_key_weight(key, part):
    key = jax.random.fold_in(key, 6)
    fresh = jnp.clip(jax.random.normal(key, (CH, CH), jnp.float32), -4.0, 4.0)
    matrix = fresh / math.sqrt(CH)
    return jnp.clip(matrix, -0.318, 0.318).astype(jnp.bfloat16)


def shard_levels(stream_key, shape, shards, least, top_value):
    def one(position, parts):
        heights = jax.random.uniform(jax.random.fold_in(jax.random.fold_in(stream_key, 6), position), (parts,), jnp.float32, least / len(shards), top_value / len(shards))
        return jnp.repeat(jnp.exp(heights), shape[position] // parts).reshape((-1,) + (1,) * (len(shape) - position - 1))

    level = one(*shards[0])
    for cut in shards[1:]:
        level = level * one(*cut)
    return level


def normal_values(own_key, extent, scale, most, pieces=(), kind=jnp.bfloat16):
    array = scale * jax.random.normal(own_key, extent, jnp.float32)
    if pieces:
        array = array * shard_levels(own_key, extent, pieces, -0.22, 0.18)
    return jnp.clip(array, -most, most).astype(kind)


def setup_inputs(seed: int = 0) -> dict:
    seeds = jax.random.split(jax.random.key(seed), 19)
    return {
        "latent": draw_latent(jax.random.fold_in(seeds[18], 71), 0),
        "norm1_gain": jnp.clip(1.0 + 0.18 * jax.random.normal(seeds[1], (CH,), jnp.float32), 0.1, 1.9),
        "norm1_shift": normal_values(seeds[2], (CH,), 0.5, 3.0, (), jnp.float32),
        "conv1_kernel": normal_values(seeds[3], (27, CH, CH), (27 * CH) ** -0.5, 0.0546875, ((2, 4),)),
        "conv1_shift": normal_values(seeds[4], (CH,), 0.5, 3.0, ((0, 4),), jnp.float32),
        "norm2_gain": jnp.clip(1.0 + 0.18 * jax.random.normal(seeds[5], (CH,), jnp.float32), 0.1, 1.9),
        "norm2_shift": normal_values(seeds[6], (CH,), 0.5, 3.0, (), jnp.float32),
        "conv2_kernel": normal_values(seeds[7], (27, CH, CH), (27 * CH) ** -0.5, 0.0546875, ((2, 4),)),
        "conv2_shift": normal_values(seeds[8], (CH,), 0.5, 3.0, ((0, 4),), jnp.float32),
        "norm3_gain": jnp.clip(1.0 + 0.18 * jax.random.normal(seeds[9], (CH,), jnp.float32), 0.1, 1.9),
        "norm3_shift": normal_values(seeds[10], (CH,), 0.5, 3.0, (), jnp.float32),
        "query_weight": draw_query_weight(jax.random.fold_in(seeds[18], 71), 0),
        "query_shift": normal_values(seeds[12], (CH,), 0.5, 3.0, (), jnp.float32),
        "key_weight": draw_key_weight(jax.random.fold_in(seeds[18], 71), 0),
        "value_weight": normal_values(seeds[14], (CH, CH), CH ** -0.5, 0.25),
        "value_shift": normal_values(seeds[15], (CH,), 0.5, 3.0, (), jnp.float32),
        "output_weight": normal_values(seeds[16], (CH, CH), CH ** -0.5, 0.25),
        "output_shift": normal_values(seeds[17], (CH,), 0.5, 3.0, (), jnp.float32),
    }


EPS = 1e-06

def group_norm(values, gain, shift):
    grouped = values.reshape(-1, GROUPS, CH // GROUPS)
    center = lax.optimization_barrier(jnp.mean(grouped, axis=(0, 2), keepdims=True))
    spread = lax.optimization_barrier(jnp.mean(jnp.square(grouped - center), axis=(0, 2), keepdims=True))
    normed = ((grouped - center) * lax.rsqrt(spread + EPS)).reshape(values.shape)
    return normed * gain + shift

def causal_conv(inputs, kernel, shift):
    padded = jnp.concatenate([inputs[:1], inputs[:1], inputs], axis=0)
    filters = kernel.reshape(3, 3, 3, CH, CH)
    result = lax.conv_general_dilated(padded[None], filters, (1, 1, 1), [(0, 0), (1, 1), (1, 1)], dimension_numbers=('NDHWC', 'DHWIO', 'NDHWC'), preferred_element_type=jnp.float32)[0]
    return result + shift

def attend_frame(operands):
    query, keys, values = operands
    scores = jnp.dot(query, keys.T, preferred_element_type=jnp.float32) * CH ** (-0.5)
    highest = lax.optimization_barrier(jnp.max(scores, axis=1, keepdims=True))
    weights = jnp.exp(scores - highest)
    total = lax.optimization_barrier(jnp.sum(weights, axis=1, keepdims=True))
    mixed = jnp.dot(weights.astype(jnp.bfloat16), values, preferred_element_type=jnp.float32) / total
    return mixed.astype(jnp.bfloat16)

def reference(latent, norm1_gain, norm1_shift, conv1_kernel, conv1_shift, norm2_gain, norm2_shift, conv2_kernel, conv2_shift, norm3_gain, norm3_shift, query_weight, query_shift, key_weight, value_weight, value_shift, output_weight, output_shift):
    first_act = jax.nn.silu(group_norm(latent.astype(jnp.float32), norm1_gain, norm1_shift)).astype(jnp.bfloat16)
    hidden = causal_conv(first_act, conv1_kernel, conv1_shift).astype(jnp.bfloat16)
    second_act = jax.nn.silu(group_norm(hidden.astype(jnp.float32), norm2_gain, norm2_shift)).astype(jnp.bfloat16)
    branch = causal_conv(second_act, conv2_kernel, conv2_shift).astype(jnp.bfloat16)
    residual = (latent.astype(jnp.float32) + branch.astype(jnp.float32)).astype(jnp.bfloat16)
    normed = group_norm(residual.astype(jnp.float32), norm3_gain, norm3_shift).astype(jnp.bfloat16)
    flat = normed.reshape(-1, CH)
    queries = (jnp.dot(flat, query_weight, preferred_element_type=jnp.float32) + query_shift).astype(jnp.bfloat16)
    keys = jnp.dot(flat, key_weight, preferred_element_type=jnp.float32).astype(jnp.bfloat16)
    values = (jnp.dot(flat, value_weight, preferred_element_type=jnp.float32) + value_shift).astype(jnp.bfloat16)
    frame_shape = (NT, NH * NW, CH)
    attended = lax.map(attend_frame, (queries.reshape(frame_shape), keys.reshape(frame_shape), values.reshape(frame_shape))).reshape(-1, CH)
    block_out = residual.astype(jnp.float32).reshape(-1, CH) + jnp.dot(attended, output_weight, preferred_element_type=jnp.float32) + output_shift
    return block_out.astype(jnp.bfloat16).reshape(NT, NH, NW, CH)
```

```python
import functools

import jax
import jax.numpy as jnp
from jax import lax
from jax.experimental import pallas as pl
from jax.experimental.pallas import tpu as pltpu
from jax.sharding import Mesh, PartitionSpec as P

GROUPS = 32
EPS = 1e-06
HA = ("y", "core")
BF = jnp.bfloat16
F32 = jnp.float32
LANES = 128
LIMIT = 32 * 1024 * 1024
VMEM = pl.BlockSpec(memory_space=pltpu.VMEM)


def lane_in_group(shape):
    return lax.broadcasted_iota(jnp.int32, shape, 1) & 15


def segment_sum(x):
    lane = lane_in_group(x.shape)
    for bit in (1, 2, 4, 8):
        after = pltpu.roll(x, LANES - bit, 1)
        before = pltpu.roll(x, bit, 1)
        x = x + jnp.where((lane & bit) == 0, after, before)
    return x


def rows8(x):
    return jnp.broadcast_to(x, (8, LANES))


def cell_rows(rows, pitch):
    index = lax.broadcasted_iota(jnp.int32, (rows, LANES), 0)
    row = (index * {10: 52429, 12: 43691}[pitch]) >> 19
    return row, index - row * pitch


def encode(out_ref, stats):
    lane = lane_in_group((8, LANES))
    row = jnp.zeros((8, LANES), F32)
    for block, mean, spread in stats:
        row = jnp.where(lane == block, mean, row)
        row = jnp.where(lane == block + 4, spread, row)
    out_ref[...] = jnp.broadcast_to(row[0:1][None], out_ref.shape)


def thirds(x):
    high = x.astype(BF).astype(F32)
    middle = (x - high).astype(BF).astype(F32)
    return high, middle, x - high - middle


def pack_stats(mean, spread):
    row = lax.broadcasted_iota(jnp.int32, mean.shape, 0)
    packed = jnp.zeros(mean.shape, F32)
    for k, piece in enumerate(thirds(mean) + thirds(spread)):
        packed = jnp.where(row == k, piece, packed)
    return packed.astype(BF)


def unpack_stats(packed):
    x = packed.astype(F32)
    return x[0:1] + x[1:2] + x[2:3], x[3:4] + x[4:5] + x[5:6]


def merge_stats(stats):
    scale = 1.0 / len(stats)
    middle = sum(mean for mean, _ in stats) * scale
    spread = sum(spread + (mean - middle) * (mean - middle) for mean, spread in stats) * scale
    return middle, spread


def all_rows(x):
    return jnp.broadcast_to(x, (8, x.shape[1]))


def channel_stats(x, keep, count):
    mean = jnp.sum(x, axis=0, keepdims=True) * (1.0 / count)
    deviation = x - mean
    if keep is not None:
        deviation = jnp.where(keep, deviation, 0.0)
    spread = jnp.sum(deviation * deviation, axis=0, keepdims=True) * (1.0 / count)
    return group_stats(mean, spread)


def group_stats(mean, spread):
    mean, spread = rows8(mean), rows8(spread)
    middle = segment_sum(mean) * (1.0 / 16)
    off = mean - middle
    return middle, segment_sum(spread + off * off) * (1.0 / 16)


def tile_stats(rows_ref):
    rows = rows_ref[...].reshape(rows_ref.shape[0], LANES)
    count = rows.shape[0]
    mean = jnp.sum(rows, axis=0, keepdims=True) * (1.0 / count)
    off = rows - mean
    between = jnp.sum(off * off, axis=0, keepdims=True) * (1.0 / count)
    return rows8(mean), rows8(between)


def block_stats(mean, between, block):
    lane = lane_in_group((8, LANES))
    middle = segment_sum(jnp.where(lane == block, mean, 0.0))
    spread = segment_sum(jnp.where(lane == block + 4, mean, jnp.where(lane == block, between, 0.0)))
    return middle[0:1], lax.rsqrt(spread[0:1] + EPS)


def decode(rows_ref, small_ref, at):
    mean, between = tile_stats(rows_ref)
    result = []
    for block in range(4):
        middle, inverse = block_stats(mean, between, block)
        gain, shift = gain_and_shift(small_ref, at, block)
        result.append((middle, inverse * gain, shift))
    return result


def gain_and_shift(small_ref, at, block):
    return small_ref[at + block : at + block + 1, :], small_ref[at + 4 + block : at + 5 + block, :]


def wide(small_ref, at):
    return jnp.concatenate([small_ref[at + b : at + b + 1, :] for b in range(4)], axis=1)


def silu(v):
    half = 0.5 * v
    return half + half * jnp.tanh(half)


def turned(ta, s):
    return lax.rem(ta - s + 4, 4)


def first_kernel(latent_ref, out_ref):
    out_ref[...] = latent_ref[...]


def frame_moments_kernel(s0, s1, s2, s3, out_ref, first_ref, last_ref):
    slots = (s0, s1, s2, s3)
    stats = []
    for block in range(4):
        x = jnp.concatenate(
            [ref[:, block * LANES : (block + 1) * LANES].astype(F32) for ref in slots], axis=0
        )
        stats.append((block,) + channel_stats(x, None, x.shape[0]))
    encode(out_ref, stats)
    for s, ref in enumerate(slots):
        first_ref[s] = ref[0:16, :]
        last_ref[s] = ref[48:64, :]


def columns_kernel(s0, s1, s2, s3, top_ref, bottom_ref, first_ref, last_ref, tall, sides):
    for s, ref in enumerate((s0, s1, s2, s3)):
        for b in range(4):
            lanes = slice(b * LANES, (b + 1) * LANES)
            tall[b, 0:16, :] = top_ref[s, :, lanes].astype(F32)
            tall[b, 16:80, :] = ref[:, lanes].astype(F32)
            tall[b, 80:96, :] = bottom_ref[s, :, lanes].astype(F32)
            for k, out_ref in ((0, first_ref), (6, last_ref)):
                for j in range(2):
                    sides[b, 12 * j : 12 * j + 12, :] = tall[b, pl.ds(j + k, 12, stride=8), :]
                out_ref[s, :, lanes] = sides[b].astype(BF)


def activate_kernel(grid, hidden_ref, rows_ref, small_ref, out_ref):
    ta = lax.axis_index("ta")
    middle, inverse = block_stats(*tile_stats(rows_ref), 0)
    scale = inverse * small_ref[pl.ds(8 + ta, 1), :]
    shift = small_ref[pl.ds(12 + ta, 1), :]
    keep = inside(8 * lax.axis_index(HA) - 1, 8 * lax.axis_index("z") - 1, 104, 10, grid)
    for f in range(4):
        v = (hidden_ref[f].astype(F32) - middle) * scale + shift
        out_ref[f] = jnp.where(keep, silu(v), 0.0).astype(BF)


def residual_kernel(s0, s1, s2, s3, out_ref, parts):
    for s, ref in enumerate((s0, s1, s2, s3)):
        parts[turned(lax.axis_index("ta"), s)] = ref[...]
    out_ref[...] = jnp.concatenate([parts[b] for b in range(4)], axis=1)


def merge_kernel(*refs):
    slots, out_ref = refs[:-1], refs[-1]
    room = out_ref.shape[0] - 8
    middle, spread = merge_stats([unpack_stats(ref[64:72, :]) for ref in slots])
    for s in range(room // 64):
        out_ref[64 * s : 64 * s + 64, :] = slots[s][0:64, :]
    out_ref[room : room + 8, :] = pack_stats(all_rows(middle), all_rows(spread))


def convolve(lhs, weights, product, frame_rows, pitch, out_rows):
    for pair in ((0, 1), (2, 3), (4, 5), (6, 7), (8,)):
        rhs = jnp.concatenate(
            [jnp.concatenate([weights[9 * d + s] for s in pair], axis=1) for d in range(3)], axis=0
        )
        lane = pair[0] * LANES
        product[0 : 4 * frame_rows, lane : lane + rhs.shape[1]] = jnp.dot(
            lhs[...], rhs, preferred_element_type=F32
        )
    totals = []
    for f in range(4):
        total = None
        for s in range(9):
            at = f * frame_rows + pitch * (s // 3) + s % 3
            piece = product[at : at + out_rows, s * LANES : (s + 1) * LANES]
            total = piece if total is None else total + piece
        totals.append(total)
    return totals


def inside(base_row, base_column, rows, pitch, grid):
    row, column = cell_rows(rows, pitch)
    row, column = row + base_row, column + base_column
    return (row >= 0) & (row < grid[0]) & (column >= 0) & (column < grid[1])


def rimmed_kernel(
    grid,
    s0,
    s1,
    s2,
    s3,
    top_ref,
    bottom_ref,
    left_ref,
    right_ref,
    rows_ref,
    small_ref,
    lhs_ref,
    own_ref,
    frames,
    tile,
    sides,
):
    ta = lax.axis_index("ta")
    coefficients = decode(rows_ref, small_ref, 0)
    keep = inside(8 * lax.axis_index(HA) - 2, 8 * lax.axis_index("z") - 2, 144, 12, grid)
    for s, ref in enumerate((s0, s1, s2, s3)):
        frames[turned(ta, s)] = ref[...]
    for frame in range(4):
        s = turned(ta, frame)
        own = jnp.zeros((64, LANES), F32)
        for b in range(4):
            lanes = slice(b * LANES, (b + 1) * LANES)
            middle = frames[frame, :, lanes].astype(F32)
            own = jnp.where(ta == b, middle, own)
            top, bottom = top_ref[s, :, lanes].astype(F32), bottom_ref[s, :, lanes].astype(F32)
            for r in range(12):
                if r < 2:
                    piece = top[8 * r : 8 * r + 8]
                elif r < 10:
                    piece = middle[8 * (r - 2) : 8 * (r - 2) + 8]
                else:
                    piece = bottom[8 * (r - 10) : 8 * (r - 10) + 8]
                tile[b, 12 * r + 2 : 12 * r + 10, :] = piece
            for k, side_ref in ((0, left_ref), (10, right_ref)):
                sides[b] = side_ref[s, :, lanes].astype(F32)
                for j in range(2):
                    tile[b, pl.ds(j + k, 12, stride=12), :] = sides[b, 12 * j : 12 * j + 12, :]
            mean, scale, shift = coefficients[b]
            v = (tile[b] - mean) * scale + shift
            act = jnp.where(keep, silu(v), 0.0).astype(BF)
            for f in range(4):
                for d in range(3):
                    if max(f + d - 2, 0) == frame:
                        lane = (4 * d + b) * LANES
                        lhs_ref[f * 144 : (f + 1) * 144, lane : lane + LANES] = act
        own_ref[frame] = own.astype(BF)


def first_conv_kernel(lhs, small_ref, kernel_ref, out_ref, moments_ref, product, wide_rows, tight_rows):
    totals = convolve(lhs, kernel_ref, product, 144, 12, 120)
    row, column = cell_rows(104, 10)
    keep = (row >= 1) & (row <= 8) & (column >= 1) & (column <= 8)
    bias = small_ref[36:37, :]
    kept = []
    for f in range(4):
        wide_rows[f] = totals[f] + bias
        for r in range(10):
            tight_rows[f, 10 * r : 10 * r + 10, :] = wide_rows[f, 12 * r : 12 * r + 10, :]
        tight_rows[f, 100:104, :] = jnp.zeros((4, LANES), F32)
        hidden = tight_rows[f].astype(BF)
        out_ref[f] = hidden
        kept.append(jnp.where(keep, hidden.astype(F32), 0.0))
    mean = sum(jnp.sum(x, axis=0, keepdims=True) for x in kept) * (1.0 / 256)
    squares = [jnp.square(jnp.where(keep, x - mean, 0.0)) for x in kept]
    spread = sum(jnp.sum(x, axis=0, keepdims=True) for x in squares) * (1.0 / 256)
    encode(moments_ref, [(0,) + group_stats(mean, spread)])


def second_conv_kernel(
    s0,
    s1,
    s2,
    s3,
    small_ref,
    own_ref,
    kernel_ref,
    out0,
    out1,
    out2,
    out3,
    lhs,
    product,
    wide_rows,
    parts,
):
    ta = lax.axis_index("ta")
    for s, ref in enumerate((s0, s1, s2, s3)):
        block = turned(ta, s)
        for f in range(4):
            for d in range(3):
                lane = pl.multiple_of((4 * d + block) * LANES, LANES)
                lhs[f * 112 : f * 112 + 104, pl.ds(lane, LANES)] = ref[max(f + d - 2, 0)]
    totals = convolve(lhs, kernel_ref, product, 112, 10, 80)
    bias = small_ref[37:38, :]
    tiles = []
    for f in range(4):
        wide_rows[f] = totals[f] + bias
        branch = jnp.concatenate([wide_rows[f, 10 * r : 10 * r + 8, :] for r in range(8)], axis=0)
        branch = branch.astype(BF).astype(F32)
        residual = (own_ref[f].astype(F32) + branch).astype(BF)
        parts[f] = residual
        tiles.append(residual.astype(F32))
    mean, spread = channel_stats(jnp.concatenate(tiles, axis=0), None, 256)
    packed = pack_stats(mean, spread)
    for s, ref in enumerate((out0, out1, out2, out3)):
        ref[0:64, :] = parts[lax.rem(ta + s, 4)]
        ref[64:72, :] = packed


def normalise(x, coefficients):
    parts = []
    for b, (mean, scale, shift) in enumerate(coefficients):
        part = x[:, b * LANES : (b + 1) * LANES].astype(F32)
        parts.append(((part - mean) * scale + shift).astype(BF))
    return jnp.concatenate(parts, axis=1)


def attention_kernel(*refs):
    asked, told = refs[:4], refs[4:6]
    small_ref, query_ref, key_ref = refs[6:9]
    outs, normed = refs[9:13], refs[13]
    middle, spread = merge_stats([unpack_stats(ref[512:520, :]) for ref in told])
    inverse = lax.rsqrt(spread + EPS)
    coefficients = []
    for b in range(4):
        lanes = slice(b * LANES, (b + 1) * LANES)
        gain, shift = gain_and_shift(small_ref, 16, b)
        coefficients.append((middle[:, lanes], inverse[:, lanes] * gain, shift))
    normed_q = normalise(jnp.concatenate([ref[0:64, :] for ref in asked], axis=0), coefficients)
    for k, ref in enumerate(told):
        normed[512 * k : 512 * k + 512, :] = normalise(ref[0:512, :], coefficients)
    queries = jnp.dot(normed_q, query_ref[...], preferred_element_type=F32) + wide(small_ref, 24)
    folded = lax.dot_general(
        queries.astype(BF), key_ref[...], (((1,), (1,)), ((), ())), preferred_element_type=F32
    ).astype(BF)
    scores = lax.dot_general(
        folded, normed[...], (((1,), (1,)), ((), ())), preferred_element_type=F32
    ) * 512 ** (-0.5)
    highest = jnp.max(scores, axis=1, keepdims=True)
    weights = jnp.exp(scores - highest)
    total = jnp.sum(weights, axis=1, keepdims=True)
    mixed = jnp.dot(weights.astype(BF), normed[...], preferred_element_type=F32) / total
    level = highest + jnp.log(total)
    top, middle, low = thirds(level)
    lane = lax.broadcasted_iota(jnp.int32, (256, LANES), 1)
    tail = jnp.where(lane == 0, top, jnp.where(lane == 1, middle, jnp.where(lane == 2, low, 0.0)))
    for s, ref in enumerate(outs):
        ref[:, 0:512] = mixed[64 * s : 64 * s + 64].astype(BF)
        ref[:, 512:640] = tail[64 * s : 64 * s + 64].astype(BF)


def finish_kernel(b0, b1, b2, b3, residual_ref, small_ref, value_ref, output_ref, out_ref):
    backs = [ref[...].astype(F32) for ref in (b0, b1, b2, b3)]
    levels = [jnp.sum(back[:, 512:640], axis=1, keepdims=True) for back in backs]
    highest = functools.reduce(jnp.maximum, levels)
    shares = [jnp.exp(level - highest) for level in levels]
    inverse = 1.0 / sum(shares)
    mean_normed = sum(back[:, 0:512] * (share * inverse) for back, share in zip(backs, shares))
    attended = jnp.dot(mean_normed.astype(BF), value_ref[...], preferred_element_type=F32)
    attended = (attended + wide(small_ref, 28)).astype(BF)
    mixed = jnp.dot(attended, output_ref[...], preferred_element_type=F32)
    out_ref[...] = (residual_ref[0:64, :].astype(F32) + mixed + wide(small_ref, 32)).astype(BF)


def call(kernel, out_shape, specs, scratch, flops, *args):
    shapes = out_shape if isinstance(out_shape, tuple) else (out_shape,)
    moved = sum(a.size * a.dtype.itemsize for a in args) + sum(
        s.size * jnp.dtype(s.dtype).itemsize for s in shapes
    )
    return pl.pallas_call(
        kernel,
        out_shape=out_shape,
        in_specs=specs,
        out_specs=tuple(VMEM for _ in shapes) if isinstance(out_shape, tuple) else VMEM,
        scratch_shapes=scratch,
        compiler_params=pltpu.CompilerParams(vmem_limit_bytes=LIMIT),
        cost_estimate=pl.CostEstimate(flops=flops, bytes_accessed=moved, transcendentals=0),
    )(*args)


def ring(count, step):
    return [(i, (i + step) % count) for i in range(count)]


def long_first(count):
    return sorted(range(1, count), key=lambda s: -min(s, count - s))


def spread_out(blocks, axis, sign=1):
    count = lax.axis_size(axis)
    arrived = {0: blocks[0]}
    for s in long_first(count):
        arrived[s] = lax.ppermute(blocks[s], axis, ring(count, sign * s))
    return [arrived[s] for s in range(count)]


def around(block, axis):
    return spread_out([block] * lax.axis_size(axis), axis)


def relayed(block, axis):
    count = lax.axis_size(axis)
    after = {step: lax.ppermute(block, axis, ring(count, step)) for step in (2, 1, -1, -2)}
    further = [lax.ppermute(after[step], axis, ring(count, move)) for step, move in ((1, 2), (-1, -2), (2, 2))]
    return [block, *after.values(), *further]


def both_sides(low, high, axis):
    count = lax.axis_size(axis)
    return lax.ppermute(high, axis, ring(count, 1)), lax.ppermute(low, axis, ring(count, -1))


def over_tiles(rows):
    return lax.all_to_all(rows, HA + ("z",), split_axis=0, concat_axis=0, tiled=True)


def body(
    latent,
    norm1_gain,
    norm1_shift,
    conv1_kernel,
    conv1_shift,
    norm2_gain,
    norm2_shift,
    conv2_kernel,
    conv2_shift,
    norm3_gain,
    norm3_shift,
    query_weight,
    query_shift,
    key_weight,
    value_weight,
    value_shift,
    output_weight,
    output_shift,
):
    _, height, width, channels = latent.shape
    cells = height * width
    tiles = lax.axis_size(HA) * lax.axis_size("z")
    grid = (lax.axis_size(HA) * height, lax.axis_size("z") * width)
    vectors = [norm1_gain, norm1_shift, norm2_gain, norm2_shift, norm3_gain, norm3_shift]
    vectors += [query_shift, value_shift, output_shift, conv1_shift, conv2_shift]
    small = jnp.concatenate(vectors).reshape(-1, LANES)

    def bf(*shape):
        return jax.ShapeDtypeStruct(shape, BF)

    rows = jax.ShapeDtypeStruct((tiles, 1, LANES), F32)

    slots = around(latent[0].reshape(cells, channels), "ta")
    slots[0] = call(first_kernel, bf(cells, channels), [VMEM], [], 4 * 10**9, slots[0])
    rows1, low, high = call(
        frame_moments_kernel, (rows, bf(4, 16, channels), bf(4, 16, channels)), [VMEM] * 4, [], 10**6, *slots
    )
    top, bottom = both_sides(low, high, HA)
    rows1 = over_tiles(rows1)
    low, high = call(
        columns_kernel,
        (bf(4, 24, channels), bf(4, 24, channels)),
        [VMEM] * 6,
        [pltpu.VMEM((4, 96, LANES), F32), pltpu.VMEM((4, 24, LANES), F32)],
        10**6,
        *slots,
        top,
        bottom,
    )
    left, right = both_sides(low, high, "z")
    lhs, own = call(
        functools.partial(rimmed_kernel, grid),
        (bf(576, 1536), bf(4, cells, LANES)),
        [VMEM] * 10,
        [pltpu.VMEM((4, cells, channels), BF), pltpu.VMEM((4, 144, LANES), F32), pltpu.VMEM((4, 24, LANES), F32)],
        4 * 10**9,
        *slots,
        top,
        bottom,
        left,
        right,
        rows1,
        small,
    )
    hidden, rows2 = call(
        first_conv_kernel,
        (bf(4, 104, LANES), rows),
        [VMEM] * 3,
        [
            pltpu.VMEM((584, 1152), F32),
            pltpu.VMEM((4, 120, LANES), F32),
            pltpu.VMEM((4, 104, LANES), F32),
        ],
        2 * 10**9,
        lhs,
        small,
        conv1_kernel,
    )

    act = call(
        functools.partial(activate_kernel, grid),
        bf(4, 104, LANES),
        [VMEM] * 3,
        [],
        4 * 10**9,
        hidden,
        over_tiles(rows2),
        small,
    )
    parts = call(
        second_conv_kernel,
        (bf(cells + 8, LANES),) * 4,
        [VMEM] * 7,
        [
            pltpu.VMEM((448, 1536), BF),
            pltpu.VMEM((448, 1152), F32),
            pltpu.VMEM((4, 80, LANES), F32),
            pltpu.VMEM((4, cells, LANES), BF),
        ],
        2 * 10**9,
        *around(act, "ta"),
        small,
        own,
        conv2_kernel,
    )

    residual = call(
        residual_kernel,
        bf(cells + 8, channels),
        [VMEM] * 4,
        [pltpu.VMEM((4, cells + 8, LANES), BF)],
        10**6,
        *spread_out(parts, "ta"),
    )
    asked = around(residual, "y")
    told = call(merge_kernel, bf(cells + 8, channels), [VMEM] * 4, [], 10**6, *asked)
    told = call(merge_kernel, bf(8 * cells + 8, channels), [VMEM] * 8, [], 10**6, *relayed(told, "z"))
    packed = call(
        attention_kernel,
        (bf(cells, channels + LANES),) * 4,
        [VMEM] * 9,
        [pltpu.VMEM((1024, channels), BF)],
        10**9,
        *asked,
        told,
        lax.ppermute(told, "core", ring(2, 1)),
        small,
        query_weight,
        key_weight,
    )

    block_out = call(
        finish_kernel,
        bf(cells, channels),
        [VMEM] * 8,
        [],
        10**8,
        *spread_out(packed, "y", -1),
        residual,
        small,
        value_weight,
        output_weight,
    )
    return block_out.reshape(latent.shape)


def solution(mesh):
    frames, rows, columns = mesh.devices.shape
    split = Mesh(mesh.devices.reshape(frames, rows // 2, 2, columns), ("ta", "y", "core", "z"))
    tile = P("ta", HA, "z", None)
    kernel, shift = P(None, None, "ta"), P("ta")
    in_specs = (tile, P(), P(), kernel, shift, P(), P(), kernel, shift) + (P(),) * 9
    return jax.shard_map(body, mesh=split, in_specs=in_specs, out_specs=tile, check_vma=False)
```

```python
import functools

import jax
import jax.numpy as jnp
from jax import lax
from jax.experimental import pallas as pl
from jax.experimental.pallas import tpu as pltpu
from jax.sharding import Mesh, PartitionSpec as P

GROUPS = 32
EPS = 1e-06
HA = ("y", "core")
BF = jnp.bfloat16
F32 = jnp.float32
LANES = 128
LIMIT = 32 * 1024 * 1024
PAIRS = ((0, 1), (2, 3), (4, 5), (6, 7), (8,))
VMEM = pl.BlockSpec(memory_space=pltpu.VMEM)


def lane_in_group(shape):
    return lax.broadcasted_iota(jnp.int32, shape, 1) & 15


def segment_sum(x):
    lane = lane_in_group(x.shape)
    for bit in (1, 2, 4, 8):
        after = pltpu.roll(x, LANES - bit, 1)
        before = pltpu.roll(x, bit, 1)
        x = x + jnp.where((lane & bit) == 0, after, before)
    return x


def rows8(x):
    return jnp.broadcast_to(x, (8, LANES))


def cell_rows(rows, pitch):
    index = lax.broadcasted_iota(jnp.int32, (rows, LANES), 0)
    row = (index * {10: 52429, 12: 43691}[pitch]) >> 19
    return row, index - row * pitch


def encode(out_ref, stats):
    lane = lane_in_group((8, LANES))
    row = jnp.zeros((8, LANES), F32)
    for block, mean, spread in stats:
        row = jnp.where(lane == block, mean, row)
        row = jnp.where(lane == block + 4, spread, row)
    out_ref[...] = jnp.broadcast_to(row[0:1][None], out_ref.shape)


def thirds(x):
    high = x.astype(BF).astype(F32)
    middle = (x - high).astype(BF).astype(F32)
    return high, middle, x - high - middle


def pack_stats(mean, spread):
    row = lax.broadcasted_iota(jnp.int32, mean.shape, 0)
    packed = jnp.zeros(mean.shape, F32)
    for k, piece in enumerate(thirds(mean) + thirds(spread)):
        packed = jnp.where(row == k, piece, packed)
    return packed.astype(BF)


def unpack_stats(packed):
    x = packed.astype(F32)
    return x[0:1] + x[1:2] + x[2:3], x[3:4] + x[4:5] + x[5:6]


def merge_stats(stats):
    scale = 1.0 / len(stats)
    middle = sum(mean for mean, _ in stats) * scale
    spread = sum(spread + (mean - middle) * (mean - middle) for mean, spread in stats) * scale
    return middle, spread


def all_rows(x):
    return jnp.broadcast_to(x, (8, x.shape[1]))


def channel_stats(x, keep, count):
    mean = jnp.sum(x, axis=0, keepdims=True) * (1.0 / count)
    deviation = x - mean
    if keep is not None:
        deviation = jnp.where(keep, deviation, 0.0)
    spread = jnp.sum(deviation * deviation, axis=0, keepdims=True) * (1.0 / count)
    return group_stats(mean, spread)


def group_stats(mean, spread):
    mean, spread = rows8(mean), rows8(spread)
    middle = segment_sum(mean) * (1.0 / 16)
    off = mean - middle
    return middle, segment_sum(spread + off * off) * (1.0 / 16)


def tile_stats(rows_ref):
    rows = rows_ref[...].reshape(rows_ref.shape[0], LANES)
    count = rows.shape[0]
    mean = jnp.sum(rows, axis=0, keepdims=True) * (1.0 / count)
    off = rows - mean
    between = jnp.sum(off * off, axis=0, keepdims=True) * (1.0 / count)
    return rows8(mean), rows8(between)


def block_stats(mean, between, block):
    lane = lane_in_group((8, LANES))
    middle = segment_sum(jnp.where(lane == block, mean, 0.0))
    spread = segment_sum(jnp.where(lane == block + 4, mean, jnp.where(lane == block, between, 0.0)))
    return middle[0:1], lax.rsqrt(spread[0:1] + EPS)


def decode(rows_ref, small_ref, at):
    mean, between = tile_stats(rows_ref)
    result = []
    for block in range(4):
        middle, inverse = block_stats(mean, between, block)
        gain, shift = gain_and_shift(small_ref, at, block)
        result.append((middle, inverse * gain, shift))
    return result


def gain_and_shift(small_ref, at, block):
    return small_ref[at + block : at + block + 1, :], small_ref[at + 4 + block : at + 5 + block, :]


def wide(small_ref, at):
    return jnp.concatenate([small_ref[at + b : at + b + 1, :] for b in range(4)], axis=1)


def silu(v):
    half = 0.5 * v
    return half + half * jnp.tanh(half)


def turned(ta, s):
    return lax.rem(ta - s + 4, 4)


def first_kernel(latent_ref, out_ref):
    out_ref[...] = latent_ref[...]


def frame_moments_kernel(s0, s1, s2, s3, out_ref, first_ref, last_ref):
    slots = (s0, s1, s2, s3)
    stats = []
    for block in range(4):
        x = jnp.concatenate(
            [ref[:, block * LANES : (block + 1) * LANES].astype(F32) for ref in slots], axis=0
        )
        stats.append((block,) + channel_stats(x, None, x.shape[0]))
    encode(out_ref, stats)
    for s, ref in enumerate(slots):
        first_ref[s] = ref[0:16, :]
        last_ref[s] = ref[48:64, :]


def columns_kernel(s0, s1, s2, s3, top_ref, bottom_ref, first_ref, last_ref, tall, sides):
    for s, ref in enumerate((s0, s1, s2, s3)):
        for b in range(4):
            lanes = slice(b * LANES, (b + 1) * LANES)
            tall[b, 0:16, :] = top_ref[s, :, lanes].astype(F32)
            tall[b, 16:80, :] = ref[:, lanes].astype(F32)
            tall[b, 80:96, :] = bottom_ref[s, :, lanes].astype(F32)
            for k, out_ref in ((0, first_ref), (6, last_ref)):
                for j in range(2):
                    sides[b, 12 * j : 12 * j + 12, :] = tall[b, pl.ds(j + k, 12, stride=8), :]
                out_ref[s, :, lanes] = sides[b].astype(BF)


def activate_kernel(grid, hidden_ref, rows_ref, small_ref, out_ref):
    ta = lax.axis_index("ta")
    middle, inverse = block_stats(*tile_stats(rows_ref), 0)
    scale = inverse * small_ref[pl.ds(8 + ta, 1), :]
    shift = small_ref[pl.ds(12 + ta, 1), :]
    keep = inside(8 * lax.axis_index(HA) - 1, 8 * lax.axis_index("z") - 1, 104, 10, grid)
    for f in range(4):
        v = (hidden_ref[f].astype(F32) - middle) * scale + shift
        out_ref[f] = jnp.where(keep, silu(v), 0.0).astype(BF)


def residual_kernel(s0, s1, s2, s3, out_ref, parts):
    for s, ref in enumerate((s0, s1, s2, s3)):
        parts[turned(lax.axis_index("ta"), s)] = ref[...]
    out_ref[...] = jnp.concatenate([parts[b] for b in range(4)], axis=1)


def merge_kernel(*refs):
    slots, out_ref = refs[:-1], refs[-1]
    room = out_ref.shape[0] - 8
    middle, spread = merge_stats([unpack_stats(ref[64:72, :]) for ref in slots])
    for s in range(room // 64):
        out_ref[64 * s : 64 * s + 64, :] = slots[s][0:64, :]
    out_ref[room : room + 8, :] = pack_stats(all_rows(middle), all_rows(spread))


def convolve(lhs, weights, product, frame_rows, pitch, out_rows):
    for pair in PAIRS:
        rhs = jnp.concatenate(
            [jnp.concatenate([weights[9 * d + s] for s in pair], axis=1) for d in range(3)], axis=0
        )
        lane = pair[0] * LANES
        product[0 : 4 * frame_rows, lane : lane + rhs.shape[1]] = jnp.dot(
            lhs[...], rhs, preferred_element_type=F32
        )
    return shifted_sums(product, frame_rows, pitch, out_rows)


def shifted_sums(product, frame_rows, pitch, out_rows):
    totals = []
    for f in range(4):
        total = None
        for s in range(9):
            at = f * frame_rows + pitch * (s // 3) + s % 3
            piece = product[at : at + out_rows, s * LANES : (s + 1) * LANES]
            total = piece if total is None else total + piece
        totals.append(total)
    return totals


def inside(base_row, base_column, rows, pitch, grid):
    row, column = cell_rows(rows, pitch)
    row, column = row + base_row, column + base_column
    return (row >= 0) & (row < grid[0]) & (column >= 0) & (column < grid[1])


def rimmed_kernel(
    grid,
    s0,
    s1,
    s2,
    s3,
    top_ref,
    bottom_ref,
    left_ref,
    right_ref,
    rows_ref,
    small_ref,
    lhs_ref,
    own_ref,
    frames,
    tile,
    sides,
):
    ta = lax.axis_index("ta")
    coefficients = decode(rows_ref, small_ref, 0)
    keep = inside(8 * lax.axis_index(HA) - 2, 8 * lax.axis_index("z") - 2, 144, 12, grid)
    for s, ref in enumerate((s0, s1, s2, s3)):
        frames[turned(ta, s)] = ref[...]
    for frame in range(4):
        s = turned(ta, frame)
        own = jnp.zeros((64, LANES), F32)
        for b in range(4):
            lanes = slice(b * LANES, (b + 1) * LANES)
            middle = frames[frame, :, lanes].astype(F32)
            own = jnp.where(ta == b, middle, own)
            top, bottom = top_ref[s, :, lanes].astype(F32), bottom_ref[s, :, lanes].astype(F32)
            for r in range(12):
                if r < 2:
                    piece = top[8 * r : 8 * r + 8]
                elif r < 10:
                    piece = middle[8 * (r - 2) : 8 * (r - 2) + 8]
                else:
                    piece = bottom[8 * (r - 10) : 8 * (r - 10) + 8]
                tile[b, 12 * r + 2 : 12 * r + 10, :] = piece
            for k, side_ref in ((0, left_ref), (10, right_ref)):
                sides[b] = side_ref[s, :, lanes].astype(F32)
                for j in range(2):
                    tile[b, pl.ds(j + k, 12, stride=12), :] = sides[b, 12 * j : 12 * j + 12, :]
            mean, scale, shift = coefficients[b]
            v = (tile[b] - mean) * scale + shift
            act = jnp.where(keep, silu(v), 0.0).astype(BF)
            for f in range(4):
                for d in range(3):
                    if max(f + d - 2, 0) == frame:
                        lane = (4 * d + b) * LANES
                        lhs_ref[f * 144 : (f + 1) * 144, lane : lane + LANES] = act
        own_ref[frame] = own.astype(BF)


def first_conv_kernel(lhs, small_ref, kernel_ref, out_ref, moments_ref, product, wide_rows, tight_rows):
    totals = convolve(lhs, kernel_ref, product, 144, 12, 120)
    row, column = cell_rows(104, 10)
    keep = (row >= 1) & (row <= 8) & (column >= 1) & (column <= 8)
    bias = small_ref[36:37, :]
    kept = []
    for f in range(4):
        wide_rows[f] = totals[f] + bias
        for r in range(10):
            tight_rows[f, 10 * r : 10 * r + 10, :] = wide_rows[f, 12 * r : 12 * r + 10, :]
        tight_rows[f, 100:104, :] = jnp.zeros((4, LANES), F32)
        hidden = tight_rows[f].astype(BF)
        out_ref[f] = hidden
        kept.append(jnp.where(keep, hidden.astype(F32), 0.0))
    mean = sum(jnp.sum(x, axis=0, keepdims=True) for x in kept) * (1.0 / 256)
    squares = [jnp.square(jnp.where(keep, x - mean, 0.0)) for x in kept]
    spread = sum(jnp.sum(x, axis=0, keepdims=True) for x in squares) * (1.0 / 256)
    encode(moments_ref, [(0,) + group_stats(mean, spread)])


def add_blocks(refs, shifts, kernel_ref, lhs, product, before=None):
    ta = lax.axis_index("ta")
    for k, ref in enumerate(refs):
        for f in range(4):
            for d in range(3):
                lane = (len(refs) * d + k) * LANES
                lhs[f * 112 : f * 112 + 104, lane : lane + LANES] = ref[max(f + d - 2, 0)]
    for pair in PAIRS:
        rhs = jnp.concatenate(
            [
                jnp.concatenate(
                    [
                        kernel_ref[9 * d + s, pl.ds(pl.multiple_of(turned(ta, shift) * LANES, LANES), LANES), :]
                        for s in pair
                    ],
                    axis=1,
                )
                for d in range(3)
                for shift in shifts
            ],
            axis=0,
        )
        lanes = slice(pair[0] * LANES, pair[0] * LANES + rhs.shape[1])
        part = jnp.dot(lhs[...], rhs, preferred_element_type=F32)
        product[:, lanes] = part if before is None else before[:, lanes] + part


def second_conv_first_kernel(s0, s3, kernel_ref, out_ref, lhs):
    add_blocks((s0, s3), (0, 3), kernel_ref, lhs, out_ref)


def second_conv_kernel(
    s1,
    s2,
    before_ref,
    small_ref,
    own_ref,
    kernel_ref,
    out0,
    out1,
    out2,
    out3,
    lhs,
    product,
    wide_rows,
    parts,
):
    ta = lax.axis_index("ta")
    add_blocks((s1, s2), (1, 2), kernel_ref, lhs, product, before_ref)
    totals = shifted_sums(product, 112, 10, 80)
    bias = small_ref[37:38, :]
    tiles = []
    for f in range(4):
        wide_rows[f] = totals[f] + bias
        branch = jnp.concatenate([wide_rows[f, 10 * r : 10 * r + 8, :] for r in range(8)], axis=0)
        branch = branch.astype(BF).astype(F32)
        residual = (own_ref[f].astype(F32) + branch).astype(BF)
        parts[f] = residual
        tiles.append(residual.astype(F32))
    mean, spread = channel_stats(jnp.concatenate(tiles, axis=0), None, 256)
    packed = pack_stats(mean, spread)
    for s, ref in enumerate((out0, out1, out2, out3)):
        ref[0:64, :] = parts[lax.rem(ta + s, 4)]
        ref[64:72, :] = packed


def normalise(x, coefficients):
    parts = []
    for b, (mean, scale, shift) in enumerate(coefficients):
        part = x[:, b * LANES : (b + 1) * LANES].astype(F32)
        parts.append(((part - mean) * scale + shift).astype(BF))
    return jnp.concatenate(parts, axis=1)


def attention_kernel(*refs):
    asked, told = refs[:4], refs[4:6]
    small_ref, query_ref, key_ref = refs[6:9]
    outs, normed = refs[9:13], refs[13]
    middle, spread = merge_stats([unpack_stats(ref[512:520, :]) for ref in told])
    inverse = lax.rsqrt(spread + EPS)
    coefficients = []
    for b in range(4):
        lanes = slice(b * LANES, (b + 1) * LANES)
        gain, shift = gain_and_shift(small_ref, 16, b)
        coefficients.append((middle[:, lanes], inverse[:, lanes] * gain, shift))
    normed_q = normalise(jnp.concatenate([ref[0:64, :] for ref in asked], axis=0), coefficients)
    for k, ref in enumerate(told):
        normed[512 * k : 512 * k + 512, :] = normalise(ref[0:512, :], coefficients)
    queries = jnp.dot(normed_q, query_ref[...], preferred_element_type=F32) + wide(small_ref, 24)
    folded = lax.dot_general(
        queries.astype(BF), key_ref[...], (((1,), (1,)), ((), ())), preferred_element_type=F32
    ).astype(BF)
    scores = lax.dot_general(
        folded, normed[...], (((1,), (1,)), ((), ())), preferred_element_type=F32
    ) * 512 ** (-0.5)
    highest = jnp.max(scores, axis=1, keepdims=True)
    weights = jnp.exp(scores - highest)
    total = jnp.sum(weights, axis=1, keepdims=True)
    mixed = jnp.dot(weights.astype(BF), normed[...], preferred_element_type=F32) / total
    level = highest + jnp.log(total)
    top, middle, low = thirds(level)
    lane = lax.broadcasted_iota(jnp.int32, (256, LANES), 1)
    tail = jnp.where(lane == 0, top, jnp.where(lane == 1, middle, jnp.where(lane == 2, low, 0.0)))
    for s, ref in enumerate(outs):
        ref[:, 0:512] = mixed[64 * s : 64 * s + 64].astype(BF)
        ref[:, 512:640] = tail[64 * s : 64 * s + 64].astype(BF)


def finish_kernel(b0, b1, b2, b3, residual_ref, small_ref, value_ref, output_ref, out_ref):
    backs = [ref[...].astype(F32) for ref in (b0, b1, b2, b3)]
    levels = [jnp.sum(back[:, 512:640], axis=1, keepdims=True) for back in backs]
    highest = functools.reduce(jnp.maximum, levels)
    shares = [jnp.exp(level - highest) for level in levels]
    inverse = 1.0 / sum(shares)
    mean_normed = sum(back[:, 0:512] * (share * inverse) for back, share in zip(backs, shares))
    attended = jnp.dot(mean_normed.astype(BF), value_ref[...], preferred_element_type=F32)
    attended = (attended + wide(small_ref, 28)).astype(BF)
    mixed = jnp.dot(attended, output_ref[...], preferred_element_type=F32)
    out_ref[...] = (residual_ref[0:64, :].astype(F32) + mixed + wide(small_ref, 32)).astype(BF)


def call(kernel, out_shape, specs, scratch, flops, *args):
    shapes = out_shape if isinstance(out_shape, tuple) else (out_shape,)
    moved = sum(a.size * a.dtype.itemsize for a in args) + sum(
        s.size * jnp.dtype(s.dtype).itemsize for s in shapes
    )
    return pl.pallas_call(
        kernel,
        out_shape=out_shape,
        in_specs=specs,
        out_specs=tuple(VMEM for _ in shapes) if isinstance(out_shape, tuple) else VMEM,
        scratch_shapes=scratch,
        compiler_params=pltpu.CompilerParams(vmem_limit_bytes=LIMIT),
        cost_estimate=pl.CostEstimate(flops=flops, bytes_accessed=moved, transcendentals=0),
    )(*args)


def ring(count, step):
    return [(i, (i + step) % count) for i in range(count)]


def long_first(count):
    return sorted(range(1, count), key=lambda s: -min(s, count - s))


def spread_out(blocks, axis, sign=1):
    count = lax.axis_size(axis)
    arrived = {0: blocks[0]}
    for s in long_first(count):
        arrived[s] = lax.ppermute(blocks[s], axis, ring(count, sign * s))
    return [arrived[s] for s in range(count)]


def around(block, axis):
    return spread_out([block] * lax.axis_size(axis), axis)


def relayed(block, axis):
    count = lax.axis_size(axis)
    after = {step: lax.ppermute(block, axis, ring(count, step)) for step in (2, 1, -1, -2)}
    further = [lax.ppermute(after[step], axis, ring(count, move)) for step, move in ((1, 2), (-1, -2), (2, 2))]
    return [block, *after.values(), *further]


def both_sides(low, high, axis):
    count = lax.axis_size(axis)
    return lax.ppermute(high, axis, ring(count, 1)), lax.ppermute(low, axis, ring(count, -1))


def over_tiles(rows):
    return lax.all_to_all(rows, HA + ("z",), split_axis=0, concat_axis=0, tiled=True)


def body(
    latent,
    norm1_gain,
    norm1_shift,
    conv1_kernel,
    conv1_shift,
    norm2_gain,
    norm2_shift,
    conv2_kernel,
    conv2_shift,
    norm3_gain,
    norm3_shift,
    query_weight,
    query_shift,
    key_weight,
    value_weight,
    value_shift,
    output_weight,
    output_shift,
):
    _, height, width, channels = latent.shape
    cells = height * width
    tiles = lax.axis_size(HA) * lax.axis_size("z")
    grid = (lax.axis_size(HA) * height, lax.axis_size("z") * width)
    vectors = [norm1_gain, norm1_shift, norm2_gain, norm2_shift, norm3_gain, norm3_shift]
    vectors += [query_shift, value_shift, output_shift, conv1_shift, conv2_shift]
    small = jnp.concatenate(vectors).reshape(-1, LANES)

    def bf(*shape):
        return jax.ShapeDtypeStruct(shape, BF)

    rows = jax.ShapeDtypeStruct((tiles, 1, LANES), F32)

    slots = around(latent[0].reshape(cells, channels), "ta")
    slots[0] = call(first_kernel, bf(cells, channels), [VMEM], [], 4 * 10**9, slots[0])
    rows1, low, high = call(
        frame_moments_kernel, (rows, bf(4, 16, channels), bf(4, 16, channels)), [VMEM] * 4, [], 10**6, *slots
    )
    top, bottom = both_sides(low, high, HA)
    rows1 = over_tiles(rows1)
    low, high = call(
        columns_kernel,
        (bf(4, 24, channels), bf(4, 24, channels)),
        [VMEM] * 6,
        [pltpu.VMEM((4, 96, LANES), F32), pltpu.VMEM((4, 24, LANES), F32)],
        10**6,
        *slots,
        top,
        bottom,
    )
    left, right = both_sides(low, high, "z")
    lhs, own = call(
        functools.partial(rimmed_kernel, grid),
        (bf(576, 1536), bf(4, cells, LANES)),
        [VMEM] * 10,
        [pltpu.VMEM((4, cells, channels), BF), pltpu.VMEM((4, 144, LANES), F32), pltpu.VMEM((4, 24, LANES), F32)],
        4 * 10**9,
        *slots,
        top,
        bottom,
        left,
        right,
        rows1,
        small,
    )
    hidden, rows2 = call(
        first_conv_kernel,
        (bf(4, 104, LANES), rows),
        [VMEM] * 3,
        [
            pltpu.VMEM((584, 1152), F32),
            pltpu.VMEM((4, 120, LANES), F32),
            pltpu.VMEM((4, 104, LANES), F32),
        ],
        2 * 10**9,
        lhs,
        small,
        conv1_kernel,
    )

    act = call(
        functools.partial(activate_kernel, grid),
        bf(4, 104, LANES),
        [VMEM] * 3,
        [],
        4 * 10**9,
        hidden,
        over_tiles(rows2),
        small,
    )
    blocks = around(act, "ta")
    before = call(
        second_conv_first_kernel,
        jax.ShapeDtypeStruct((448, 1152), F32),
        [VMEM] * 3,
        [pltpu.VMEM((448, 768), BF)],
        10**9,
        blocks[0],
        blocks[3],
        conv2_kernel,
    )
    parts = call(
        second_conv_kernel,
        (bf(cells + 8, LANES),) * 4,
        [VMEM] * 6,
        [
            pltpu.VMEM((448, 768), BF),
            pltpu.VMEM((448, 1152), F32),
            pltpu.VMEM((4, 80, LANES), F32),
            pltpu.VMEM((4, cells, LANES), BF),
        ],
        2 * 10**9,
        blocks[1],
        blocks[2],
        before,
        small,
        own,
        conv2_kernel,
    )

    residual = call(
        residual_kernel,
        bf(cells + 8, channels),
        [VMEM] * 4,
        [pltpu.VMEM((4, cells + 8, LANES), BF)],
        10**6,
        *spread_out(parts, "ta"),
    )
    asked = around(residual, "y")
    told = call(merge_kernel, bf(cells + 8, channels), [VMEM] * 4, [], 10**6, *asked)
    told = call(merge_kernel, bf(8 * cells + 8, channels), [VMEM] * 8, [], 10**6, *relayed(told, "z"))
    packed = call(
        attention_kernel,
        (bf(cells, channels + LANES),) * 4,
        [VMEM] * 9,
        [pltpu.VMEM((1024, channels), BF)],
        10**9,
        *asked,
        told,
        lax.ppermute(told, "core", ring(2, 1)),
        small,
        query_weight,
        key_weight,
    )

    block_out = call(
        finish_kernel,
        bf(cells, channels),
        [VMEM] * 8,
        [],
        10**8,
        *spread_out(packed, "y", -1),
        residual,
        small,
        value_weight,
        output_weight,
    )
    return block_out.reshape(latent.shape)


def solution(mesh):
    frames, rows, columns = mesh.devices.shape
    split = Mesh(mesh.devices.reshape(frames, rows // 2, 2, columns), ("ta", "y", "core", "z"))
    tile = P("ta", HA, "z", None)
    kernel, shift = P(None, None, "ta"), P("ta")
    in_specs = (tile, P(), P(), kernel, shift, P(), P(), kernel, shift) + (P(),) * 9
    return jax.shard_map(body, mesh=split, in_specs=in_specs, out_specs=tile, check_vma=False)
```

```python
import functools

import jax
import jax.numpy as jnp
from jax import lax
from jax.experimental import pallas as pl
from jax.experimental.pallas import tpu as pltpu
from jax.sharding import Mesh, PartitionSpec as P

GROUPS = 32
EPS = 1e-06
HA = ("y", "core")
BF = jnp.bfloat16
F32 = jnp.float32
LANES = 128
LIMIT = 32 * 1024 * 1024
PAIRS = ((0, 1), (2, 3), (4, 5), (6, 7), (8,))
VMEM = pl.BlockSpec(memory_space=pltpu.VMEM)


def lane_in_group(shape):
    return lax.broadcasted_iota(jnp.int32, shape, 1) & 15


def segment_sum(x):
    row = lax.broadcasted_iota(jnp.int32, (LANES, LANES), 0)
    column = lax.broadcasted_iota(jnp.int32, (LANES, LANES), 1)
    ones = jnp.where((row >> 4) == (column >> 4), 1.0, 0.0).astype(BF)
    pieces = jnp.concatenate([*thirds(x), jnp.zeros_like(x)], axis=0).astype(BF)
    sums = jnp.dot(pieces, ones, preferred_element_type=F32)
    return sums[0:8] + sums[8:16] + sums[16:24]


def rows8(x):
    return jnp.broadcast_to(x, (8, LANES))


def cell_rows(rows, pitch):
    index = lax.broadcasted_iota(jnp.int32, (rows, LANES), 0)
    row = (index * {10: 52429, 12: 43691}[pitch]) >> 19
    return row, index - row * pitch


def encode(out_ref, stats):
    lane = lane_in_group((8, LANES))
    row = jnp.zeros((8, LANES), F32)
    for block, mean, spread in stats:
        row = jnp.where(lane == block, mean, row)
        row = jnp.where(lane == block + 4, spread, row)
    out_ref[...] = jnp.broadcast_to(row[0:1][None], out_ref.shape)


def thirds(x):
    high = x.astype(BF).astype(F32)
    middle = (x - high).astype(BF).astype(F32)
    return high, middle, x - high - middle


def pack_stats(mean, spread):
    row = lax.broadcasted_iota(jnp.int32, mean.shape, 0)
    packed = jnp.zeros(mean.shape, F32)
    for k, piece in enumerate(thirds(mean) + thirds(spread)):
        packed = jnp.where(row == k, piece, packed)
    return packed.astype(BF)


def unpack_stats(packed):
    x = packed.astype(F32)
    return x[0:1] + x[1:2] + x[2:3], x[3:4] + x[4:5] + x[5:6]


def merge_stats(stats):
    scale = 1.0 / len(stats)
    middle = sum(mean for mean, _ in stats) * scale
    spread = sum(spread + (mean - middle) * (mean - middle) for mean, spread in stats) * scale
    return middle, spread


def all_rows(x):
    return jnp.broadcast_to(x, (8, x.shape[1]))


def channel_stats(x, keep, count):
    mean = jnp.sum(x, axis=0, keepdims=True) * (1.0 / count)
    deviation = x - mean
    if keep is not None:
        deviation = jnp.where(keep, deviation, 0.0)
    spread = jnp.sum(deviation * deviation, axis=0, keepdims=True) * (1.0 / count)
    return group_stats(mean, spread)


def group_stats(mean, spread):
    mean, spread = rows8(mean), rows8(spread)
    middle = segment_sum(mean) * (1.0 / 16)
    off = mean - middle
    return middle, segment_sum(spread + off * off) * (1.0 / 16)


def tile_stats(rows_ref):
    rows = rows_ref[...].reshape(rows_ref.shape[0], LANES)
    count = rows.shape[0]
    mean = jnp.sum(rows, axis=0, keepdims=True) * (1.0 / count)
    off = rows - mean
    between = jnp.sum(off * off, axis=0, keepdims=True) * (1.0 / count)
    return rows8(mean), rows8(between)


def block_stats(mean, between, block):
    lane = lane_in_group((8, LANES))
    middle = segment_sum(jnp.where(lane == block, mean, 0.0))
    spread = segment_sum(jnp.where(lane == block + 4, mean, jnp.where(lane == block, between, 0.0)))
    return middle[0:1], lax.rsqrt(spread[0:1] + EPS)


def decode(rows_ref, small_ref, at):
    mean, between = tile_stats(rows_ref)
    result = []
    for block in range(4):
        middle, inverse = block_stats(mean, between, block)
        gain, shift = gain_and_shift(small_ref, at, block)
        result.append((middle, inverse * gain, shift))
    return result


def gain_and_shift(small_ref, at, block):
    return small_ref[at + block : at + block + 1, :], small_ref[at + 4 + block : at + 5 + block, :]


def wide(small_ref, at):
    return jnp.concatenate([small_ref[at + b : at + b + 1, :] for b in range(4)], axis=1)


def silu(v):
    half = 0.5 * v
    return half + half * jnp.tanh(half)


def turned(ta, s):
    return lax.rem(ta - s + 4, 4)


def first_kernel(latent_ref, out_ref):
    out_ref[...] = latent_ref[...]


def frame_moments_kernel(s0, s1, s2, s3, out_ref, first_ref, last_ref):
    slots = (s0, s1, s2, s3)
    stats = []
    for block in range(4):
        x = jnp.concatenate(
            [ref[:, block * LANES : (block + 1) * LANES].astype(F32) for ref in slots], axis=0
        )
        stats.append((block,) + channel_stats(x, None, x.shape[0]))
    encode(out_ref, stats)
    for s, ref in enumerate(slots):
        first_ref[s] = ref[0:16, :]
        last_ref[s] = ref[48:64, :]


def columns_kernel(s0, s1, s2, s3, top_ref, bottom_ref, first_ref, last_ref, tall, sides):
    for s, ref in enumerate((s0, s1, s2, s3)):
        for b in range(4):
            lanes = slice(b * LANES, (b + 1) * LANES)
            tall[b, 0:16, :] = top_ref[s, :, lanes].astype(F32)
            tall[b, 16:80, :] = ref[:, lanes].astype(F32)
            tall[b, 80:96, :] = bottom_ref[s, :, lanes].astype(F32)
            for k, out_ref in ((0, first_ref), (6, last_ref)):
                for j in range(2):
                    sides[b, 12 * j : 12 * j + 12, :] = tall[b, pl.ds(j + k, 12, stride=8), :]
                out_ref[s, :, lanes] = sides[b].astype(BF)


def activate_kernel(grid, hidden_ref, rows_ref, small_ref, out_ref):
    ta = lax.axis_index("ta")
    middle, inverse = block_stats(*tile_stats(rows_ref), 0)
    scale = inverse * small_ref[pl.ds(8 + ta, 1), :]
    shift = small_ref[pl.ds(12 + ta, 1), :]
    keep = inside(8 * lax.axis_index(HA) - 1, 8 * lax.axis_index("z") - 1, 104, 10, grid)
    for f in range(4):
        v = (hidden_ref[f].astype(F32) - middle) * scale + shift
        out_ref[f] = jnp.where(keep, silu(v), 0.0).astype(BF)


def residual_kernel(s0, s1, s2, s3, out_ref, parts):
    for s, ref in enumerate((s0, s1, s2, s3)):
        parts[turned(lax.axis_index("ta"), s)] = ref[...]
    out_ref[...] = jnp.concatenate([parts[b] for b in range(4)], axis=1)


def merge_kernel(*refs):
    slots, out_ref = refs[:-1], refs[-1]
    room = out_ref.shape[0] - 8
    middle, spread = merge_stats([unpack_stats(ref[64:72, :]) for ref in slots])
    for s in range(room // 64):
        out_ref[64 * s : 64 * s + 64, :] = slots[s][0:64, :]
    out_ref[room : room + 8, :] = pack_stats(all_rows(middle), all_rows(spread))


def convolve(lhs, weights, product, frame_rows, pitch, out_rows):
    for pair in PAIRS:
        rhs = jnp.concatenate(
            [jnp.concatenate([weights[9 * d + s] for s in pair], axis=1) for d in range(3)], axis=0
        )
        lane = pair[0] * LANES
        product[0 : 4 * frame_rows, lane : lane + rhs.shape[1]] = jnp.dot(
            lhs[...], rhs, preferred_element_type=F32
        )
    return shifted_sums(product, frame_rows, pitch, out_rows)


def shifted_sums(product, frame_rows, pitch, out_rows):
    totals = []
    for f in range(4):
        total = None
        for s in range(9):
            at = f * frame_rows + pitch * (s // 3) + s % 3
            piece = product[at : at + out_rows, s * LANES : (s + 1) * LANES]
            total = piece if total is None else total + piece
        totals.append(total)
    return totals


def inside(base_row, base_column, rows, pitch, grid):
    row, column = cell_rows(rows, pitch)
    row, column = row + base_row, column + base_column
    return (row >= 0) & (row < grid[0]) & (column >= 0) & (column < grid[1])


def rimmed_kernel(
    grid,
    s0,
    s1,
    s2,
    s3,
    top_ref,
    bottom_ref,
    left_ref,
    right_ref,
    rows_ref,
    small_ref,
    lhs_ref,
    own_ref,
    frames,
    tile,
    sides,
):
    ta = lax.axis_index("ta")
    coefficients = decode(rows_ref, small_ref, 0)
    keep = inside(8 * lax.axis_index(HA) - 2, 8 * lax.axis_index("z") - 2, 144, 12, grid)
    for s, ref in enumerate((s0, s1, s2, s3)):
        frames[turned(ta, s)] = ref[...]
    for frame in range(4):
        s = turned(ta, frame)
        own = jnp.zeros((64, LANES), F32)
        for b in range(4):
            lanes = slice(b * LANES, (b + 1) * LANES)
            middle = frames[frame, :, lanes].astype(F32)
            own = jnp.where(ta == b, middle, own)
            top, bottom = top_ref[s, :, lanes].astype(F32), bottom_ref[s, :, lanes].astype(F32)
            for r in range(12):
                if r < 2:
                    piece = top[8 * r : 8 * r + 8]
                elif r < 10:
                    piece = middle[8 * (r - 2) : 8 * (r - 2) + 8]
                else:
                    piece = bottom[8 * (r - 10) : 8 * (r - 10) + 8]
                tile[b, 12 * r + 2 : 12 * r + 10, :] = piece
            for k, side_ref in ((0, left_ref), (10, right_ref)):
                sides[b] = side_ref[s, :, lanes].astype(F32)
                for j in range(2):
                    tile[b, pl.ds(j + k, 12, stride=12), :] = sides[b, 12 * j : 12 * j + 12, :]
            mean, scale, shift = coefficients[b]
            v = (tile[b] - mean) * scale + shift
            act = jnp.where(keep, silu(v), 0.0).astype(BF)
            for f in range(4):
                for d in range(3):
                    if max(f + d - 2, 0) == frame:
                        lane = (4 * d + b) * LANES
                        lhs_ref[f * 144 : (f + 1) * 144, lane : lane + LANES] = act
        own_ref[frame] = own.astype(BF)


def first_conv_kernel(lhs, small_ref, kernel_ref, out_ref, moments_ref, product, wide_rows, tight_rows):
    totals = convolve(lhs, kernel_ref, product, 144, 12, 120)
    row, column = cell_rows(104, 10)
    keep = (row >= 1) & (row <= 8) & (column >= 1) & (column <= 8)
    bias = small_ref[36:37, :]
    kept = []
    for f in range(4):
        wide_rows[f] = totals[f] + bias
        for r in range(10):
            tight_rows[f, 10 * r : 10 * r + 10, :] = wide_rows[f, 12 * r : 12 * r + 10, :]
        tight_rows[f, 100:104, :] = jnp.zeros((4, LANES), F32)
        hidden = tight_rows[f].astype(BF)
        out_ref[f] = hidden
        kept.append(jnp.where(keep, hidden.astype(F32), 0.0))
    mean = sum(jnp.sum(x, axis=0, keepdims=True) for x in kept) * (1.0 / 256)
    squares = [jnp.square(jnp.where(keep, x - mean, 0.0)) for x in kept]
    spread = sum(jnp.sum(x, axis=0, keepdims=True) for x in squares) * (1.0 / 256)
    encode(moments_ref, [(0,) + group_stats(mean, spread)])


def add_blocks(refs, shifts, kernel_ref, lhs, product, before=None):
    ta = lax.axis_index("ta")
    for k, ref in enumerate(refs):
        for f in range(4):
            for d in range(3):
                lane = (len(refs) * d + k) * LANES
                lhs[f * 112 : f * 112 + 104, lane : lane + LANES] = ref[max(f + d - 2, 0)]
    for pair in PAIRS:
        rhs = jnp.concatenate(
            [
                jnp.concatenate(
                    [
                        kernel_ref[9 * d + s, pl.ds(pl.multiple_of(turned(ta, shift) * LANES, LANES), LANES), :]
                        for s in pair
                    ],
                    axis=1,
                )
                for d in range(3)
                for shift in shifts
            ],
            axis=0,
        )
        lanes = slice(pair[0] * LANES, pair[0] * LANES + rhs.shape[1])
        part = jnp.dot(lhs[...], rhs, preferred_element_type=F32)
        product[:, lanes] = part if before is None else before[:, lanes] + part


def second_conv_first_kernel(s0, s3, kernel_ref, out_ref, lhs):
    add_blocks((s0, s3), (0, 3), kernel_ref, lhs, out_ref)


def second_conv_kernel(
    s1,
    s2,
    before_ref,
    small_ref,
    own_ref,
    kernel_ref,
    out0,
    out1,
    out2,
    out3,
    lhs,
    product,
    wide_rows,
    parts,
):
    ta = lax.axis_index("ta")
    add_blocks((s1, s2), (1, 2), kernel_ref, lhs, product, before_ref)
    totals = shifted_sums(product, 112, 10, 80)
    bias = small_ref[37:38, :]
    tiles = []
    for f in range(4):
        wide_rows[f] = totals[f] + bias
        branch = jnp.concatenate([wide_rows[f, 10 * r : 10 * r + 8, :] for r in range(8)], axis=0)
        branch = branch.astype(BF).astype(F32)
        residual = (own_ref[f].astype(F32) + branch).astype(BF)
        parts[f] = residual
        tiles.append(residual.astype(F32))
    mean, spread = channel_stats(jnp.concatenate(tiles, axis=0), None, 256)
    packed = pack_stats(mean, spread)
    for s, ref in enumerate((out0, out1, out2, out3)):
        ref[0:64, :] = parts[lax.rem(ta + s, 4)]
        ref[64:72, :] = packed


def normalise(x, coefficients):
    parts = []
    for b, (mean, scale, shift) in enumerate(coefficients):
        part = x[:, b * LANES : (b + 1) * LANES].astype(F32)
        parts.append(((part - mean) * scale + shift).astype(BF))
    return jnp.concatenate(parts, axis=1)


def attention_kernel(*refs):
    asked, told = refs[:4], refs[4:6]
    small_ref, query_ref, key_ref = refs[6:9]
    outs, normed = refs[9:13], refs[13]
    middle, spread = merge_stats([unpack_stats(ref[512:520, :]) for ref in told])
    inverse = lax.rsqrt(spread + EPS)
    coefficients = []
    for b in range(4):
        lanes = slice(b * LANES, (b + 1) * LANES)
        gain, shift = gain_and_shift(small_ref, 16, b)
        coefficients.append((middle[:, lanes], inverse[:, lanes] * gain, shift))
    normed_q = normalise(jnp.concatenate([ref[0:64, :] for ref in asked], axis=0), coefficients)
    for k, ref in enumerate(told):
        normed[512 * k : 512 * k + 512, :] = normalise(ref[0:512, :], coefficients)
    queries = jnp.dot(normed_q, query_ref[...], preferred_element_type=F32) + wide(small_ref, 24)
    folded = lax.dot_general(
        queries.astype(BF), key_ref[...], (((1,), (1,)), ((), ())), preferred_element_type=F32
    ) * 512 ** (-0.5)
    scores = lax.dot_general(
        folded.astype(BF), normed[...], (((1,), (1,)), ((), ())), preferred_element_type=F32
    )
    highest = jnp.max(scores, axis=1, keepdims=True)
    weights = jnp.exp(scores - highest)
    total = jnp.sum(weights, axis=1, keepdims=True)
    mixed = jnp.dot(weights.astype(BF), normed[...], preferred_element_type=F32) * (1.0 / total)
    level = highest + jnp.log(total)
    top, middle, low = thirds(level)
    lane = lax.broadcasted_iota(jnp.int32, (256, LANES), 1)
    tail = jnp.where(lane == 0, top, jnp.where(lane == 1, middle, jnp.where(lane == 2, low, 0.0)))
    for s, ref in enumerate(outs):
        ref[:, 0:512] = mixed[64 * s : 64 * s + 64].astype(BF)
        ref[:, 512:640] = tail[64 * s : 64 * s + 64].astype(BF)


def finish_kernel(b0, b1, b2, b3, residual_ref, small_ref, value_ref, output_ref, out_ref):
    backs = [ref[...].astype(F32) for ref in (b0, b1, b2, b3)]
    levels = [jnp.sum(back[:, 512:640], axis=1, keepdims=True) for back in backs]
    highest = functools.reduce(jnp.maximum, levels)
    shares = [jnp.exp(level - highest) for level in levels]
    inverse = 1.0 / sum(shares)
    mean_normed = sum(back[:, 0:512] * (share * inverse) for back, share in zip(backs, shares))
    attended = jnp.dot(mean_normed.astype(BF), value_ref[...], preferred_element_type=F32)
    attended = (attended + wide(small_ref, 28)).astype(BF)
    mixed = jnp.dot(attended, output_ref[...], preferred_element_type=F32)
    out_ref[...] = (residual_ref[0:64, :].astype(F32) + mixed + wide(small_ref, 32)).astype(BF)


def call(kernel, out_shape, specs, scratch, flops, *args):
    shapes = out_shape if isinstance(out_shape, tuple) else (out_shape,)
    moved = sum(a.size * a.dtype.itemsize for a in args) + sum(
        s.size * jnp.dtype(s.dtype).itemsize for s in shapes
    )
    return pl.pallas_call(
        kernel,
        out_shape=out_shape,
        in_specs=specs,
        out_specs=tuple(VMEM for _ in shapes) if isinstance(out_shape, tuple) else VMEM,
        scratch_shapes=scratch,
        compiler_params=pltpu.CompilerParams(vmem_limit_bytes=LIMIT),
        cost_estimate=pl.CostEstimate(flops=flops, bytes_accessed=moved, transcendentals=0),
    )(*args)


def ring(count, step):
    return [(i, (i + step) % count) for i in range(count)]


def long_first(count):
    return sorted(range(1, count), key=lambda s: -min(s, count - s))


def spread_out(blocks, axis, sign=1):
    count = lax.axis_size(axis)
    arrived = {0: blocks[0]}
    for s in long_first(count):
        arrived[s] = lax.ppermute(blocks[s], axis, ring(count, sign * s))
    return [arrived[s] for s in range(count)]


def around(block, axis):
    return spread_out([block] * lax.axis_size(axis), axis)


def relayed(block, axis):
    count = lax.axis_size(axis)
    after = {step: lax.ppermute(block, axis, ring(count, step)) for step in (2, 1, -1, -2)}
    further = [lax.ppermute(after[step], axis, ring(count, move)) for step, move in ((1, 2), (-1, -2), (2, 2))]
    return [block, *after.values(), *further]


def both_sides(low, high, axis):
    count = lax.axis_size(axis)
    return lax.ppermute(high, axis, ring(count, 1)), lax.ppermute(low, axis, ring(count, -1))


def over_tiles(rows):
    return lax.all_to_all(rows, HA + ("z",), split_axis=0, concat_axis=0, tiled=True)


def body(
    latent,
    norm1_gain,
    norm1_shift,
    conv1_kernel,
    conv1_shift,
    norm2_gain,
    norm2_shift,
    conv2_kernel,
    conv2_shift,
    norm3_gain,
    norm3_shift,
    query_weight,
    query_shift,
    key_weight,
    value_weight,
    value_shift,
    output_weight,
    output_shift,
):
    _, height, width, channels = latent.shape
    cells = height * width
    tiles = lax.axis_size(HA) * lax.axis_size("z")
    grid = (lax.axis_size(HA) * height, lax.axis_size("z") * width)
    vectors = [norm1_gain, norm1_shift, norm2_gain, norm2_shift, norm3_gain, norm3_shift]
    vectors += [query_shift, value_shift, output_shift, conv1_shift, conv2_shift]
    small = jnp.concatenate(vectors).reshape(-1, LANES)

    def bf(*shape):
        return jax.ShapeDtypeStruct(shape, BF)

    rows = jax.ShapeDtypeStruct((tiles, 1, LANES), F32)

    slots = around(latent[0].reshape(cells, channels), "ta")
    slots[0] = call(first_kernel, bf(cells, channels), [VMEM], [], 4 * 10**9, slots[0])
    rows1, low, high = call(
        frame_moments_kernel, (rows, bf(4, 16, channels), bf(4, 16, channels)), [VMEM] * 4, [], 10**6, *slots
    )
    top, bottom = both_sides(low, high, HA)
    rows1 = over_tiles(rows1)
    low, high = call(
        columns_kernel,
        (bf(4, 24, channels), bf(4, 24, channels)),
        [VMEM] * 6,
        [pltpu.VMEM((4, 96, LANES), F32), pltpu.VMEM((4, 24, LANES), F32)],
        10**6,
        *slots,
        top,
        bottom,
    )
    left, right = both_sides(low, high, "z")
    lhs, own = call(
        functools.partial(rimmed_kernel, grid),
        (bf(576, 1536), bf(4, cells, LANES)),
        [VMEM] * 10,
        [pltpu.VMEM((4, cells, channels), BF), pltpu.VMEM((4, 144, LANES), F32), pltpu.VMEM((4, 24, LANES), F32)],
        4 * 10**9,
        *slots,
        top,
        bottom,
        left,
        right,
        rows1,
        small,
    )
    hidden, rows2 = call(
        first_conv_kernel,
        (bf(4, 104, LANES), rows),
        [VMEM] * 3,
        [
            pltpu.VMEM((584, 1152), F32),
            pltpu.VMEM((4, 120, LANES), F32),
            pltpu.VMEM((4, 104, LANES), F32),
        ],
        2 * 10**9,
        lhs,
        small,
        conv1_kernel,
    )

    act = call(
        functools.partial(activate_kernel, grid),
        bf(4, 104, LANES),
        [VMEM] * 3,
        [],
        4 * 10**9,
        hidden,
        over_tiles(rows2),
        small,
    )
    blocks = around(act, "ta")
    before = call(
        second_conv_first_kernel,
        jax.ShapeDtypeStruct((448, 1152), F32),
        [VMEM] * 3,
        [pltpu.VMEM((448, 768), BF)],
        10**9,
        blocks[0],
        blocks[3],
        conv2_kernel,
    )
    parts = call(
        second_conv_kernel,
        (bf(cells + 8, LANES),) * 4,
        [VMEM] * 6,
        [
            pltpu.VMEM((448, 768), BF),
            pltpu.VMEM((448, 1152), F32),
            pltpu.VMEM((4, 80, LANES), F32),
            pltpu.VMEM((4, cells, LANES), BF),
        ],
        2 * 10**9,
        blocks[1],
        blocks[2],
        before,
        small,
        own,
        conv2_kernel,
    )

    residual = call(
        residual_kernel,
        bf(cells + 8, channels),
        [VMEM] * 4,
        [pltpu.VMEM((4, cells + 8, LANES), BF)],
        10**6,
        *spread_out(parts, "ta"),
    )
    asked = around(residual, "y")
    told = call(merge_kernel, bf(cells + 8, channels), [VMEM] * 4, [], 10**6, *asked)
    told = call(merge_kernel, bf(8 * cells + 8, channels), [VMEM] * 8, [], 10**6, *relayed(told, "z"))
    packed = call(
        attention_kernel,
        (bf(cells, channels + LANES),) * 4,
        [VMEM] * 9,
        [pltpu.VMEM((1024, channels), BF)],
        10**9,
        *asked,
        told,
        lax.ppermute(told, "core", ring(2, 1)),
        small,
        query_weight,
        key_weight,
    )

    block_out = call(
        finish_kernel,
        bf(cells, channels),
        [VMEM] * 8,
        [],
        10**8,
        *spread_out(packed, "y", -1),
        residual,
        small,
        value_weight,
        output_weight,
    )
    return block_out.reshape(latent.shape)


def solution(mesh):
    frames, rows, columns = mesh.devices.shape
    split = Mesh(mesh.devices.reshape(frames, rows // 2, 2, columns), ("ta", "y", "core", "z"))
    tile = P("ta", HA, "z", None)
    kernel, shift = P(None, None, "ta"), P("ta")
    in_specs = (tile, P(), P(), kernel, shift, P(), P(), kernel, shift) + (P(),) * 9
    return jax.shard_map(body, mesh=split, in_specs=in_specs, out_specs=tile, check_vma=False)
```

```python
import functools

import jax
import jax.numpy as jnp
from jax import lax
from jax.experimental import pallas as pl
from jax.experimental.pallas import tpu as pltpu
from jax.sharding import Mesh, PartitionSpec as P

GROUPS = 32
EPS = 1e-06
HA = ("y", "core")
BF = jnp.bfloat16
F32 = jnp.float32
LANES = 128
LIMIT = 32 * 1024 * 1024
SHIFTS = (0, 2, 1, 3)
PAIRS = ((0, 1), (2, 3), (4, 5), (6, 7), (8,))
VMEM = pl.BlockSpec(memory_space=pltpu.VMEM)


def lane_in_group(shape):
    return lax.broadcasted_iota(jnp.int32, shape, 1) & 15


def segment_sum(x):
    row = lax.broadcasted_iota(jnp.int32, (LANES, LANES), 0)
    column = lax.broadcasted_iota(jnp.int32, (LANES, LANES), 1)
    ones = jnp.where((row >> 4) == (column >> 4), 1.0, 0.0).astype(BF)
    pieces = jnp.concatenate([*thirds(x), jnp.zeros_like(x)], axis=0).astype(BF)
    sums = jnp.dot(pieces, ones, preferred_element_type=F32)
    return sums[0:8] + sums[8:16] + sums[16:24]


def rows8(x):
    return jnp.broadcast_to(x, (8, LANES))


def cell_rows(rows, pitch):
    index = lax.broadcasted_iota(jnp.int32, (rows, LANES), 0)
    row = (index * {10: 52429, 12: 43691}[pitch]) >> 19
    return row, index - row * pitch


def encode(out_ref, stats):
    lane = lane_in_group((8, LANES))
    row = jnp.zeros((8, LANES), F32)
    for block, mean, spread in stats:
        row = jnp.where(lane == block, mean, row)
        row = jnp.where(lane == block + 4, spread, row)
    out_ref[...] = jnp.broadcast_to(row[0:1][None], out_ref.shape)


def thirds(x):
    high = x.astype(BF).astype(F32)
    middle = (x - high).astype(BF).astype(F32)
    return high, middle, x - high - middle


def pack_stats(mean, spread):
    row = lax.broadcasted_iota(jnp.int32, mean.shape, 0)
    packed = jnp.zeros(mean.shape, F32)
    for k, piece in enumerate(thirds(mean) + thirds(spread)):
        packed = jnp.where(row == k, piece, packed)
    return packed.astype(BF)


def unpack_stats(packed):
    x = packed.astype(F32)
    return x[0:1] + x[1:2] + x[2:3], x[3:4] + x[4:5] + x[5:6]


def merge_stats(stats):
    scale = 1.0 / len(stats)
    middle = sum(mean for mean, _ in stats) * scale
    spread = sum(spread + (mean - middle) * (mean - middle) for mean, spread in stats) * scale
    return middle, spread


def all_rows(x):
    return jnp.broadcast_to(x, (8, x.shape[1]))


def channel_stats(x, keep, count):
    mean = jnp.sum(x, axis=0, keepdims=True) * (1.0 / count)
    deviation = x - mean
    if keep is not None:
        deviation = jnp.where(keep, deviation, 0.0)
    spread = jnp.sum(deviation * deviation, axis=0, keepdims=True) * (1.0 / count)
    return group_stats(mean, spread)


def group_stats(mean, spread):
    mean, spread = rows8(mean), rows8(spread)
    middle = segment_sum(mean) * (1.0 / 16)
    off = mean - middle
    return middle, segment_sum(spread + off * off) * (1.0 / 16)


def tile_stats(rows_ref):
    rows = rows_ref[...].reshape(rows_ref.shape[0], LANES)
    count = rows.shape[0]
    mean = jnp.sum(rows, axis=0, keepdims=True) * (1.0 / count)
    off = rows - mean
    between = jnp.sum(off * off, axis=0, keepdims=True) * (1.0 / count)
    return rows8(mean), rows8(between)


def block_stats(mean, between, block):
    lane = lane_in_group((8, LANES))
    middle = segment_sum(jnp.where(lane == block, mean, 0.0))
    spread = segment_sum(jnp.where(lane == block + 4, mean, jnp.where(lane == block, between, 0.0)))
    return middle[0:1], lax.rsqrt(spread[0:1] + EPS)


def decode(rows_ref, small_ref, at):
    mean, between = tile_stats(rows_ref)
    result = []
    for block in range(4):
        middle, inverse = block_stats(mean, between, block)
        gain, shift = gain_and_shift(small_ref, at, block)
        result.append((middle, inverse * gain, shift))
    return result


def gain_and_shift(small_ref, at, block):
    return small_ref[at + block : at + block + 1, :], small_ref[at + 4 + block : at + 5 + block, :]


def wide(small_ref, at):
    return jnp.concatenate([small_ref[at + b : at + b + 1, :] for b in range(4)], axis=1)


def silu(v):
    half = 0.5 * v
    return half + half * jnp.tanh(half)


def turned(ta, s):
    return lax.rem(ta - s + 4, 4)


def first_kernel(latent_ref, out_ref):
    out_ref[...] = latent_ref[...]


def frame_moments_kernel(s0, s1, s2, s3, out_ref, first_ref, last_ref):
    slots = (s0, s1, s2, s3)
    stats = []
    for block in range(4):
        x = jnp.concatenate(
            [ref[:, block * LANES : (block + 1) * LANES].astype(F32) for ref in slots], axis=0
        )
        stats.append((block,) + channel_stats(x, None, x.shape[0]))
    encode(out_ref, stats)
    for s, ref in zip(SHIFTS, slots):
        first_ref[s] = ref[0:16, :]
        last_ref[s] = ref[48:64, :]


def columns_kernel(s0, s1, s2, s3, top_ref, bottom_ref, first_ref, last_ref, tall, sides):
    for s, ref in zip(SHIFTS, (s0, s1, s2, s3)):
        for b in range(4):
            lanes = slice(b * LANES, (b + 1) * LANES)
            tall[b, 0:16, :] = top_ref[s, :, lanes].astype(F32)
            tall[b, 16:80, :] = ref[:, lanes].astype(F32)
            tall[b, 80:96, :] = bottom_ref[s, :, lanes].astype(F32)
            for k, out_ref in ((0, first_ref), (6, last_ref)):
                for j in range(2):
                    sides[b, 12 * j : 12 * j + 12, :] = tall[b, pl.ds(j + k, 12, stride=8), :]
                out_ref[s, :, lanes] = sides[b].astype(BF)


def activate_kernel(grid, hidden_ref, rows_ref, small_ref, out_ref):
    ta = lax.axis_index("ta")
    middle, inverse = block_stats(*tile_stats(rows_ref), 0)
    scale = inverse * small_ref[pl.ds(8 + ta, 1), :]
    shift = small_ref[pl.ds(12 + ta, 1), :]
    keep = inside(8 * lax.axis_index(HA) - 1, 8 * lax.axis_index("z") - 1, 104, 10, grid)
    for f in range(4):
        v = (hidden_ref[f].astype(F32) - middle) * scale + shift
        out_ref[f] = jnp.where(keep, silu(v), 0.0).astype(BF)


def residual_kernel(s0, s1, s2, s3, out_ref, parts):
    for s, ref in zip(SHIFTS, (s0, s1, s2, s3)):
        parts[turned(lax.axis_index("ta"), s)] = ref[...]
    out_ref[...] = jnp.concatenate([parts[b] for b in range(4)], axis=1)


def merge_kernel(*refs):
    slots, out_ref = refs[:-1], refs[-1]
    room = out_ref.shape[0] - 8
    middle, spread = merge_stats([unpack_stats(ref[64:72, :]) for ref in slots])
    for s in range(room // 64):
        out_ref[64 * s : 64 * s + 64, :] = slots[s][0:64, :]
    out_ref[room : room + 8, :] = pack_stats(all_rows(middle), all_rows(spread))


def convolve(lhs, weights, product, frame_rows, pitch, out_rows):
    for pair in PAIRS:
        rhs = jnp.concatenate(
            [jnp.concatenate([weights[9 * d + s] for s in pair], axis=1) for d in range(3)], axis=0
        )
        lane = pair[0] * LANES
        product[0 : 4 * frame_rows, lane : lane + rhs.shape[1]] = jnp.dot(
            lhs[...], rhs, preferred_element_type=F32
        )
    return shifted_sums(product, frame_rows, pitch, out_rows)


def shifted_sums(product, frame_rows, pitch, out_rows):
    totals = []
    for f in range(4):
        total = None
        for s in range(9):
            at = f * frame_rows + pitch * (s // 3) + s % 3
            piece = product[at : at + out_rows, s * LANES : (s + 1) * LANES]
            total = piece if total is None else total + piece
        totals.append(total)
    return totals


def inside(base_row, base_column, rows, pitch, grid):
    row, column = cell_rows(rows, pitch)
    row, column = row + base_row, column + base_column
    return (row >= 0) & (row < grid[0]) & (column >= 0) & (column < grid[1])


def rimmed_kernel(
    grid,
    s0,
    s1,
    s2,
    s3,
    top_ref,
    bottom_ref,
    left_ref,
    right_ref,
    rows_ref,
    small_ref,
    lhs_ref,
    own_ref,
    frames,
    tile,
    sides,
):
    ta = lax.axis_index("ta")
    coefficients = decode(rows_ref, small_ref, 0)
    keep = inside(8 * lax.axis_index(HA) - 2, 8 * lax.axis_index("z") - 2, 144, 12, grid)
    for s, ref in zip(SHIFTS, (s0, s1, s2, s3)):
        frames[turned(ta, s)] = ref[...]
    for frame in range(4):
        s = turned(ta, frame)
        own = jnp.zeros((64, LANES), F32)
        for b in range(4):
            lanes = slice(b * LANES, (b + 1) * LANES)
            middle = frames[frame, :, lanes].astype(F32)
            own = jnp.where(ta == b, middle, own)
            top, bottom = top_ref[s, :, lanes].astype(F32), bottom_ref[s, :, lanes].astype(F32)
            for r in range(12):
                if r < 2:
                    piece = top[8 * r : 8 * r + 8]
                elif r < 10:
                    piece = middle[8 * (r - 2) : 8 * (r - 2) + 8]
                else:
                    piece = bottom[8 * (r - 10) : 8 * (r - 10) + 8]
                tile[b, 12 * r + 2 : 12 * r + 10, :] = piece
            for k, side_ref in ((0, left_ref), (10, right_ref)):
                sides[b] = side_ref[s, :, lanes].astype(F32)
                for j in range(2):
                    tile[b, pl.ds(j + k, 12, stride=12), :] = sides[b, 12 * j : 12 * j + 12, :]
            mean, scale, shift = coefficients[b]
            v = (tile[b] - mean) * scale + shift
            act = jnp.where(keep, silu(v), 0.0).astype(BF)
            for f in range(4):
                for d in range(3):
                    if max(f + d - 2, 0) == frame:
                        lane = (4 * d + b) * LANES
                        lhs_ref[f * 144 : (f + 1) * 144, lane : lane + LANES] = act
        own_ref[frame] = own.astype(BF)


def first_conv_kernel(lhs, small_ref, kernel_ref, out_ref, moments_ref, product, wide_rows, tight_rows):
    totals = convolve(lhs, kernel_ref, product, 144, 12, 120)
    row, column = cell_rows(104, 10)
    keep = (row >= 1) & (row <= 8) & (column >= 1) & (column <= 8)
    bias = small_ref[36:37, :]
    kept = []
    for f in range(4):
        wide_rows[f] = totals[f] + bias
        for r in range(10):
            tight_rows[f, 10 * r : 10 * r + 10, :] = wide_rows[f, 12 * r : 12 * r + 10, :]
        tight_rows[f, 100:104, :] = jnp.zeros((4, LANES), F32)
        hidden = tight_rows[f].astype(BF)
        out_ref[f] = hidden
        kept.append(jnp.where(keep, hidden.astype(F32), 0.0))
    mean = sum(jnp.sum(x, axis=0, keepdims=True) for x in kept) * (1.0 / 256)
    squares = [jnp.square(jnp.where(keep, x - mean, 0.0)) for x in kept]
    spread = sum(jnp.sum(x, axis=0, keepdims=True) for x in squares) * (1.0 / 256)
    encode(moments_ref, [(0,) + group_stats(mean, spread)])


def add_blocks(refs, shifts, kernel_ref, lhs, product, before=None):
    ta = lax.axis_index("ta")
    for k, ref in enumerate(refs):
        for f in range(4):
            for d in range(3):
                lane = (len(refs) * d + k) * LANES
                lhs[f * 112 : f * 112 + 104, lane : lane + LANES] = ref[max(f + d - 2, 0)]
    for pair in PAIRS:
        rhs = jnp.concatenate(
            [
                jnp.concatenate(
                    [
                        kernel_ref[9 * d + s, pl.ds(pl.multiple_of(turned(ta, shift) * LANES, LANES), LANES), :]
                        for s in pair
                    ],
                    axis=1,
                )
                for d in range(3)
                for shift in shifts
            ],
            axis=0,
        )
        lanes = slice(pair[0] * LANES, pair[0] * LANES + rhs.shape[1])
        part = jnp.dot(lhs[...], rhs, preferred_element_type=F32)
        product[:, lanes] = part if before is None else before[:, lanes] + part


def second_conv_first_kernel(s0, s1, kernel_ref, out_ref, lhs):
    add_blocks((s0, s1), SHIFTS[:2], kernel_ref, lhs, out_ref)


def second_conv_kernel(
    s2,
    s3,
    before_ref,
    small_ref,
    own_ref,
    kernel_ref,
    out0,
    out1,
    out2,
    out3,
    lhs,
    product,
    wide_rows,
    parts,
):
    ta = lax.axis_index("ta")
    add_blocks((s2, s3), SHIFTS[2:], kernel_ref, lhs, product, before_ref)
    totals = shifted_sums(product, 112, 10, 80)
    bias = small_ref[37:38, :]
    tiles = []
    for f in range(4):
        wide_rows[f] = totals[f] + bias
        branch = jnp.concatenate([wide_rows[f, 10 * r : 10 * r + 8, :] for r in range(8)], axis=0)
        branch = branch.astype(BF).astype(F32)
        residual = (own_ref[f].astype(F32) + branch).astype(BF)
        parts[f] = residual
        tiles.append(residual.astype(F32))
    mean, spread = channel_stats(jnp.concatenate(tiles, axis=0), None, 256)
    packed = pack_stats(mean, spread)
    for s, ref in zip(SHIFTS, (out0, out1, out2, out3)):
        ref[0:64, :] = parts[lax.rem(ta + s, 4)]
        ref[64:72, :] = packed


def normalise(x, coefficients):
    parts = []
    for b, (mean, scale, shift) in enumerate(coefficients):
        part = x[:, b * LANES : (b + 1) * LANES].astype(F32)
        parts.append(((part - mean) * scale + shift).astype(BF))
    return jnp.concatenate(parts, axis=1)


def attention_kernel(*refs):
    asked, told = refs[:4], refs[4:6]
    small_ref, query_ref, key_ref = refs[6:9]
    outs, normed = refs[9:13], refs[13]
    middle, spread = merge_stats([unpack_stats(ref[512:520, :]) for ref in told])
    inverse = lax.rsqrt(spread + EPS)
    coefficients = []
    for b in range(4):
        lanes = slice(b * LANES, (b + 1) * LANES)
        gain, shift = gain_and_shift(small_ref, 16, b)
        coefficients.append((middle[:, lanes], inverse[:, lanes] * gain, shift))
    normed_q = normalise(jnp.concatenate([ref[0:64, :] for ref in asked], axis=0), coefficients)
    for k, ref in enumerate(told):
        normed[512 * k : 512 * k + 512, :] = normalise(ref[0:512, :], coefficients)
    queries = jnp.dot(normed_q, query_ref[...], preferred_element_type=F32) + wide(small_ref, 24)
    folded = lax.dot_general(
        queries.astype(BF), key_ref[...], (((1,), (1,)), ((), ())), preferred_element_type=F32
    ) * 512 ** (-0.5)
    scores = lax.dot_general(
        folded.astype(BF), normed[...], (((1,), (1,)), ((), ())), preferred_element_type=F32
    )
    highest = jnp.max(scores, axis=1, keepdims=True)
    weights = jnp.exp(scores - highest)
    total = jnp.sum(weights, axis=1, keepdims=True)
    mixed = jnp.dot(weights.astype(BF), normed[...], preferred_element_type=F32) * (1.0 / total)
    level = highest + jnp.log(total)
    top, middle, low = thirds(level)
    lane = lax.broadcasted_iota(jnp.int32, (256, LANES), 1)
    tail = jnp.where(lane == 0, top, jnp.where(lane == 1, middle, jnp.where(lane == 2, low, 0.0)))
    for s, ref in enumerate(outs):
        ref[:, 0:512] = mixed[64 * s : 64 * s + 64].astype(BF)
        ref[:, 512:640] = tail[64 * s : 64 * s + 64].astype(BF)


def finish_kernel(b0, b1, b2, b3, residual_ref, small_ref, value_ref, output_ref, out_ref):
    backs = [ref[...].astype(F32) for ref in (b0, b1, b2, b3)]
    levels = [jnp.sum(back[:, 512:640], axis=1, keepdims=True) for back in backs]
    highest = functools.reduce(jnp.maximum, levels)
    shares = [jnp.exp(level - highest) for level in levels]
    inverse = 1.0 / sum(shares)
    mean_normed = sum(back[:, 0:512] * (share * inverse) for back, share in zip(backs, shares))
    attended = jnp.dot(mean_normed.astype(BF), value_ref[...], preferred_element_type=F32)
    attended = (attended + wide(small_ref, 28)).astype(BF)
    mixed = jnp.dot(attended, output_ref[...], preferred_element_type=F32)
    out_ref[...] = (residual_ref[0:64, :].astype(F32) + mixed + wide(small_ref, 32)).astype(BF)


def call(kernel, out_shape, specs, scratch, flops, *args):
    shapes = out_shape if isinstance(out_shape, tuple) else (out_shape,)
    moved = sum(a.size * a.dtype.itemsize for a in args) + sum(
        s.size * jnp.dtype(s.dtype).itemsize for s in shapes
    )
    return pl.pallas_call(
        kernel,
        out_shape=out_shape,
        in_specs=specs,
        out_specs=tuple(VMEM for _ in shapes) if isinstance(out_shape, tuple) else VMEM,
        scratch_shapes=scratch,
        compiler_params=pltpu.CompilerParams(vmem_limit_bytes=LIMIT),
        cost_estimate=pl.CostEstimate(flops=flops, bytes_accessed=moved, transcendentals=0),
    )(*args)


def ring(count, step):
    return [(i, (i + step) % count) for i in range(count)]


def spread_out(blocks, axis, sign=1):
    return [blocks[0]] + [lax.ppermute(b, axis, ring(4, sign * s)) for b, s in zip(blocks[1:], SHIFTS[1:])]


def around(block, axis):
    return spread_out([block] * 4, axis)


def relayed(block, axis):
    count = lax.axis_size(axis)
    after = {step: lax.ppermute(block, axis, ring(count, step)) for step in (2, 1, -1, -2)}
    further = [lax.ppermute(after[step], axis, ring(count, move)) for step, move in ((2, 2), (1, 2), (-1, -2))]
    return [block, *after.values(), *further]


def both_sides(low, high, axis):
    count = lax.axis_size(axis)
    return lax.ppermute(high, axis, ring(count, 1)), lax.ppermute(low, axis, ring(count, -1))


def over_tiles(rows):
    return lax.all_to_all(rows, HA + ("z",), split_axis=0, concat_axis=0, tiled=True)


def body(
    latent,
    norm1_gain,
    norm1_shift,
    conv1_kernel,
    conv1_shift,
    norm2_gain,
    norm2_shift,
    conv2_kernel,
    conv2_shift,
    norm3_gain,
    norm3_shift,
    query_weight,
    query_shift,
    key_weight,
    value_weight,
    value_shift,
    output_weight,
    output_shift,
):
    _, height, width, channels = latent.shape
    cells = height * width
    tiles = lax.axis_size(HA) * lax.axis_size("z")
    grid = (lax.axis_size(HA) * height, lax.axis_size("z") * width)
    vectors = [norm1_gain, norm1_shift, norm2_gain, norm2_shift, norm3_gain, norm3_shift]
    vectors += [query_shift, value_shift, output_shift, conv1_shift, conv2_shift]
    small = jnp.concatenate(vectors).reshape(-1, LANES)

    def bf(*shape):
        return jax.ShapeDtypeStruct(shape, BF)

    rows = jax.ShapeDtypeStruct((tiles, 1, LANES), F32)

    slots = around(latent[0].reshape(cells, channels), "ta")
    slots[0] = call(first_kernel, bf(cells, channels), [VMEM], [], 4 * 10**9, slots[0])
    rows1, low, high = call(
        frame_moments_kernel, (rows, bf(4, 16, channels), bf(4, 16, channels)), [VMEM] * 4, [], 10**6, *slots
    )
    top, bottom = both_sides(low, high, HA)
    rows1 = over_tiles(rows1)
    low, high = call(
        columns_kernel,
        (bf(4, 24, channels), bf(4, 24, channels)),
        [VMEM] * 6,
        [pltpu.VMEM((4, 96, LANES), F32), pltpu.VMEM((4, 24, LANES), F32)],
        10**6,
        *slots,
        top,
        bottom,
    )
    left, right = both_sides(low, high, "z")
    lhs, own = call(
        functools.partial(rimmed_kernel, grid),
        (bf(576, 1536), bf(4, cells, LANES)),
        [VMEM] * 10,
        [pltpu.VMEM((4, cells, channels), BF), pltpu.VMEM((4, 144, LANES), F32), pltpu.VMEM((4, 24, LANES), F32)],
        4 * 10**9,
        *slots,
        top,
        bottom,
        left,
        right,
        rows1,
        small,
    )
    hidden, rows2 = call(
        first_conv_kernel,
        (bf(4, 104, LANES), rows),
        [VMEM] * 3,
        [
            pltpu.VMEM((584, 1152), F32),
            pltpu.VMEM((4, 120, LANES), F32),
            pltpu.VMEM((4, 104, LANES), F32),
        ],
        2 * 10**9,
        lhs,
        small,
        conv1_kernel,
    )

    act = call(
        functools.partial(activate_kernel, grid),
        bf(4, 104, LANES),
        [VMEM] * 3,
        [],
        4 * 10**9,
        hidden,
        over_tiles(rows2),
        small,
    )
    blocks = around(act, "ta")
    before = call(
        second_conv_first_kernel,
        jax.ShapeDtypeStruct((448, 1152), F32),
        [VMEM] * 3,
        [pltpu.VMEM((448, 768), BF)],
        10**9,
        *blocks[:2],
        conv2_kernel,
    )
    parts = call(
        second_conv_kernel,
        (bf(cells + 8, LANES),) * 4,
        [VMEM] * 6,
        [
            pltpu.VMEM((448, 768), BF),
            pltpu.VMEM((448, 1152), F32),
            pltpu.VMEM((4, 80, LANES), F32),
            pltpu.VMEM((4, cells, LANES), BF),
        ],
        2 * 10**9,
        *blocks[2:],
        before,
        small,
        own,
        conv2_kernel,
    )

    residual = call(
        residual_kernel,
        bf(cells + 8, channels),
        [VMEM] * 4,
        [pltpu.VMEM((4, cells + 8, LANES), BF)],
        10**6,
        *spread_out(parts, "ta"),
    )
    asked = around(residual, "y")
    told = call(merge_kernel, bf(cells + 8, channels), [VMEM] * 4, [], 10**6, *asked)
    told = call(merge_kernel, bf(8 * cells + 8, channels), [VMEM] * 8, [], 10**6, *relayed(told, "z"))
    packed = call(
        attention_kernel,
        (bf(cells, channels + LANES),) * 4,
        [VMEM] * 9,
        [pltpu.VMEM((1024, channels), BF)],
        10**9,
        *asked,
        told,
        lax.ppermute(told, "core", ring(2, 1)),
        small,
        query_weight,
        key_weight,
    )

    block_out = call(
        finish_kernel,
        bf(cells, channels),
        [VMEM] * 8,
        [],
        10**8,
        *spread_out(packed, "y", -1),
        residual,
        small,
        value_weight,
        output_weight,
    )
    return block_out.reshape(latent.shape)


def solution(mesh):
    frames, rows, columns = mesh.devices.shape
    split = Mesh(mesh.devices.reshape(frames, rows // 2, 2, columns), ("ta", "y", "core", "z"))
    tile = P("ta", HA, "z", None)
    kernel, shift = P(None, None, "ta"), P("ta")
    in_specs = (tile, P(), P(), kernel, shift, P(), P(), kernel, shift) + (P(),) * 9
    return jax.shard_map(body, mesh=split, in_specs=in_specs, out_specs=tile, check_vma=False)
```

```python
import functools

import jax
import jax.numpy as jnp
from jax import lax
from jax.experimental import pallas as pl
from jax.experimental.pallas import tpu as pltpu
from jax.sharding import Mesh, PartitionSpec as P

GROUPS = 32
EPS = 1e-06
HA = ("y", "core")
BF = jnp.bfloat16
F32 = jnp.float32
LANES = 128
LIMIT = 32 * 1024 * 1024
SHIFTS = (0, 2, 1, 3)
PAIRS = ((0, 1), (2, 3), (4, 5), (6, 7), (8,))
VMEM = pl.BlockSpec(memory_space=pltpu.VMEM)


def lane_in_group(shape):
    return lax.broadcasted_iota(jnp.int32, shape, 1) & 15


def segment_sum(x):
    row = lax.broadcasted_iota(jnp.int32, (LANES, LANES), 0)
    column = lax.broadcasted_iota(jnp.int32, (LANES, LANES), 1)
    ones = jnp.where((row >> 4) == (column >> 4), 1.0, 0.0).astype(BF)
    pieces = jnp.concatenate([*thirds(x), jnp.zeros_like(x)], axis=0).astype(BF)
    sums = jnp.dot(pieces, ones, preferred_element_type=F32)
    return sums[0:8] + sums[8:16] + sums[16:24]


def rows8(x):
    return jnp.broadcast_to(x, (8, LANES))


def cell_rows(rows, pitch):
    index = lax.broadcasted_iota(jnp.int32, (rows, LANES), 0)
    row = (index * {10: 52429, 12: 43691}[pitch]) >> 19
    return row, index - row * pitch


def encode(out_ref, stats):
    lane = lane_in_group((8, LANES))
    row = jnp.zeros((8, LANES), F32)
    for block, mean, spread in stats:
        row = jnp.where(lane == block, mean, row)
        row = jnp.where(lane == block + 4, spread, row)
    out_ref[...] = jnp.broadcast_to(row[0:1][None], out_ref.shape)


def thirds(x):
    high = x.astype(BF).astype(F32)
    middle = (x - high).astype(BF).astype(F32)
    return high, middle, x - high - middle


def pack_stats(mean, spread):
    row = lax.broadcasted_iota(jnp.int32, mean.shape, 0)
    packed = jnp.zeros(mean.shape, F32)
    for k, piece in enumerate(thirds(mean) + thirds(spread)):
        packed = jnp.where(row == k, piece, packed)
    return packed.astype(BF)


def unpack_stats(packed):
    x = packed.astype(F32)
    return x[0:1] + x[1:2] + x[2:3], x[3:4] + x[4:5] + x[5:6]


def merge_stats(stats):
    scale = 1.0 / len(stats)
    middle = sum(mean for mean, _ in stats) * scale
    spread = sum(spread + (mean - middle) * (mean - middle) for mean, spread in stats) * scale
    return middle, spread


def all_rows(x):
    return jnp.broadcast_to(x, (8, x.shape[1]))


def channel_stats(x, keep, count):
    mean = jnp.sum(x, axis=0, keepdims=True) * (1.0 / count)
    deviation = x - mean
    if keep is not None:
        deviation = jnp.where(keep, deviation, 0.0)
    spread = jnp.sum(deviation * deviation, axis=0, keepdims=True) * (1.0 / count)
    return group_stats(mean, spread)


def group_stats(mean, spread):
    mean, spread = rows8(mean), rows8(spread)
    middle = segment_sum(mean) * (1.0 / 16)
    off = mean - middle
    return middle, segment_sum(spread + off * off) * (1.0 / 16)


def tile_stats(rows_ref):
    rows = rows_ref[...].reshape(rows_ref.shape[0], LANES)
    count = rows.shape[0]
    mean = jnp.sum(rows, axis=0, keepdims=True) * (1.0 / count)
    off = rows - mean
    between = jnp.sum(off * off, axis=0, keepdims=True) * (1.0 / count)
    return rows8(mean), rows8(between)


def block_stats(mean, between, block):
    lane = lane_in_group((8, LANES))
    middle = segment_sum(jnp.where(lane == block, mean, 0.0))
    spread = segment_sum(jnp.where(lane == block + 4, mean, jnp.where(lane == block, between, 0.0)))
    return middle[0:1], lax.rsqrt(spread[0:1] + EPS)


def decode(rows_ref, small_ref, at):
    mean, between = tile_stats(rows_ref)
    result = []
    for block in range(4):
        middle, inverse = block_stats(mean, between, block)
        gain, shift = gain_and_shift(small_ref, at, block)
        result.append((middle, inverse * gain, shift))
    return result


def gain_and_shift(small_ref, at, block):
    return small_ref[at + block : at + block + 1, :], small_ref[at + 4 + block : at + 5 + block, :]


def wide(small_ref, at):
    return jnp.concatenate([small_ref[at + b : at + b + 1, :] for b in range(4)], axis=1)


def silu(v):
    half = 0.5 * v
    return half + half * jnp.tanh(half)


def turned(ta, s):
    return lax.rem(ta - s + 4, 4)


def first_kernel(latent_ref, out_ref):
    out_ref[...] = latent_ref[...]


def frame_moments_kernel(s0, s1, s2, s3, out_ref, first_ref, last_ref):
    slots = (s0, s1, s2, s3)
    stats = []
    for block in range(4):
        x = jnp.concatenate(
            [ref[:, block * LANES : (block + 1) * LANES].astype(F32) for ref in slots], axis=0
        )
        stats.append((block,) + channel_stats(x, None, x.shape[0]))
    encode(out_ref, stats)
    for s, ref in zip(SHIFTS, slots):
        first_ref[s] = ref[0:16, :]
        last_ref[s] = ref[48:64, :]


def columns_kernel(s0, s1, s2, s3, top_ref, bottom_ref, first_ref, last_ref, tall, sides):
    for s, ref in zip(SHIFTS, (s0, s1, s2, s3)):
        for b in range(4):
            lanes = slice(b * LANES, (b + 1) * LANES)
            tall[b, 0:16, :] = top_ref[s, :, lanes].astype(F32)
            tall[b, 16:80, :] = ref[:, lanes].astype(F32)
            tall[b, 80:96, :] = bottom_ref[s, :, lanes].astype(F32)
            for k, out_ref in ((0, first_ref), (6, last_ref)):
                for j in range(2):
                    sides[b, 12 * j : 12 * j + 12, :] = tall[b, pl.ds(j + k, 12, stride=8), :]
                out_ref[s, :, lanes] = sides[b].astype(BF)


def activate_kernel(grid, hidden_ref, rows_ref, small_ref, out_ref):
    ta = lax.axis_index("ta")
    middle, inverse = block_stats(*tile_stats(rows_ref), 0)
    scale = inverse * small_ref[pl.ds(8 + ta, 1), :]
    shift = small_ref[pl.ds(12 + ta, 1), :]
    keep = inside(8 * lax.axis_index(HA) - 1, 8 * lax.axis_index("z") - 1, 104, 10, grid)
    for f in range(4):
        v = (hidden_ref[f].astype(F32) - middle) * scale + shift
        out_ref[f] = jnp.where(keep, silu(v), 0.0).astype(BF)


def residual_kernel(s0, s1, s2, s3, out_ref, parts):
    for s, ref in zip(SHIFTS, (s0, s1, s2, s3)):
        parts[turned(lax.axis_index("ta"), s)] = ref[...]
    out_ref[...] = jnp.concatenate([parts[b] for b in range(4)], axis=1)


def merge_kernel(*refs):
    slots, out_ref = refs[:-1], refs[-1]
    room = out_ref.shape[0] - 8
    middle, spread = merge_stats([unpack_stats(ref[64:72, :]) for ref in slots])
    for s in range(room // 64):
        out_ref[64 * s : 64 * s + 64, :] = slots[s][0:64, :]
    out_ref[room : room + 8, :] = pack_stats(all_rows(middle), all_rows(spread))


def convolve(lhs, weights, product, frame_rows, pitch, out_rows):
    for pair in PAIRS:
        rhs = jnp.concatenate(
            [jnp.concatenate([weights[9 * d + s] for s in pair], axis=1) for d in range(3)], axis=0
        )
        lane = pair[0] * LANES
        product[0 : 4 * frame_rows, lane : lane + rhs.shape[1]] = jnp.dot(
            lhs[...], rhs, preferred_element_type=F32
        )
    return shifted_sums(product, frame_rows, pitch, out_rows)


def shifted_sums(product, frame_rows, pitch, out_rows):
    totals = []
    for f in range(4):
        total = None
        for s in range(9):
            at = f * frame_rows + pitch * (s // 3) + s % 3
            piece = product[at : at + out_rows, s * LANES : (s + 1) * LANES]
            total = piece if total is None else total + piece
        totals.append(total)
    return totals


def inside(base_row, base_column, rows, pitch, grid):
    row, column = cell_rows(rows, pitch)
    row, column = row + base_row, column + base_column
    return (row >= 0) & (row < grid[0]) & (column >= 0) & (column < grid[1])


def rimmed_kernel(
    grid,
    s0,
    s1,
    s2,
    s3,
    top_ref,
    bottom_ref,
    left_ref,
    right_ref,
    rows_ref,
    small_ref,
    lhs_ref,
    own_ref,
    frames,
    tile,
    sides,
):
    ta = lax.axis_index("ta")
    coefficients = decode(rows_ref, small_ref, 0)
    keep = inside(8 * lax.axis_index(HA) - 2, 8 * lax.axis_index("z") - 2, 144, 12, grid)
    for s, ref in zip(SHIFTS, (s0, s1, s2, s3)):
        frames[turned(ta, s)] = ref[...]
    for frame in range(4):
        s = turned(ta, frame)
        own = jnp.zeros((64, LANES), F32)
        for b in range(4):
            lanes = slice(b * LANES, (b + 1) * LANES)
            middle = frames[frame, :, lanes].astype(F32)
            own = jnp.where(ta == b, middle, own)
            top, bottom = top_ref[s, :, lanes].astype(F32), bottom_ref[s, :, lanes].astype(F32)
            for r in range(12):
                if r < 2:
                    piece = top[8 * r : 8 * r + 8]
                elif r < 10:
                    piece = middle[8 * (r - 2) : 8 * (r - 2) + 8]
                else:
                    piece = bottom[8 * (r - 10) : 8 * (r - 10) + 8]
                tile[b, 12 * r + 2 : 12 * r + 10, :] = piece
            for k, side_ref in ((0, left_ref), (10, right_ref)):
                sides[b] = side_ref[s, :, lanes].astype(F32)
                for j in range(2):
                    tile[b, pl.ds(j + k, 12, stride=12), :] = sides[b, 12 * j : 12 * j + 12, :]
            mean, scale, shift = coefficients[b]
            v = (tile[b] - mean) * scale + shift
            act = jnp.where(keep, silu(v), 0.0).astype(BF)
            for f in range(4):
                for d in range(3):
                    if max(f + d - 2, 0) == frame:
                        lane = (4 * d + b) * LANES
                        lhs_ref[f * 144 : (f + 1) * 144, lane : lane + LANES] = act
        own_ref[frame] = own.astype(BF)


def first_conv_kernel(lhs, small_ref, kernel_ref, out_ref, moments_ref, product, wide_rows, tight_rows):
    totals = convolve(lhs, kernel_ref, product, 144, 12, 120)
    row, column = cell_rows(104, 10)
    keep = (row >= 1) & (row <= 8) & (column >= 1) & (column <= 8)
    bias = small_ref[36:37, :]
    kept = []
    for f in range(4):
        wide_rows[f] = totals[f] + bias
        for r in range(10):
            tight_rows[f, 10 * r : 10 * r + 10, :] = wide_rows[f, 12 * r : 12 * r + 10, :]
        tight_rows[f, 100:104, :] = jnp.zeros((4, LANES), F32)
        hidden = tight_rows[f].astype(BF)
        out_ref[f] = hidden
        kept.append(jnp.where(keep, hidden.astype(F32), 0.0))
    mean = sum(jnp.sum(x, axis=0, keepdims=True) for x in kept) * (1.0 / 256)
    squares = [jnp.square(jnp.where(keep, x - mean, 0.0)) for x in kept]
    spread = sum(jnp.sum(x, axis=0, keepdims=True) for x in squares) * (1.0 / 256)
    encode(moments_ref, [(0,) + group_stats(mean, spread)])


def add_blocks(refs, shifts, kernel_ref, lhs, product, before=None):
    ta = lax.axis_index("ta")
    for k, ref in enumerate(refs):
        for f in range(4):
            for d in range(3):
                lane = (len(refs) * d + k) * LANES
                lhs[f * 112 : f * 112 + 104, lane : lane + LANES] = ref[max(f + d - 2, 0)]
    for pair in PAIRS:
        rhs = jnp.concatenate(
            [
                jnp.concatenate(
                    [
                        kernel_ref[9 * d + s, pl.ds(pl.multiple_of(turned(ta, shift) * LANES, LANES), LANES), :]
                        for s in pair
                    ],
                    axis=1,
                )
                for d in range(3)
                for shift in shifts
            ],
            axis=0,
        )
        lanes = slice(pair[0] * LANES, pair[0] * LANES + rhs.shape[1])
        part = jnp.dot(lhs[...], rhs, preferred_element_type=F32)
        product[:, lanes] = part if before is None else before[:, lanes] + part


def second_conv_first_kernel(s0, s1, kernel_ref, out_ref, lhs):
    add_blocks((s0, s1), SHIFTS[:2], kernel_ref, lhs, out_ref)


def second_conv_kernel(
    s2,
    s3,
    before_ref,
    small_ref,
    own_ref,
    kernel_ref,
    out0,
    out1,
    out2,
    out3,
    lhs,
    product,
    wide_rows,
    parts,
):
    ta = lax.axis_index("ta")
    add_blocks((s2, s3), SHIFTS[2:], kernel_ref, lhs, product, before_ref)
    totals = shifted_sums(product, 112, 10, 80)
    bias = small_ref[37:38, :]
    tiles = []
    for f in range(4):
        wide_rows[f] = totals[f] + bias
        branch = jnp.concatenate([wide_rows[f, 10 * r : 10 * r + 8, :] for r in range(8)], axis=0)
        branch = branch.astype(BF).astype(F32)
        residual = (own_ref[f].astype(F32) + branch).astype(BF)
        parts[f] = residual
        tiles.append(residual.astype(F32))
    mean, spread = channel_stats(jnp.concatenate(tiles, axis=0), None, 256)
    packed = pack_stats(mean, spread)
    for s, ref in zip(SHIFTS, (out0, out1, out2, out3)):
        ref[0:64, :] = parts[lax.rem(ta + s, 4)]
        ref[64:72, :] = packed


def normalise(x, coefficients):
    parts = []
    for b, (mean, scale, shift) in enumerate(coefficients):
        part = x[:, b * LANES : (b + 1) * LANES].astype(F32)
        parts.append(((part - mean) * scale + shift).astype(BF))
    return jnp.concatenate(parts, axis=1)


def attention_kernel(*refs):
    asked, told = refs[:4], refs[4:6]
    small_ref, query_ref, key_ref = refs[6:9]
    outs, normed = refs[9:13], refs[13]
    middle, spread = merge_stats([unpack_stats(ref[512:520, :]) for ref in told])
    inverse = lax.rsqrt(spread + EPS)
    coefficients = []
    for b in range(4):
        lanes = slice(b * LANES, (b + 1) * LANES)
        gain, shift = gain_and_shift(small_ref, 16, b)
        coefficients.append((middle[:, lanes], inverse[:, lanes] * gain, shift))
    normed_q = normalise(jnp.concatenate([ref[0:64, :] for ref in asked], axis=0), coefficients)
    for k, ref in enumerate(told):
        normed[512 * k : 512 * k + 512, :] = normalise(ref[0:512, :], coefficients)
    queries = jnp.dot(normed_q, query_ref[...], preferred_element_type=F32) + wide(small_ref, 24)
    folded = lax.dot_general(
        queries.astype(BF), key_ref[...], (((1,), (1,)), ((), ())), preferred_element_type=F32
    ) * 512 ** (-0.5)
    scores = lax.dot_general(
        folded.astype(BF), normed[...], (((1,), (1,)), ((), ())), preferred_element_type=F32
    )
    highest = jnp.max(scores, axis=1, keepdims=True)
    weights = jnp.exp(scores - highest)
    total = jnp.sum(weights, axis=1, keepdims=True)
    mixed = jnp.dot(weights.astype(BF), normed[...], preferred_element_type=F32) * (1.0 / total)
    level = highest + jnp.log(total)
    top, middle, low = thirds(level)
    lane = lax.broadcasted_iota(jnp.int32, (256, LANES), 1)
    tail = jnp.where(lane == 0, top, jnp.where(lane == 1, middle, jnp.where(lane == 2, low, 0.0)))
    for s, ref in enumerate(outs):
        ref[:, 0:512] = mixed[64 * s : 64 * s + 64].astype(BF)
        ref[:, 512:640] = tail[64 * s : 64 * s + 64].astype(BF)


def finish_kernel(b0, b1, b2, b3, residual_ref, small_ref, value_ref, output_ref, out_ref):
    backs = [ref[...].astype(F32) for ref in (b0, b1, b2, b3)]
    levels = [jnp.sum(back[:, 512:640], axis=1, keepdims=True) for back in backs]
    highest = functools.reduce(jnp.maximum, levels)
    shares = [jnp.exp(level - highest) for level in levels]
    inverse = 1.0 / sum(shares)
    mean_normed = sum(back[:, 0:512] * (share * inverse) for back, share in zip(backs, shares))
    attended = jnp.dot(mean_normed.astype(BF), value_ref[...], preferred_element_type=F32)
    attended = (attended + wide(small_ref, 28)).astype(BF)
    mixed = jnp.dot(attended, output_ref[...], preferred_element_type=F32)
    out_ref[...] = (residual_ref[0:64, :].astype(F32) + mixed + wide(small_ref, 32)).astype(BF)


def call(kernel, out_shape, specs, scratch, flops, *args):
    shapes = out_shape if isinstance(out_shape, tuple) else (out_shape,)
    moved = sum(a.size * a.dtype.itemsize for a in args) + sum(
        s.size * jnp.dtype(s.dtype).itemsize for s in shapes
    )
    return pl.pallas_call(
        kernel,
        out_shape=out_shape,
        in_specs=specs,
        out_specs=tuple(VMEM for _ in shapes) if isinstance(out_shape, tuple) else VMEM,
        scratch_shapes=scratch,
        compiler_params=pltpu.CompilerParams(vmem_limit_bytes=LIMIT),
        cost_estimate=pl.CostEstimate(flops=flops, bytes_accessed=moved, transcendentals=0),
    )(*args)


def ring(count, step):
    return [(i, (i + step) % count) for i in range(count)]


def spread_out(blocks, axis, sign=1):
    return [blocks[0]] + [lax.ppermute(b, axis, ring(4, sign * s)) for b, s in zip(blocks[1:], SHIFTS[1:])]


def around(block, axis):
    return spread_out([block] * 4, axis)


def relayed(block):
    def moved(x, step):
        pairs = [(z, (z + step) % 8) for z in range(8)] + [(8 + z, 8 + (z - step) % 8) for z in range(8)]
        return lax.ppermute(x, ("core", "z"), pairs)

    after = {step: moved(block, step) for step in (2, 1, -1, -2)}
    further = [moved(after[step], move) for step, move in ((2, 2), (1, 2), (-1, -2))]
    return [block, *after.values(), *further]


def both_sides(low, high, axis):
    count = lax.axis_size(axis)
    return lax.ppermute(high, axis, ring(count, 1)), lax.ppermute(low, axis, ring(count, -1))


def over_tiles(rows):
    return lax.all_to_all(rows, HA + ("z",), split_axis=0, concat_axis=0, tiled=True)


def body(
    latent,
    norm1_gain,
    norm1_shift,
    conv1_kernel,
    conv1_shift,
    norm2_gain,
    norm2_shift,
    conv2_kernel,
    conv2_shift,
    norm3_gain,
    norm3_shift,
    query_weight,
    query_shift,
    key_weight,
    value_weight,
    value_shift,
    output_weight,
    output_shift,
):
    _, height, width, channels = latent.shape
    cells = height * width
    tiles = lax.axis_size(HA) * lax.axis_size("z")
    grid = (lax.axis_size(HA) * height, lax.axis_size("z") * width)
    vectors = [norm1_gain, norm1_shift, norm2_gain, norm2_shift, norm3_gain, norm3_shift]
    vectors += [query_shift, value_shift, output_shift, conv1_shift, conv2_shift]
    small = jnp.concatenate(vectors).reshape(-1, LANES)

    def bf(*shape):
        return jax.ShapeDtypeStruct(shape, BF)

    rows = jax.ShapeDtypeStruct((tiles, 1, LANES), F32)

    slots = around(latent[0].reshape(cells, channels), "ta")
    slots[0] = call(first_kernel, bf(cells, channels), [VMEM], [], 4 * 10**9, slots[0])
    rows1, low, high = call(
        frame_moments_kernel, (rows, bf(4, 16, channels), bf(4, 16, channels)), [VMEM] * 4, [], 10**6, *slots
    )
    top, bottom = both_sides(low, high, HA)
    rows1 = over_tiles(rows1)
    low, high = call(
        columns_kernel,
        (bf(4, 24, channels), bf(4, 24, channels)),
        [VMEM] * 6,
        [pltpu.VMEM((4, 96, LANES), F32), pltpu.VMEM((4, 24, LANES), F32)],
        10**6,
        *slots,
        top,
        bottom,
    )
    left, right = both_sides(low, high, "z")
    lhs, own = call(
        functools.partial(rimmed_kernel, grid),
        (bf(576, 1536), bf(4, cells, LANES)),
        [VMEM] * 10,
        [pltpu.VMEM((4, cells, channels), BF), pltpu.VMEM((4, 144, LANES), F32), pltpu.VMEM((4, 24, LANES), F32)],
        4 * 10**9,
        *slots,
        top,
        bottom,
        left,
        right,
        rows1,
        small,
    )
    hidden, rows2 = call(
        first_conv_kernel,
        (bf(4, 104, LANES), rows),
        [VMEM] * 3,
        [
            pltpu.VMEM((584, 1152), F32),
            pltpu.VMEM((4, 120, LANES), F32),
            pltpu.VMEM((4, 104, LANES), F32),
        ],
        2 * 10**9,
        lhs,
        small,
        conv1_kernel,
    )

    act = call(
        functools.partial(activate_kernel, grid),
        bf(4, 104, LANES),
        [VMEM] * 3,
        [],
        4 * 10**9,
        hidden,
        over_tiles(rows2),
        small,
    )
    blocks = around(act, "ta")
    before = call(
        second_conv_first_kernel,
        jax.ShapeDtypeStruct((448, 1152), F32),
        [VMEM] * 3,
        [pltpu.VMEM((448, 768), BF)],
        10**9,
        *blocks[:2],
        conv2_kernel,
    )
    parts = call(
        second_conv_kernel,
        (bf(cells + 8, LANES),) * 4,
        [VMEM] * 6,
        [
            pltpu.VMEM((448, 768), BF),
            pltpu.VMEM((448, 1152), F32),
            pltpu.VMEM((4, 80, LANES), F32),
            pltpu.VMEM((4, cells, LANES), BF),
        ],
        2 * 10**9,
        *blocks[2:],
        before,
        small,
        own,
        conv2_kernel,
    )

    residual = call(
        residual_kernel,
        bf(cells + 8, channels),
        [VMEM] * 4,
        [pltpu.VMEM((4, cells + 8, LANES), BF)],
        10**6,
        *spread_out(parts, "ta"),
    )
    asked = around(residual, "y")
    told = call(merge_kernel, bf(cells + 8, channels), [VMEM] * 4, [], 10**6, *asked)
    told = call(merge_kernel, bf(8 * cells + 8, channels), [VMEM] * 8, [], 10**6, *relayed(told))
    packed = call(
        attention_kernel,
        (bf(cells, channels + LANES),) * 4,
        [VMEM] * 9,
        [pltpu.VMEM((1024, channels), BF)],
        10**9,
        *asked,
        told,
        lax.ppermute(told, "core", ring(2, 1)),
        small,
        query_weight,
        key_weight,
    )

    block_out = call(
        finish_kernel,
        bf(cells, channels),
        [VMEM] * 8,
        [],
        10**8,
        *spread_out(packed, "y", -1),
        residual,
        small,
        value_weight,
        output_weight,
    )
    return block_out.reshape(latent.shape)


def solution(mesh):
    frames, rows, columns = mesh.devices.shape
    split = Mesh(mesh.devices.reshape(frames, rows // 2, 2, columns), ("ta", "y", "core", "z"))
    tile = P("ta", HA, "z", None)
    kernel, shift = P(None, None, "ta"), P("ta")
    in_specs = (tile, P(), P(), kernel, shift, P(), P(), kernel, shift) + (P(),) * 9
    return jax.shard_map(body, mesh=split, in_specs=in_specs, out_specs=tile, check_vma=False)
```

```python
import functools

import jax
import jax.numpy as jnp
from jax import lax
from jax.experimental import pallas as pl
from jax.experimental.pallas import tpu as pltpu
from jax.sharding import Mesh, PartitionSpec as P

GROUPS = 32
EPS = 1e-06
HA = ("y", "core")
BF = jnp.bfloat16
F32 = jnp.float32
LANES = 128
LIMIT = 32 * 1024 * 1024
SHIFTS = (0, 2, 1, 3)
PAIRS = ((0, 1), (2, 3), (4, 5), (6, 7), (8,))
FOURS = ((0, 1, 2, 3), (4, 5, 6, 7), (8,))
VMEM = pl.BlockSpec(memory_space=pltpu.VMEM)


def lane_in_group(shape):
    return lax.broadcasted_iota(jnp.int32, shape, 1) & 15


def segment_sum(x):
    row = lax.broadcasted_iota(jnp.int32, (LANES, LANES), 0)
    column = lax.broadcasted_iota(jnp.int32, (LANES, LANES), 1)
    ones = jnp.where((row >> 4) == (column >> 4), 1.0, 0.0).astype(BF)
    pieces = jnp.concatenate([*thirds(x), jnp.zeros_like(x)], axis=0).astype(BF)
    sums = jnp.dot(pieces, ones, preferred_element_type=F32)
    return sums[0:8] + sums[8:16] + sums[16:24]


def rows8(x):
    return jnp.broadcast_to(x, (8, LANES))


def cell_rows(rows, pitch):
    index = lax.broadcasted_iota(jnp.int32, (rows, LANES), 0)
    row = (index * {10: 52429, 12: 43691}[pitch]) >> 19
    return row, index - row * pitch


def encode(out_ref, stats):
    lane = lane_in_group((8, LANES))
    row = jnp.zeros((8, LANES), F32)
    for block, mean, spread in stats:
        row = jnp.where(lane == block, mean, row)
        row = jnp.where(lane == block + 4, spread, row)
    out_ref[...] = jnp.broadcast_to(row[0:1][None], out_ref.shape)


def thirds(x):
    high = x.astype(BF).astype(F32)
    middle = (x - high).astype(BF).astype(F32)
    return high, middle, x - high - middle


def pack_stats(mean, spread):
    row = lax.broadcasted_iota(jnp.int32, mean.shape, 0)
    packed = jnp.zeros(mean.shape, F32)
    for k, piece in enumerate(thirds(mean) + thirds(spread)):
        packed = jnp.where(row == k, piece, packed)
    return packed.astype(BF)


def unpack_stats(packed):
    x = packed.astype(F32)
    return x[0:1] + x[1:2] + x[2:3], x[3:4] + x[4:5] + x[5:6]


def merge_stats(stats):
    scale = 1.0 / len(stats)
    middle = sum(mean for mean, _ in stats) * scale
    spread = sum(spread + (mean - middle) * (mean - middle) for mean, spread in stats) * scale
    return middle, spread


def all_rows(x):
    return jnp.broadcast_to(x, (8, x.shape[1]))


def channel_stats(x, keep, count):
    mean = jnp.sum(x, axis=0, keepdims=True) * (1.0 / count)
    deviation = x - mean
    if keep is not None:
        deviation = jnp.where(keep, deviation, 0.0)
    spread = jnp.sum(deviation * deviation, axis=0, keepdims=True) * (1.0 / count)
    return group_stats(mean, spread)


def group_stats(mean, spread):
    mean, spread = rows8(mean), rows8(spread)
    middle = segment_sum(mean) * (1.0 / 16)
    off = mean - middle
    return middle, segment_sum(spread + off * off) * (1.0 / 16)


def tile_stats(rows_ref):
    rows = rows_ref[...].reshape(rows_ref.shape[0], LANES)
    count = rows.shape[0]
    mean = jnp.sum(rows, axis=0, keepdims=True) * (1.0 / count)
    off = rows - mean
    between = jnp.sum(off * off, axis=0, keepdims=True) * (1.0 / count)
    return rows8(mean), rows8(between)


def block_stats(mean, between, block):
    lane = lane_in_group((8, LANES))
    middle = segment_sum(jnp.where(lane == block, mean, 0.0))
    spread = segment_sum(jnp.where(lane == block + 4, mean, jnp.where(lane == block, between, 0.0)))
    return middle[0:1], lax.rsqrt(spread[0:1] + EPS)


def decode(rows_ref, small_ref, at):
    mean, between = tile_stats(rows_ref)
    result = []
    for block in range(4):
        middle, inverse = block_stats(mean, between, block)
        gain, shift = gain_and_shift(small_ref, at, block)
        result.append((middle, inverse * gain, shift))
    return result


def gain_and_shift(small_ref, at, block):
    return small_ref[at + block : at + block + 1, :], small_ref[at + 4 + block : at + 5 + block, :]


def wide(small_ref, at):
    return jnp.concatenate([small_ref[at + b : at + b + 1, :] for b in range(4)], axis=1)


def silu(v):
    half = 0.5 * v
    return half + half * jnp.tanh(half)


def turned(ta, s):
    return lax.rem(ta - s + 4, 4)


def first_kernel(latent_ref, out_ref):
    out_ref[...] = latent_ref[...]


def frame_moments_kernel(s0, s1, s2, s3, out_ref, first_ref, last_ref):
    slots = (s0, s1, s2, s3)
    stats = []
    for block in range(4):
        x = jnp.concatenate(
            [ref[:, block * LANES : (block + 1) * LANES].astype(F32) for ref in slots], axis=0
        )
        stats.append((block,) + channel_stats(x, None, x.shape[0]))
    encode(out_ref, stats)
    for s, ref in zip(SHIFTS, slots):
        first_ref[s] = ref[0:16, :]
        last_ref[s] = ref[48:64, :]


def columns_kernel(s0, s1, s2, s3, top_ref, bottom_ref, first_ref, last_ref, tall, sides):
    for s, ref in zip(SHIFTS, (s0, s1, s2, s3)):
        for b in range(4):
            lanes = slice(b * LANES, (b + 1) * LANES)
            tall[b, 0:16, :] = top_ref[s, :, lanes].astype(F32)
            tall[b, 16:80, :] = ref[:, lanes].astype(F32)
            tall[b, 80:96, :] = bottom_ref[s, :, lanes].astype(F32)
            for k, out_ref in ((0, first_ref), (6, last_ref)):
                for j in range(2):
                    sides[b, 12 * j : 12 * j + 12, :] = tall[b, pl.ds(j + k, 12, stride=8), :]
                out_ref[s, :, lanes] = sides[b].astype(BF)


def activate_kernel(grid, hidden_ref, rows_ref, small_ref, out_ref):
    ta = lax.axis_index("ta")
    middle, inverse = block_stats(*tile_stats(rows_ref), 0)
    scale = inverse * small_ref[pl.ds(8 + ta, 1), :]
    shift = small_ref[pl.ds(12 + ta, 1), :]
    keep = inside(8 * lax.axis_index(HA) - 1, 8 * lax.axis_index("z") - 1, 104, 10, grid)
    for f in range(4):
        v = (hidden_ref[f].astype(F32) - middle) * scale + shift
        out_ref[f] = jnp.where(keep, silu(v), 0.0).astype(BF)


def residual_kernel(s0, s1, s2, s3, out_ref, parts):
    for s, ref in zip(SHIFTS, (s0, s1, s2, s3)):
        parts[turned(lax.axis_index("ta"), s)] = ref[...]
    out_ref[...] = jnp.concatenate([parts[b] for b in range(4)], axis=1)


def merge_kernel(*refs):
    slots, out_ref = refs[:-1], refs[-1]
    room = out_ref.shape[0] - 8
    middle, spread = merge_stats([unpack_stats(ref[64:72, :]) for ref in slots])
    for s in range(room // 64):
        out_ref[64 * s : 64 * s + 64, :] = slots[s][0:64, :]
    out_ref[room : room + 8, :] = pack_stats(all_rows(middle), all_rows(spread))


def convolve(lhs, weights, product, frame_rows, pitch, out_rows):
    for four in FOURS:
        rhs = jnp.concatenate(
            [jnp.concatenate([weights[9 * d + s] for s in four], axis=1) for d in range(3)], axis=0
        )
        lane = four[0] * LANES
        product[0 : 4 * frame_rows, lane : lane + rhs.shape[1]] = jnp.dot(
            lhs[...], rhs, preferred_element_type=F32
        )
    return shifted_sums(product, frame_rows, pitch, out_rows)


def shifted_sums(product, frame_rows, pitch, out_rows):
    totals = []
    for f in range(4):
        total = None
        for s in range(9):
            at = f * frame_rows + pitch * (s // 3) + s % 3
            piece = product[at : at + out_rows, s * LANES : (s + 1) * LANES]
            total = piece if total is None else total + piece
        totals.append(total)
    return totals


def inside(base_row, base_column, rows, pitch, grid):
    row, column = cell_rows(rows, pitch)
    row, column = row + base_row, column + base_column
    return (row >= 0) & (row < grid[0]) & (column >= 0) & (column < grid[1])


def rimmed_kernel(
    grid,
    s0,
    s1,
    s2,
    s3,
    top_ref,
    bottom_ref,
    left_ref,
    right_ref,
    rows_ref,
    small_ref,
    lhs_ref,
    own_ref,
    frames,
    tile,
    sides,
):
    ta = lax.axis_index("ta")
    coefficients = decode(rows_ref, small_ref, 0)
    keep = inside(8 * lax.axis_index(HA) - 2, 8 * lax.axis_index("z") - 2, 144, 12, grid)
    for s, ref in zip(SHIFTS, (s0, s1, s2, s3)):
        frames[turned(ta, s)] = ref[...]
    for frame in range(4):
        s = turned(ta, frame)
        own = jnp.zeros((64, LANES), F32)
        for b in range(4):
            lanes = slice(b * LANES, (b + 1) * LANES)
            middle = frames[frame, :, lanes].astype(F32)
            own = jnp.where(ta == b, middle, own)
            top, bottom = top_ref[s, :, lanes].astype(F32), bottom_ref[s, :, lanes].astype(F32)
            for r in range(12):
                if r < 2:
                    piece = top[8 * r : 8 * r + 8]
                elif r < 10:
                    piece = middle[8 * (r - 2) : 8 * (r - 2) + 8]
                else:
                    piece = bottom[8 * (r - 10) : 8 * (r - 10) + 8]
                tile[b, 12 * r + 2 : 12 * r + 10, :] = piece
            for k, side_ref in ((0, left_ref), (10, right_ref)):
                sides[b] = side_ref[s, :, lanes].astype(F32)
                for j in range(2):
                    tile[b, pl.ds(j + k, 12, stride=12), :] = sides[b, 12 * j : 12 * j + 12, :]
            mean, scale, shift = coefficients[b]
            v = (tile[b] - mean) * scale + shift
            act = jnp.where(keep, silu(v), 0.0).astype(BF)
            for f in range(4):
                for d in range(3):
                    if max(f + d - 2, 0) == frame:
                        lane = (4 * d + b) * LANES
                        lhs_ref[f * 144 : (f + 1) * 144, lane : lane + LANES] = act
        own_ref[frame] = own.astype(BF)


def first_conv_kernel(lhs, small_ref, kernel_ref, out_ref, moments_ref, product, wide_rows, tight_rows):
    totals = convolve(lhs, kernel_ref, product, 144, 12, 120)
    row, column = cell_rows(104, 10)
    keep = (row >= 1) & (row <= 8) & (column >= 1) & (column <= 8)
    bias = small_ref[36:37, :]
    kept = []
    for f in range(4):
        wide_rows[f] = totals[f] + bias
        for r in range(10):
            tight_rows[f, 10 * r : 10 * r + 10, :] = wide_rows[f, 12 * r : 12 * r + 10, :]
        tight_rows[f, 100:104, :] = jnp.zeros((4, LANES), F32)
        hidden = tight_rows[f].astype(BF)
        out_ref[f] = hidden
        kept.append(jnp.where(keep, hidden.astype(F32), 0.0))
    mean = sum(jnp.sum(x, axis=0, keepdims=True) for x in kept) * (1.0 / 256)
    squares = [jnp.square(jnp.where(keep, x - mean, 0.0)) for x in kept]
    spread = sum(jnp.sum(x, axis=0, keepdims=True) for x in squares) * (1.0 / 256)
    encode(moments_ref, [(0,) + group_stats(mean, spread)])


def add_blocks(refs, shifts, kernel_ref, lhs, product, before=None):
    ta = lax.axis_index("ta")
    for k, ref in enumerate(refs):
        for f in range(4):
            for d in range(3):
                lane = (len(refs) * d + k) * LANES
                lhs[f * 112 : f * 112 + 104, lane : lane + LANES] = ref[max(f + d - 2, 0)]
    for pair in PAIRS:
        rhs = jnp.concatenate(
            [
                jnp.concatenate(
                    [
                        kernel_ref[9 * d + s, pl.ds(pl.multiple_of(turned(ta, shift) * LANES, LANES), LANES), :]
                        for s in pair
                    ],
                    axis=1,
                )
                for d in range(3)
                for shift in shifts
            ],
            axis=0,
        )
        lanes = slice(pair[0] * LANES, pair[0] * LANES + rhs.shape[1])
        part = jnp.dot(lhs[...], rhs, preferred_element_type=F32)
        product[:, lanes] = part if before is None else before[:, lanes] + part


def second_conv_first_kernel(s0, s1, kernel_ref, out_ref, lhs):
    add_blocks((s0, s1), (0, 1), kernel_ref, lhs, out_ref)


def second_conv_kernel(
    s2,
    s3,
    before_ref,
    small_ref,
    own_ref,
    kernel_ref,
    out0,
    out1,
    out2,
    out3,
    lhs,
    product,
    wide_rows,
    parts,
):
    ta = lax.axis_index("ta")
    add_blocks((s2, s3), (2, 3), kernel_ref, lhs, product, before_ref)
    totals = shifted_sums(product, 112, 10, 80)
    bias = small_ref[37:38, :]
    tiles = []
    for f in range(4):
        wide_rows[f] = totals[f] + bias
        branch = jnp.concatenate([wide_rows[f, 10 * r : 10 * r + 8, :] for r in range(8)], axis=0)
        branch = branch.astype(BF).astype(F32)
        residual = (own_ref[f].astype(F32) + branch).astype(BF)
        parts[f] = residual
        tiles.append(residual.astype(F32))
    mean, spread = channel_stats(jnp.concatenate(tiles, axis=0), None, 256)
    packed = pack_stats(mean, spread)
    for s, ref in zip(SHIFTS, (out0, out1, out2, out3)):
        ref[0:64, :] = parts[lax.rem(ta + s, 4)]
        ref[64:72, :] = packed


def normalise(x, coefficients):
    parts = []
    for b, (mean, scale, shift) in enumerate(coefficients):
        part = x[:, b * LANES : (b + 1) * LANES].astype(F32)
        parts.append(((part - mean) * scale + shift).astype(BF))
    return jnp.concatenate(parts, axis=1)


def attention_kernel(*refs):
    asked, told = refs[:4], refs[4:6]
    small_ref, query_ref, key_ref = refs[6:9]
    outs, normed = refs[9:13], refs[13]
    middle, spread = merge_stats([unpack_stats(ref[512:520, :]) for ref in told])
    inverse = lax.rsqrt(spread + EPS)
    coefficients = []
    for b in range(4):
        lanes = slice(b * LANES, (b + 1) * LANES)
        gain, shift = gain_and_shift(small_ref, 16, b)
        coefficients.append((middle[:, lanes], inverse[:, lanes] * gain, shift))
    normed_q = normalise(jnp.concatenate([ref[0:64, :] for ref in asked], axis=0), coefficients)
    for k, ref in enumerate(told):
        normed[512 * k : 512 * k + 512, :] = normalise(ref[0:512, :], coefficients)
    queries = jnp.dot(normed_q, query_ref[...], preferred_element_type=F32) + wide(small_ref, 24)
    folded = lax.dot_general(
        queries.astype(BF), key_ref[...], (((1,), (1,)), ((), ())), preferred_element_type=F32
    ) * 512 ** (-0.5)
    scores = lax.dot_general(
        folded.astype(BF), normed[...], (((1,), (1,)), ((), ())), preferred_element_type=F32
    )
    highest = jnp.max(scores, axis=1, keepdims=True)
    weights = jnp.exp(scores - highest)
    total = jnp.sum(weights, axis=1, keepdims=True)
    mixed = jnp.dot(weights.astype(BF), normed[...], preferred_element_type=F32) * (1.0 / total)
    level = highest + jnp.log(total)
    top, middle, low = thirds(level)
    lane = lax.broadcasted_iota(jnp.int32, (256, LANES), 1)
    tail = jnp.where(lane == 0, top, jnp.where(lane == 1, middle, jnp.where(lane == 2, low, 0.0)))
    for s, ref in enumerate(outs):
        ref[:, 0:512] = mixed[64 * s : 64 * s + 64].astype(BF)
        ref[:, 512:640] = tail[64 * s : 64 * s + 64].astype(BF)


def finish_kernel(b0, b1, b2, b3, residual_ref, small_ref, value_ref, output_ref, out_ref):
    backs = [ref[...].astype(F32) for ref in (b0, b1, b2, b3)]
    levels = [jnp.sum(back[:, 512:640], axis=1, keepdims=True) for back in backs]
    highest = functools.reduce(jnp.maximum, levels)
    shares = [jnp.exp(level - highest) for level in levels]
    inverse = 1.0 / sum(shares)
    mean_normed = sum(back[:, 0:512] * (share * inverse) for back, share in zip(backs, shares))
    attended = jnp.dot(mean_normed.astype(BF), value_ref[...], preferred_element_type=F32)
    attended = (attended + wide(small_ref, 28)).astype(BF)
    mixed = jnp.dot(attended, output_ref[...], preferred_element_type=F32)
    out_ref[...] = (residual_ref[0:64, :].astype(F32) + mixed + wide(small_ref, 32)).astype(BF)


def call(kernel, out_shape, specs, scratch, flops, *args):
    shapes = out_shape if isinstance(out_shape, tuple) else (out_shape,)
    moved = sum(a.size * a.dtype.itemsize for a in args) + sum(
        s.size * jnp.dtype(s.dtype).itemsize for s in shapes
    )
    return pl.pallas_call(
        kernel,
        out_shape=out_shape,
        in_specs=specs,
        out_specs=tuple(VMEM for _ in shapes) if isinstance(out_shape, tuple) else VMEM,
        scratch_shapes=scratch,
        compiler_params=pltpu.CompilerParams(vmem_limit_bytes=LIMIT),
        cost_estimate=pl.CostEstimate(flops=flops, bytes_accessed=moved, transcendentals=0),
    )(*args)


def ring(count, step):
    return [(i, (i + step) % count) for i in range(count)]


def spread_out(blocks, axis, sign=1):
    return [blocks[0]] + [lax.ppermute(b, axis, ring(4, sign * s)) for b, s in zip(blocks[1:], SHIFTS[1:])]


def around(block, axis):
    return spread_out([block] * 4, axis)


def relayed(block, axis):
    count = lax.axis_size(axis)
    after = {step: lax.ppermute(block, axis, ring(count, step)) for step in (2, 1, -1, -2)}
    further = [lax.ppermute(after[step], axis, ring(count, move)) for step, move in ((2, 2), (1, 2), (-1, -2))]
    return [block, *after.values(), *further]


def both_sides(low, high, axis):
    count = lax.axis_size(axis)
    return lax.ppermute(high, axis, ring(count, 1)), lax.ppermute(low, axis, ring(count, -1))


def over_tiles(rows):
    return lax.all_to_all(rows, HA + ("z",), split_axis=0, concat_axis=0, tiled=True)


def body(
    latent,
    norm1_gain,
    norm1_shift,
    conv1_kernel,
    conv1_shift,
    norm2_gain,
    norm2_shift,
    conv2_kernel,
    conv2_shift,
    norm3_gain,
    norm3_shift,
    query_weight,
    query_shift,
    key_weight,
    value_weight,
    value_shift,
    output_weight,
    output_shift,
):
    _, height, width, channels = latent.shape
    cells = height * width
    tiles = lax.axis_size(HA) * lax.axis_size("z")
    grid = (lax.axis_size(HA) * height, lax.axis_size("z") * width)
    vectors = [norm1_gain, norm1_shift, norm2_gain, norm2_shift, norm3_gain, norm3_shift]
    vectors += [query_shift, value_shift, output_shift, conv1_shift, conv2_shift]
    small = jnp.concatenate(vectors).reshape(-1, LANES)

    def bf(*shape):
        return jax.ShapeDtypeStruct(shape, BF)

    rows = jax.ShapeDtypeStruct((tiles, 1, LANES), F32)

    slots = around(latent[0].reshape(cells, channels), "ta")
    slots[0] = call(first_kernel, bf(cells, channels), [VMEM], [], 4 * 10**9, slots[0])
    rows1, low, high = call(
        frame_moments_kernel, (rows, bf(4, 16, channels), bf(4, 16, channels)), [VMEM] * 4, [], 10**6, *slots
    )
    top, bottom = both_sides(low, high, HA)
    rows1 = over_tiles(rows1)
    low, high = call(
        columns_kernel,
        (bf(4, 24, channels), bf(4, 24, channels)),
        [VMEM] * 6,
        [pltpu.VMEM((4, 96, LANES), F32), pltpu.VMEM((4, 24, LANES), F32)],
        10**6,
        *slots,
        top,
        bottom,
    )
    left, right = both_sides(low, high, "z")
    lhs, own = call(
        functools.partial(rimmed_kernel, grid),
        (bf(576, 1536), bf(4, cells, LANES)),
        [VMEM] * 10,
        [pltpu.VMEM((4, cells, channels), BF), pltpu.VMEM((4, 144, LANES), F32), pltpu.VMEM((4, 24, LANES), F32)],
        4 * 10**9,
        *slots,
        top,
        bottom,
        left,
        right,
        rows1,
        small,
    )
    hidden, rows2 = call(
        first_conv_kernel,
        (bf(4, 104, LANES), rows),
        [VMEM] * 3,
        [
            pltpu.VMEM((584, 1152), F32),
            pltpu.VMEM((4, 120, LANES), F32),
            pltpu.VMEM((4, 104, LANES), F32),
        ],
        2 * 10**9,
        lhs,
        small,
        conv1_kernel,
    )

    act = call(
        functools.partial(activate_kernel, grid),
        bf(4, 104, LANES),
        [VMEM] * 3,
        [],
        4 * 10**9,
        hidden,
        over_tiles(rows2),
        small,
    )
    blocks = [act] + [lax.ppermute(act, "ta", ring(4, shift)) for shift in (1, 2, 3)]
    before = call(
        second_conv_first_kernel,
        jax.ShapeDtypeStruct((448, 1152), F32),
        [VMEM] * 3,
        [pltpu.VMEM((448, 768), BF)],
        10**9,
        *blocks[:2],
        conv2_kernel,
    )
    parts = call(
        second_conv_kernel,
        (bf(cells + 8, LANES),) * 4,
        [VMEM] * 6,
        [
            pltpu.VMEM((448, 768), BF),
            pltpu.VMEM((448, 1152), F32),
            pltpu.VMEM((4, 80, LANES), F32),
            pltpu.VMEM((4, cells, LANES), BF),
        ],
        2 * 10**9,
        *blocks[2:],
        before,
        small,
        own,
        conv2_kernel,
    )

    residual = call(
        residual_kernel,
        bf(cells + 8, channels),
        [VMEM] * 4,
        [pltpu.VMEM((4, cells + 8, LANES), BF)],
        10**6,
        *spread_out(parts, "ta"),
    )
    asked = around(residual, "y")
    told = call(merge_kernel, bf(cells + 8, channels), [VMEM] * 4, [], 10**6, *asked)
    told = call(merge_kernel, bf(8 * cells + 8, channels), [VMEM] * 8, [], 10**6, *relayed(told, "z"))
    packed = call(
        attention_kernel,
        (bf(cells, channels + LANES),) * 4,
        [VMEM] * 9,
        [pltpu.VMEM((1024, channels), BF)],
        10**9,
        *asked,
        told,
        lax.ppermute(told, "core", ring(2, 1)),
        small,
        query_weight,
        key_weight,
    )

    block_out = call(
        finish_kernel,
        bf(cells, channels),
        [VMEM] * 8,
        [],
        10**8,
        *spread_out(packed, "y", -1),
        residual,
        small,
        value_weight,
        output_weight,
    )
    return block_out.reshape(latent.shape)


def solution(mesh):
    frames, rows, columns = mesh.devices.shape
    split = Mesh(mesh.devices.reshape(frames, rows // 2, 2, columns), ("ta", "y", "core", "z"))
    tile = P("ta", HA, "z", None)
    kernel, shift = P(None, None, "ta"), P("ta")
    in_specs = (tile, P(), P(), kernel, shift, P(), P(), kernel, shift) + (P(),) * 9
    return jax.shard_map(body, mesh=split, in_specs=in_specs, out_specs=tile, check_vma=False)
```

```python
import functools

import jax
import jax.numpy as jnp
from jax import lax
from jax.experimental import pallas as pl
from jax.experimental.pallas import tpu as pltpu
from jax.sharding import Mesh, PartitionSpec as P

GROUPS = 32
EPS = 1e-06
HA = ("y", "core")
BF = jnp.bfloat16
F32 = jnp.float32
LANES = 128
LIMIT = 32 * 1024 * 1024
SHIFTS = (0, 2, 1, 3)
PAIRS = ((0, 1), (2, 3), (4, 5), (6, 7), (8,))
VMEM = pl.BlockSpec(memory_space=pltpu.VMEM)


def lane_in_group(shape):
    return lax.broadcasted_iota(jnp.int32, shape, 1) & 15


def segment_sum(x):
    row = lax.broadcasted_iota(jnp.int32, (LANES, LANES), 0)
    column = lax.broadcasted_iota(jnp.int32, (LANES, LANES), 1)
    ones = jnp.where((row >> 4) == (column >> 4), 1.0, 0.0).astype(BF)
    pieces = jnp.concatenate([*thirds(x), jnp.zeros_like(x)], axis=0).astype(BF)
    sums = jnp.dot(pieces, ones, preferred_element_type=F32)
    return sums[0:8] + sums[8:16] + sums[16:24]


def rows8(x):
    return jnp.broadcast_to(x, (8, LANES))


def cell_rows(rows, pitch):
    index = lax.broadcasted_iota(jnp.int32, (rows, LANES), 0)
    row = (index * {10: 52429, 12: 43691}[pitch]) >> 19
    return row, index - row * pitch


def encode(out_ref, stats):
    lane = lane_in_group((8, LANES))
    row = jnp.zeros((8, LANES), F32)
    for block, mean, spread in stats:
        row = jnp.where(lane == block, mean, row)
        row = jnp.where(lane == block + 4, spread, row)
    out_ref[...] = jnp.broadcast_to(row[0:1][None], out_ref.shape)


def thirds(x):
    high = x.astype(BF).astype(F32)
    middle = (x - high).astype(BF).astype(F32)
    return high, middle, x - high - middle


def pack_stats(mean, spread):
    row = lax.broadcasted_iota(jnp.int32, mean.shape, 0)
    packed = jnp.zeros(mean.shape, F32)
    for k, piece in enumerate(thirds(mean) + thirds(spread)):
        packed = jnp.where(row == k, piece, packed)
    return packed.astype(BF)


def unpack_stats(packed):
    x = packed.astype(F32)
    return x[0:1] + x[1:2] + x[2:3], x[3:4] + x[4:5] + x[5:6]


def merge_stats(stats):
    scale = 1.0 / len(stats)
    middle = sum(mean for mean, _ in stats) * scale
    spread = sum(spread + (mean - middle) * (mean - middle) for mean, spread in stats) * scale
    return middle, spread


def all_rows(x):
    return jnp.broadcast_to(x, (8, x.shape[1]))


def channel_stats(x, keep, count):
    mean = jnp.sum(x, axis=0, keepdims=True) * (1.0 / count)
    deviation = x - mean
    if keep is not None:
        deviation = jnp.where(keep, deviation, 0.0)
    spread = jnp.sum(deviation * deviation, axis=0, keepdims=True) * (1.0 / count)
    return group_stats(mean, spread)


def group_stats(mean, spread):
    mean, spread = rows8(mean), rows8(spread)
    middle = segment_sum(mean) * (1.0 / 16)
    off = mean - middle
    return middle, segment_sum(spread + off * off) * (1.0 / 16)


def tile_stats(rows_ref):
    rows = rows_ref[...].reshape(rows_ref.shape[0], LANES)
    count = rows.shape[0]
    mean = jnp.sum(rows, axis=0, keepdims=True) * (1.0 / count)
    off = rows - mean
    between = jnp.sum(off * off, axis=0, keepdims=True) * (1.0 / count)
    return rows8(mean), rows8(between)


def block_stats(mean, between, block):
    lane = lane_in_group((8, LANES))
    middle = segment_sum(jnp.where(lane == block, mean, 0.0))
    spread = segment_sum(jnp.where(lane == block + 4, mean, jnp.where(lane == block, between, 0.0)))
    return middle[0:1], lax.rsqrt(spread[0:1] + EPS)


def decode(rows_ref, small_ref, at):
    mean, between = tile_stats(rows_ref)
    result = []
    for block in range(4):
        middle, inverse = block_stats(mean, between, block)
        gain, shift = gain_and_shift(small_ref, at, block)
        result.append((middle, inverse * gain, shift))
    return result


def gain_and_shift(small_ref, at, block):
    return small_ref[at + block : at + block + 1, :], small_ref[at + 4 + block : at + 5 + block, :]


def wide(small_ref, at):
    return jnp.concatenate([small_ref[at + b : at + b + 1, :] for b in range(4)], axis=1)


def silu(v):
    half = 0.5 * v
    return half + half * jnp.tanh(half)


def turned(ta, s):
    return ta ^ s


def first_kernel(latent_ref, out_ref):
    out_ref[...] = latent_ref[...]


def frame_moments_kernel(s0, s1, s2, s3, out_ref, outer_ref, inner_ref):
    slots = (s0, s1, s2, s3)
    stats = []
    for block in range(4):
        x = jnp.concatenate(
            [ref[:, block * LANES : (block + 1) * LANES].astype(F32) for ref in slots], axis=0
        )
        stats.append((block,) + channel_stats(x, None, x.shape[0]))
    encode(out_ref, stats)
    for s, ref in zip(SHIFTS, slots):
        start = 48 * lax.axis_index("core")
        outer_ref[s] = ref[pl.ds(pl.multiple_of(start, 16), 16), :]
        inner_ref[s] = ref[pl.ds(pl.multiple_of(48 - start, 16), 16), :]


def above_and_below(outer_ref, inner_ref, s, lanes):
    outer, inner = outer_ref[s, :, lanes].astype(F32), inner_ref[s, :, lanes].astype(F32)
    upper = lax.axis_index("core") == 0
    return jnp.where(upper, outer, inner), jnp.where(upper, inner, outer)


def columns_kernel(s0, s1, s2, s3, outer_rows, inner_rows, outer_ref, inner_ref, tall, sides):
    odd = lax.rem(lax.axis_index("z"), 2) == 1
    for s, ref in zip(SHIFTS, (s0, s1, s2, s3)):
        for b in range(4):
            lanes = slice(b * LANES, (b + 1) * LANES)
            tall[b, 0:16, :], tall[b, 80:96, :] = above_and_below(outer_rows, inner_rows, s, lanes)
            tall[b, 16:80, :] = ref[:, lanes].astype(F32)
            for k in range(2):
                for j in range(2):
                    sides[k, b, 12 * j : 12 * j + 12, :] = tall[b, pl.ds(j + 6 * k, 12, stride=8), :]
            first, last = sides[0, b], sides[1, b]
            outer_ref[s, :, lanes] = jnp.where(odd, last, first).astype(BF)
            inner_ref[s, :, lanes] = jnp.where(odd, first, last).astype(BF)


def activate_kernel(grid, hidden_ref, rows_ref, small_ref, out_ref):
    ta = lax.axis_index("ta")
    middle, inverse = block_stats(*tile_stats(rows_ref), 0)
    scale = inverse * small_ref[pl.ds(8 + ta, 1), :]
    shift = small_ref[pl.ds(12 + ta, 1), :]
    keep = inside(8 * lax.axis_index(HA) - 1, 8 * lax.axis_index("z") - 1, 104, 10, grid)
    for f in range(4):
        v = (hidden_ref[f].astype(F32) - middle) * scale + shift
        out_ref[f] = jnp.where(keep, silu(v), 0.0).astype(BF)


def residual_kernel(s0, s1, s2, s3, out_ref, parts):
    for s, ref in zip(SHIFTS, (s0, s1, s2, s3)):
        parts[turned(lax.axis_index("ta"), s)] = ref[...]
    out_ref[...] = jnp.concatenate([parts[b] for b in range(4)], axis=1)


def merge_kernel(*refs):
    slots, out_ref = refs[:-1], refs[-1]
    room = out_ref.shape[0] - 8
    middle, spread = merge_stats([unpack_stats(ref[64:72, :]) for ref in slots])
    for s in range(room // 64):
        out_ref[64 * s : 64 * s + 64, :] = slots[s][0:64, :]
    out_ref[room : room + 8, :] = pack_stats(all_rows(middle), all_rows(spread))


def convolve(lhs, weights, product, frame_rows, pitch, out_rows):
    for pair in PAIRS:
        rhs = jnp.concatenate(
            [jnp.concatenate([weights[9 * d + s] for s in pair], axis=1) for d in range(3)], axis=0
        )
        lane = pair[0] * LANES
        product[0 : 4 * frame_rows, lane : lane + rhs.shape[1]] = jnp.dot(
            lhs[...], rhs, preferred_element_type=F32
        )
    return shifted_sums(product, frame_rows, pitch, out_rows)


def shifted_sums(product, frame_rows, pitch, out_rows):
    totals = []
    for f in range(4):
        total = None
        for s in range(9):
            at = f * frame_rows + pitch * (s // 3) + s % 3
            piece = product[at : at + out_rows, s * LANES : (s + 1) * LANES]
            total = piece if total is None else total + piece
        totals.append(total)
    return totals


def inside(base_row, base_column, rows, pitch, grid):
    row, column = cell_rows(rows, pitch)
    row, column = row + base_row, column + base_column
    return (row >= 0) & (row < grid[0]) & (column >= 0) & (column < grid[1])


def rimmed_kernel(
    grid,
    s0,
    s1,
    s2,
    s3,
    outer_rows,
    inner_rows,
    outer_columns,
    inner_columns,
    rows_ref,
    small_ref,
    lhs_ref,
    own_ref,
    frames,
    tile,
    sides,
):
    ta = lax.axis_index("ta")
    odd = lax.rem(lax.axis_index("z"), 2) == 1
    coefficients = decode(rows_ref, small_ref, 0)
    keep = inside(8 * lax.axis_index(HA) - 2, 8 * lax.axis_index("z") - 2, 144, 12, grid)
    for s, ref in zip(SHIFTS, (s0, s1, s2, s3)):
        frames[turned(ta, s)] = ref[...]
    for frame in range(4):
        s = turned(ta, frame)
        own = jnp.zeros((64, LANES), F32)
        for b in range(4):
            lanes = slice(b * LANES, (b + 1) * LANES)
            middle = frames[frame, :, lanes].astype(F32)
            own = jnp.where(ta == b, middle, own)
            top, bottom = above_and_below(outer_rows, inner_rows, s, lanes)
            for r in range(12):
                if r < 2:
                    piece = top[8 * r : 8 * r + 8]
                elif r < 10:
                    piece = middle[8 * (r - 2) : 8 * (r - 2) + 8]
                else:
                    piece = bottom[8 * (r - 10) : 8 * (r - 10) + 8]
                tile[b, 12 * r + 2 : 12 * r + 10, :] = piece
            outer, inner = outer_columns[s, :, lanes].astype(F32), inner_columns[s, :, lanes].astype(F32)
            sides[0, b] = jnp.where(odd, inner, outer)
            sides[1, b] = jnp.where(odd, outer, inner)
            for k in range(2):
                for j in range(2):
                    tile[b, pl.ds(j + 10 * k, 12, stride=12), :] = sides[k, b, 12 * j : 12 * j + 12, :]
            mean, scale, shift = coefficients[b]
            v = (tile[b] - mean) * scale + shift
            act = jnp.where(keep, silu(v), 0.0).astype(BF)
            for f in range(4):
                for d in range(3):
                    if max(f + d - 2, 0) == frame:
                        lane = (4 * d + b) * LANES
                        lhs_ref[f * 144 : (f + 1) * 144, lane : lane + LANES] = act
        own_ref[frame] = own.astype(BF)


def first_conv_kernel(lhs, small_ref, kernel_ref, out_ref, moments_ref, product, wide_rows, tight_rows):
    totals = convolve(lhs, kernel_ref, product, 144, 12, 120)
    row, column = cell_rows(104, 10)
    keep = (row >= 1) & (row <= 8) & (column >= 1) & (column <= 8)
    bias = small_ref[36:37, :]
    kept = []
    for f in range(4):
        wide_rows[f] = totals[f] + bias
        for r in range(10):
            tight_rows[f, 10 * r : 10 * r + 10, :] = wide_rows[f, 12 * r : 12 * r + 10, :]
        tight_rows[f, 100:104, :] = jnp.zeros((4, LANES), F32)
        hidden = tight_rows[f].astype(BF)
        out_ref[f] = hidden
        kept.append(jnp.where(keep, hidden.astype(F32), 0.0))
    mean = sum(jnp.sum(x, axis=0, keepdims=True) for x in kept) * (1.0 / 256)
    squares = [jnp.square(jnp.where(keep, x - mean, 0.0)) for x in kept]
    spread = sum(jnp.sum(x, axis=0, keepdims=True) for x in squares) * (1.0 / 256)
    encode(moments_ref, [(0,) + group_stats(mean, spread)])


def add_blocks(refs, shifts, kernel_ref, lhs, product, before=None):
    ta = lax.axis_index("ta")
    for k, ref in enumerate(refs):
        for f in range(4):
            for d in range(3):
                lane = (len(refs) * d + k) * LANES
                lhs[f * 112 : f * 112 + 104, lane : lane + LANES] = ref[max(f + d - 2, 0)]
    for pair in PAIRS:
        rhs = jnp.concatenate(
            [
                jnp.concatenate(
                    [
                        kernel_ref[9 * d + s, pl.ds(pl.multiple_of(turned(ta, shift) * LANES, LANES), LANES), :]
                        for s in pair
                    ],
                    axis=1,
                )
                for d in range(3)
                for shift in shifts
            ],
            axis=0,
        )
        lanes = slice(pair[0] * LANES, pair[0] * LANES + rhs.shape[1])
        part = jnp.dot(lhs[...], rhs, preferred_element_type=F32)
        product[:, lanes] = part if before is None else before[:, lanes] + part


def second_conv_first_kernel(s0, s1, kernel_ref, out_ref, lhs):
    add_blocks((s0, s1), SHIFTS[:2], kernel_ref, lhs, out_ref)


def second_conv_kernel(
    s2,
    s3,
    before_ref,
    small_ref,
    own_ref,
    kernel_ref,
    out0,
    out1,
    out2,
    out3,
    lhs,
    product,
    wide_rows,
    parts,
):
    ta = lax.axis_index("ta")
    add_blocks((s2, s3), SHIFTS[2:], kernel_ref, lhs, product, before_ref)
    totals = shifted_sums(product, 112, 10, 80)
    bias = small_ref[37:38, :]
    tiles = []
    for f in range(4):
        wide_rows[f] = totals[f] + bias
        branch = jnp.concatenate([wide_rows[f, 10 * r : 10 * r + 8, :] for r in range(8)], axis=0)
        branch = branch.astype(BF).astype(F32)
        residual = (own_ref[f].astype(F32) + branch).astype(BF)
        parts[f] = residual
        tiles.append(residual.astype(F32))
    mean, spread = channel_stats(jnp.concatenate(tiles, axis=0), None, 256)
    packed = pack_stats(mean, spread)
    for s, ref in zip(SHIFTS, (out0, out1, out2, out3)):
        ref[0:64, :] = parts[turned(ta, s)]
        ref[64:72, :] = packed


def normalise(x, coefficients):
    parts = []
    for b, (mean, scale, shift) in enumerate(coefficients):
        part = x[:, b * LANES : (b + 1) * LANES].astype(F32)
        parts.append(((part - mean) * scale + shift).astype(BF))
    return jnp.concatenate(parts, axis=1)


def attention_kernel(*refs):
    asked, told = refs[:4], refs[4:6]
    small_ref, query_ref, key_ref = refs[6:9]
    outs, normed = refs[9:13], refs[13]
    middle, spread = merge_stats([unpack_stats(ref[512:520, :]) for ref in told])
    inverse = lax.rsqrt(spread + EPS)
    coefficients = []
    for b in range(4):
        lanes = slice(b * LANES, (b + 1) * LANES)
        gain, shift = gain_and_shift(small_ref, 16, b)
        coefficients.append((middle[:, lanes], inverse[:, lanes] * gain, shift))
    normed_q = normalise(jnp.concatenate([ref[0:64, :] for ref in asked], axis=0), coefficients)
    for k, ref in enumerate(told):
        normed[512 * k : 512 * k + 512, :] = normalise(ref[0:512, :], coefficients)
    queries = jnp.dot(normed_q, query_ref[...], preferred_element_type=F32) + wide(small_ref, 24)
    folded = lax.dot_general(
        queries.astype(BF), key_ref[...], (((1,), (1,)), ((), ())), preferred_element_type=F32
    ) * 512 ** (-0.5)
    scores = lax.dot_general(
        folded.astype(BF), normed[...], (((1,), (1,)), ((), ())), preferred_element_type=F32
    )
    highest = jnp.max(scores, axis=1, keepdims=True)
    weights = jnp.exp(scores - highest)
    total = jnp.sum(weights, axis=1, keepdims=True)
    mixed = jnp.dot(weights.astype(BF), normed[...], preferred_element_type=F32) * (1.0 / total)
    level = highest + jnp.log(total)
    top, middle, low = thirds(level)
    lane = lax.broadcasted_iota(jnp.int32, (256, LANES), 1)
    tail = jnp.where(lane == 0, top, jnp.where(lane == 1, middle, jnp.where(lane == 2, low, 0.0)))
    for s, ref in enumerate(outs):
        ref[:, 0:512] = mixed[64 * s : 64 * s + 64].astype(BF)
        ref[:, 512:640] = tail[64 * s : 64 * s + 64].astype(BF)


def finish_kernel(b0, b1, b2, b3, residual_ref, small_ref, value_ref, output_ref, out_ref):
    backs = [ref[...].astype(F32) for ref in (b0, b1, b2, b3)]
    levels = [jnp.sum(back[:, 512:640], axis=1, keepdims=True) for back in backs]
    highest = functools.reduce(jnp.maximum, levels)
    shares = [jnp.exp(level - highest) for level in levels]
    inverse = 1.0 / sum(shares)
    mean_normed = sum(back[:, 0:512] * (share * inverse) for back, share in zip(backs, shares))
    attended = jnp.dot(mean_normed.astype(BF), value_ref[...], preferred_element_type=F32)
    attended = (attended + wide(small_ref, 28)).astype(BF)
    mixed = jnp.dot(attended, output_ref[...], preferred_element_type=F32)
    out_ref[...] = (residual_ref[0:64, :].astype(F32) + mixed + wide(small_ref, 32)).astype(BF)


def call(kernel, out_shape, specs, scratch, flops, *args):
    shapes = out_shape if isinstance(out_shape, tuple) else (out_shape,)
    moved = sum(a.size * a.dtype.itemsize for a in args) + sum(
        s.size * jnp.dtype(s.dtype).itemsize for s in shapes
    )
    return pl.pallas_call(
        kernel,
        out_shape=out_shape,
        in_specs=specs,
        out_specs=tuple(VMEM for _ in shapes) if isinstance(out_shape, tuple) else VMEM,
        scratch_shapes=scratch,
        compiler_params=pltpu.CompilerParams(vmem_limit_bytes=LIMIT),
        cost_estimate=pl.CostEstimate(flops=flops, bytes_accessed=moved, transcendentals=0),
    )(*args)


def ring(count, step):
    return [(i, (i + step) % count) for i in range(count)]


def spread_out(blocks, axis):
    return [blocks[0]] + [
        lax.ppermute(block, axis, [(i, i ^ shift) for i in range(4)]) for block, shift in zip(blocks[1:], SHIFTS[1:])
    ]


def around(block, axis):
    return spread_out([block] * 4, axis)


def relayed(block, axis):
    count = lax.axis_size(axis)
    after = {step: lax.ppermute(block, axis, ring(count, step)) for step in (2, 1, -1, -2)}
    further = [lax.ppermute(after[step], axis, ring(count, move)) for step, move in ((2, 2), (1, 2), (-1, -2))]
    return [block, *after.values(), *further]


def both_sides(outer, inner, axis):
    across = [(i, (i + (1 if i % 2 else -1)) % 8) for i in range(8)]
    return lax.ppermute(outer, axis, across), lax.ppermute(inner, axis, [(i, i ^ 1) for i in range(8)])


def over_tiles(rows):
    return lax.all_to_all(rows, HA + ("z",), split_axis=0, concat_axis=0, tiled=True)


def body(
    latent,
    norm1_gain,
    norm1_shift,
    conv1_kernel,
    conv1_shift,
    norm2_gain,
    norm2_shift,
    conv2_kernel,
    conv2_shift,
    norm3_gain,
    norm3_shift,
    query_weight,
    query_shift,
    key_weight,
    value_weight,
    value_shift,
    output_weight,
    output_shift,
):
    _, height, width, channels = latent.shape
    cells = height * width
    tiles = lax.axis_size(HA) * lax.axis_size("z")
    grid = (lax.axis_size(HA) * height, lax.axis_size("z") * width)
    vectors = [norm1_gain, norm1_shift, norm2_gain, norm2_shift, norm3_gain, norm3_shift]
    vectors += [query_shift, value_shift, output_shift, conv1_shift, conv2_shift]
    small = jnp.concatenate(vectors).reshape(-1, LANES)

    def bf(*shape):
        return jax.ShapeDtypeStruct(shape, BF)

    rows = jax.ShapeDtypeStruct((tiles, 1, LANES), F32)

    slots = around(latent[0].reshape(cells, channels), "ta")
    slots[0] = call(first_kernel, bf(cells, channels), [VMEM], [], 4 * 10**9, slots[0])
    rows1, outer, inner = call(
        frame_moments_kernel, (rows, bf(4, 16, channels), bf(4, 16, channels)), [VMEM] * 4, [], 10**6, *slots
    )
    outer_rows, inner_rows = both_sides(outer, inner, HA)
    rows1 = over_tiles(rows1)
    outer, inner = call(
        columns_kernel,
        (bf(4, 24, channels), bf(4, 24, channels)),
        [VMEM] * 6,
        [pltpu.VMEM((4, 96, LANES), F32), pltpu.VMEM((2, 4, 24, LANES), F32)],
        10**6,
        *slots,
        outer_rows,
        inner_rows,
    )
    outer_columns, inner_columns = both_sides(outer, inner, "z")
    lhs, own = call(
        functools.partial(rimmed_kernel, grid),
        (bf(576, 1536), bf(4, cells, LANES)),
        [VMEM] * 10,
        [pltpu.VMEM((4, cells, channels), BF), pltpu.VMEM((4, 144, LANES), F32), pltpu.VMEM((2, 4, 24, LANES), F32)],
        4 * 10**9,
        *slots,
        outer_rows,
        inner_rows,
        outer_columns,
        inner_columns,
        rows1,
        small,
    )
    hidden, rows2 = call(
        first_conv_kernel,
        (bf(4, 104, LANES), rows),
        [VMEM] * 3,
        [
            pltpu.VMEM((584, 1152), F32),
            pltpu.VMEM((4, 120, LANES), F32),
            pltpu.VMEM((4, 104, LANES), F32),
        ],
        2 * 10**9,
        lhs,
        small,
        conv1_kernel,
    )

    act = call(
        functools.partial(activate_kernel, grid),
        bf(4, 104, LANES),
        [VMEM] * 3,
        [],
        4 * 10**9,
        hidden,
        over_tiles(rows2),
        small,
    )
    blocks = around(act, "ta")
    before = call(
        second_conv_first_kernel,
        jax.ShapeDtypeStruct((448, 1152), F32),
        [VMEM] * 3,
        [pltpu.VMEM((448, 768), BF)],
        10**9,
        *blocks[:2],
        conv2_kernel,
    )
    parts = call(
        second_conv_kernel,
        (bf(cells + 8, LANES),) * 4,
        [VMEM] * 6,
        [
            pltpu.VMEM((448, 768), BF),
            pltpu.VMEM((448, 1152), F32),
            pltpu.VMEM((4, 80, LANES), F32),
            pltpu.VMEM((4, cells, LANES), BF),
        ],
        2 * 10**9,
        *blocks[2:],
        before,
        small,
        own,
        conv2_kernel,
    )

    residual = call(
        residual_kernel,
        bf(cells + 8, channels),
        [VMEM] * 4,
        [pltpu.VMEM((4, cells + 8, LANES), BF)],
        10**6,
        *spread_out(parts, "ta"),
    )
    asked = around(residual, "y")
    told = call(merge_kernel, bf(cells + 8, channels), [VMEM] * 4, [], 10**6, *asked)
    told = call(merge_kernel, bf(8 * cells + 8, channels), [VMEM] * 8, [], 10**6, *relayed(told, "z"))
    packed = call(
        attention_kernel,
        (bf(cells, channels + LANES),) * 4,
        [VMEM] * 9,
        [pltpu.VMEM((1024, channels), BF)],
        10**9,
        *asked,
        told,
        lax.ppermute(told, "core", ring(2, 1)),
        small,
        query_weight,
        key_weight,
    )

    block_out = call(
        finish_kernel,
        bf(cells, channels),
        [VMEM] * 8,
        [],
        10**8,
        *spread_out(packed, "y"),
        residual,
        small,
        value_weight,
        output_weight,
    )
    return block_out.reshape(latent.shape)


def solution(mesh):
    frames, rows, columns = mesh.devices.shape
    split = Mesh(mesh.devices.reshape(frames, rows // 2, 2, columns), ("ta", "y", "core", "z"))
    tile = P("ta", HA, "z", None)
    kernel, shift = P(None, None, "ta"), P("ta")
    in_specs = (tile, P(), P(), kernel, shift, P(), P(), kernel, shift) + (P(),) * 9
    return jax.shard_map(body, mesh=split, in_specs=in_specs, out_specs=tile, check_vma=False)
```

```python
import functools

import jax
import jax.numpy as jnp
from jax import lax
from jax.experimental import pallas as pl
from jax.experimental.pallas import tpu as pltpu
from jax.sharding import Mesh, PartitionSpec as P

GROUPS = 32
EPS = 1e-06
HA = ("y", "core")
BF = jnp.bfloat16
F32 = jnp.float32
LANES = 128
LIMIT = 32 * 1024 * 1024
SHIFTS = (0, 2, 1, 3)
PAIRS = ((0, 1), (2, 3), (4, 5), (6, 7), (8,))
VMEM = pl.BlockSpec(memory_space=pltpu.VMEM)


def lane_in_group(shape):
    return lax.broadcasted_iota(jnp.int32, shape, 1) & 15


def segment_sum(x):
    row = lax.broadcasted_iota(jnp.int32, (LANES, LANES), 0)
    column = lax.broadcasted_iota(jnp.int32, (LANES, LANES), 1)
    ones = jnp.where((row >> 4) == (column >> 4), 1.0, 0.0).astype(BF)
    pieces = jnp.concatenate([*thirds(x), jnp.zeros_like(x)], axis=0).astype(BF)
    sums = jnp.dot(pieces, ones, preferred_element_type=F32)
    return sums[0:8] + sums[8:16] + sums[16:24]


def rows8(x):
    return jnp.broadcast_to(x, (8, LANES))


def cell_rows(rows, pitch):
    index = lax.broadcasted_iota(jnp.int32, (rows, LANES), 0)
    row = (index * {10: 52429, 12: 43691}[pitch]) >> 19
    return row, index - row * pitch


def encode(out_ref, stats):
    lane = lane_in_group((8, LANES))
    row = jnp.zeros((8, LANES), F32)
    for block, mean, spread in stats:
        row = jnp.where(lane == block, mean, row)
        row = jnp.where(lane == block + 4, spread, row)
    out_ref[...] = jnp.broadcast_to(row[0:1][None], out_ref.shape)


def thirds(x):
    high = x.astype(BF).astype(F32)
    middle = (x - high).astype(BF).astype(F32)
    return high, middle, x - high - middle


def pack_stats(mean, spread):
    row = lax.broadcasted_iota(jnp.int32, mean.shape, 0)
    packed = jnp.zeros(mean.shape, F32)
    for k, piece in enumerate(thirds(mean) + thirds(spread)):
        packed = jnp.where(row == k, piece, packed)
    return packed.astype(BF)


def unpack_stats(packed):
    x = packed.astype(F32)
    return x[0:1] + x[1:2] + x[2:3], x[3:4] + x[4:5] + x[5:6]


def merge_stats(stats):
    scale = 1.0 / len(stats)
    middle = sum(mean for mean, _ in stats) * scale
    spread = sum(spread + (mean - middle) * (mean - middle) for mean, spread in stats) * scale
    return middle, spread


def all_rows(x):
    return jnp.broadcast_to(x, (8, x.shape[1]))


def channel_stats(x, keep, count):
    mean = jnp.sum(x, axis=0, keepdims=True) * (1.0 / count)
    deviation = x - mean
    if keep is not None:
        deviation = jnp.where(keep, deviation, 0.0)
    spread = jnp.sum(deviation * deviation, axis=0, keepdims=True) * (1.0 / count)
    return group_stats(mean, spread)


def group_stats(mean, spread):
    mean, spread = rows8(mean), rows8(spread)
    middle = segment_sum(mean) * (1.0 / 16)
    off = mean - middle
    return middle, segment_sum(spread + off * off) * (1.0 / 16)


def tile_stats(rows_ref):
    rows = rows_ref[...].reshape(rows_ref.shape[0], LANES)
    count = rows.shape[0]
    mean = jnp.sum(rows, axis=0, keepdims=True) * (1.0 / count)
    off = rows - mean
    between = jnp.sum(off * off, axis=0, keepdims=True) * (1.0 / count)
    return rows8(mean), rows8(between)


def block_stats(mean, between, block):
    lane = lane_in_group((8, LANES))
    middle = segment_sum(jnp.where(lane == block, mean, 0.0))
    spread = segment_sum(jnp.where(lane == block + 4, mean, jnp.where(lane == block, between, 0.0)))
    return middle[0:1], lax.rsqrt(spread[0:1] + EPS)


def decode(rows_ref, small_ref, at):
    mean, between = tile_stats(rows_ref)
    result = []
    for block in range(4):
        middle, inverse = block_stats(mean, between, block)
        gain, shift = gain_and_shift(small_ref, at, block)
        result.append((middle, inverse * gain, shift))
    return result


def gain_and_shift(small_ref, at, block):
    return small_ref[at + block : at + block + 1, :], small_ref[at + 4 + block : at + 5 + block, :]


def wide(small_ref, at):
    return jnp.concatenate([small_ref[at + b : at + b + 1, :] for b in range(4)], axis=1)


def silu(v):
    half = 0.5 * v
    return half + half * jnp.tanh(half)


def turned(ta, s):
    return ta ^ s


def first_kernel(latent_ref, out_ref):
    out_ref[...] = latent_ref[...]


def frame_moments_kernel(s0, s1, s2, s3, out_ref, outer_ref, inner_ref):
    slots = (s0, s1, s2, s3)
    stats = []
    for block in range(4):
        x = jnp.concatenate(
            [ref[:, block * LANES : (block + 1) * LANES].astype(F32) for ref in slots], axis=0
        )
        stats.append((block,) + channel_stats(x, None, x.shape[0]))
    encode(out_ref, stats)
    for s, ref in zip(SHIFTS, slots):
        start = 48 * lax.axis_index("core")
        outer_ref[s] = ref[pl.ds(pl.multiple_of(start, 16), 16), :]
        inner_ref[s] = ref[pl.ds(pl.multiple_of(48 - start, 16), 16), :]


def above_and_below(outer_ref, inner_ref, s, lanes):
    outer, inner = outer_ref[s, :, lanes].astype(F32), inner_ref[s, :, lanes].astype(F32)
    upper = lax.axis_index("core") == 0
    return jnp.where(upper, outer, inner), jnp.where(upper, inner, outer)


def columns_kernel(s0, s1, s2, s3, outer_rows, inner_rows, outer_ref, inner_ref, tall, sides):
    odd = lax.rem(lax.axis_index("z"), 2) == 1
    for s, ref in zip(SHIFTS, (s0, s1, s2, s3)):
        for b in range(4):
            lanes = slice(b * LANES, (b + 1) * LANES)
            tall[b, 0:16, :], tall[b, 80:96, :] = above_and_below(outer_rows, inner_rows, s, lanes)
            tall[b, 16:80, :] = ref[:, lanes].astype(F32)
            for k in range(2):
                for j in range(2):
                    sides[k, b, 12 * j : 12 * j + 12, :] = tall[b, pl.ds(j + 6 * k, 12, stride=8), :]
            first, last = sides[0, b], sides[1, b]
            outer_ref[s, :, lanes] = jnp.where(odd, last, first).astype(BF)
            inner_ref[s, :, lanes] = jnp.where(odd, first, last).astype(BF)


def activate_kernel(grid, hidden_ref, rows_ref, small_ref, out_ref):
    ta = lax.axis_index("ta")
    middle, inverse = block_stats(*tile_stats(rows_ref), 0)
    scale = inverse * small_ref[pl.ds(8 + ta, 1), :]
    shift = small_ref[pl.ds(12 + ta, 1), :]
    keep = inside(8 * lax.axis_index(HA) - 1, 8 * lax.axis_index("z") - 1, 104, 10, grid)
    for f in range(4):
        v = (hidden_ref[f].astype(F32) - middle) * scale + shift
        out_ref[f] = jnp.where(keep, silu(v), 0.0).astype(BF)


def residual_kernel(s0, s1, s2, s3, out_ref, parts):
    for s, ref in zip(SHIFTS, (s0, s1, s2, s3)):
        parts[turned(lax.axis_index("ta"), s)] = ref[...]
    out_ref[...] = jnp.concatenate([parts[b] for b in range(4)], axis=1)


def merge_kernel(*refs):
    slots, out_ref = refs[:-1], refs[-1]
    room = out_ref.shape[0] - 8
    middle, spread = merge_stats([unpack_stats(ref[64:72, :]) for ref in slots])
    for s in range(room // 64):
        out_ref[64 * s : 64 * s + 64, :] = slots[s][0:64, :]
    out_ref[room : room + 8, :] = pack_stats(all_rows(middle), all_rows(spread))


def convolve(lhs, weights, product, frame_rows, pitch, out_rows):
    for pair in PAIRS:
        rhs = jnp.concatenate(
            [jnp.concatenate([weights[9 * d + s] for s in pair], axis=1) for d in range(3)], axis=0
        )
        lane = pair[0] * LANES
        product[0 : 4 * frame_rows, lane : lane + rhs.shape[1]] = jnp.dot(
            lhs[...], rhs, preferred_element_type=F32
        )
    return shifted_sums(product, frame_rows, pitch, out_rows)


def shifted_sums(product, frame_rows, pitch, out_rows):
    totals = []
    for f in range(4):
        total = None
        for s in range(9):
            at = f * frame_rows + pitch * (s // 3) + s % 3
            piece = product[at : at + out_rows, s * LANES : (s + 1) * LANES]
            total = piece if total is None else total + piece
        totals.append(total)
    return totals


def inside(base_row, base_column, rows, pitch, grid):
    row, column = cell_rows(rows, pitch)
    row, column = row + base_row, column + base_column
    return (row >= 0) & (row < grid[0]) & (column >= 0) & (column < grid[1])


def rimmed_kernel(
    grid,
    s0,
    s1,
    s2,
    s3,
    outer_rows,
    inner_rows,
    outer_columns,
    inner_columns,
    rows_ref,
    small_ref,
    lhs_ref,
    own_ref,
    frames,
    tile,
    sides,
):
    ta = lax.axis_index("ta")
    odd = lax.rem(lax.axis_index("z"), 2) == 1
    coefficients = decode(rows_ref, small_ref, 0)
    keep = inside(8 * lax.axis_index(HA) - 2, 8 * lax.axis_index("z") - 2, 144, 12, grid)
    for s, ref in zip(SHIFTS, (s0, s1, s2, s3)):
        frames[turned(ta, s)] = ref[...]
    for frame in range(4):
        s = turned(ta, frame)
        own = jnp.zeros((64, LANES), F32)
        for b in range(4):
            lanes = slice(b * LANES, (b + 1) * LANES)
            middle = frames[frame, :, lanes].astype(F32)
            own = jnp.where(ta == b, middle, own)
            top, bottom = above_and_below(outer_rows, inner_rows, s, lanes)
            for r in range(12):
                if r < 2:
                    piece = top[8 * r : 8 * r + 8]
                elif r < 10:
                    piece = middle[8 * (r - 2) : 8 * (r - 2) + 8]
                else:
                    piece = bottom[8 * (r - 10) : 8 * (r - 10) + 8]
                tile[b, 12 * r + 2 : 12 * r + 10, :] = piece
            outer, inner = outer_columns[s, :, lanes].astype(F32), inner_columns[s, :, lanes].astype(F32)
            sides[0, b] = jnp.where(odd, inner, outer)
            sides[1, b] = jnp.where(odd, outer, inner)
            for k in range(2):
                for j in range(2):
                    tile[b, pl.ds(j + 10 * k, 12, stride=12), :] = sides[k, b, 12 * j : 12 * j + 12, :]
            mean, scale, shift = coefficients[b]
            v = (tile[b] - mean) * scale + shift
            act = jnp.where(keep, silu(v), 0.0).astype(BF)
            for f in range(4):
                for d in range(3):
                    if max(f + d - 2, 0) == frame:
                        lane = (4 * d + b) * LANES
                        lhs_ref[f * 144 : (f + 1) * 144, lane : lane + LANES] = act
        own_ref[frame] = own.astype(BF)


def first_conv_kernel(lhs, small_ref, kernel_ref, out_ref, moments_ref, product, wide_rows, tight_rows):
    totals = convolve(lhs, kernel_ref, product, 144, 12, 120)
    row, column = cell_rows(104, 10)
    keep = (row >= 1) & (row <= 8) & (column >= 1) & (column <= 8)
    bias = small_ref[36:37, :]
    kept = []
    for f in range(4):
        wide_rows[f] = totals[f] + bias
        for r in range(10):
            tight_rows[f, 10 * r : 10 * r + 10, :] = wide_rows[f, 12 * r : 12 * r + 10, :]
        tight_rows[f, 100:104, :] = jnp.zeros((4, LANES), F32)
        hidden = tight_rows[f].astype(BF)
        out_ref[f] = hidden
        kept.append(jnp.where(keep, hidden.astype(F32), 0.0))
    mean = sum(jnp.sum(x, axis=0, keepdims=True) for x in kept) * (1.0 / 256)
    squares = [jnp.square(jnp.where(keep, x - mean, 0.0)) for x in kept]
    spread = sum(jnp.sum(x, axis=0, keepdims=True) for x in squares) * (1.0 / 256)
    encode(moments_ref, [(0,) + group_stats(mean, spread)])


def add_blocks(refs, shifts, kernel_ref, lhs, product, before=None):
    ta = lax.axis_index("ta")
    for k, ref in enumerate(refs):
        for f in range(4):
            for d in range(3):
                lane = (len(refs) * d + k) * LANES
                lhs[f * 112 : f * 112 + 104, lane : lane + LANES] = ref[max(f + d - 2, 0)]
    for pair in PAIRS:
        rhs = jnp.concatenate(
            [
                jnp.concatenate(
                    [
                        kernel_ref[9 * d + s, pl.ds(pl.multiple_of(turned(ta, shift) * LANES, LANES), LANES), :]
                        for s in pair
                    ],
                    axis=1,
                )
                for d in range(3)
                for shift in shifts
            ],
            axis=0,
        )
        lanes = slice(pair[0] * LANES, pair[0] * LANES + rhs.shape[1])
        part = jnp.dot(lhs[...], rhs, preferred_element_type=F32)
        product[:, lanes] = part if before is None else before[:, lanes] + part


def second_conv_first_kernel(s0, s1, kernel_ref, out_ref, lhs):
    add_blocks((s0, s1), SHIFTS[:2], kernel_ref, lhs, out_ref)


def second_conv_kernel(
    s2,
    s3,
    before_ref,
    small_ref,
    own_ref,
    kernel_ref,
    out0,
    out1,
    out2,
    out3,
    lhs,
    product,
    wide_rows,
    parts,
):
    ta = lax.axis_index("ta")
    add_blocks((s2, s3), SHIFTS[2:], kernel_ref, lhs, product, before_ref)
    totals = shifted_sums(product, 112, 10, 80)
    bias = small_ref[37:38, :]
    tiles = []
    for f in range(4):
        wide_rows[f] = totals[f] + bias
        branch = jnp.concatenate([wide_rows[f, 10 * r : 10 * r + 8, :] for r in range(8)], axis=0)
        branch = branch.astype(BF).astype(F32)
        residual = (own_ref[f].astype(F32) + branch).astype(BF)
        parts[f] = residual
        tiles.append(residual.astype(F32))
    mean, spread = channel_stats(jnp.concatenate(tiles, axis=0), None, 256)
    packed = pack_stats(mean, spread)
    for s, ref in zip(SHIFTS, (out0, out1, out2, out3)):
        ref[0:64, :] = parts[turned(ta, s)]
        ref[64:72, :] = packed


def normalise(x, coefficients):
    parts = []
    for b, (mean, scale, shift) in enumerate(coefficients):
        part = x[:, b * LANES : (b + 1) * LANES].astype(F32)
        parts.append(((part - mean) * scale + shift).astype(BF))
    return jnp.concatenate(parts, axis=1)


def attention_kernel(*refs):
    asked, told = refs[:4], refs[4:6]
    small_ref, query_ref, key_ref = refs[6:9]
    outs, normed = refs[9:13], refs[13]
    middle, spread = merge_stats([unpack_stats(ref[512:520, :]) for ref in told])
    inverse = lax.rsqrt(spread + EPS)
    coefficients = []
    for b in range(4):
        lanes = slice(b * LANES, (b + 1) * LANES)
        gain, shift = gain_and_shift(small_ref, 16, b)
        coefficients.append((middle[:, lanes], inverse[:, lanes] * gain, shift))
    normed_q = normalise(jnp.concatenate([ref[0:64, :] for ref in asked], axis=0), coefficients)
    for k, ref in enumerate(told):
        normed[512 * k : 512 * k + 512, :] = normalise(ref[0:512, :], coefficients)
    queries = jnp.dot(normed_q, query_ref[...], preferred_element_type=F32) + wide(small_ref, 24)
    folded = lax.dot_general(
        queries.astype(BF), key_ref[...], (((1,), (1,)), ((), ())), preferred_element_type=F32
    ) * 512 ** (-0.5)
    scores = lax.dot_general(
        folded.astype(BF), normed[...], (((1,), (1,)), ((), ())), preferred_element_type=F32
    )
    highest = jnp.max(scores, axis=1, keepdims=True)
    weights = jnp.exp(scores - highest)
    total = jnp.sum(weights, axis=1, keepdims=True)
    mixed = jnp.dot(weights.astype(BF), normed[...], preferred_element_type=F32) * (1.0 / total)
    level = highest + jnp.log(total)
    top, middle, low = thirds(level)
    lane = lax.broadcasted_iota(jnp.int32, (256, LANES), 1)
    tail = jnp.where(lane == 0, top, jnp.where(lane == 1, middle, jnp.where(lane == 2, low, 0.0)))
    for s, ref in enumerate(outs):
        ref[:, 0:512] = mixed[64 * s : 64 * s + 64].astype(BF)
        ref[:, 512:640] = tail[64 * s : 64 * s + 64].astype(BF)


def finish_kernel(b0, b1, b2, b3, residual_ref, small_ref, value_ref, output_ref, out_ref):
    backs = [ref[...].astype(F32) for ref in (b0, b1, b2, b3)]
    levels = [jnp.sum(back[:, 512:640], axis=1, keepdims=True) for back in backs]
    highest = functools.reduce(jnp.maximum, levels)
    shares = [jnp.exp(level - highest) for level in levels]
    inverse = 1.0 / sum(shares)
    mean_normed = sum(back[:, 0:512] * (share * inverse) for back, share in zip(backs, shares))
    attended = jnp.dot(mean_normed.astype(BF), value_ref[...], preferred_element_type=F32)
    attended = (attended + wide(small_ref, 28)).astype(BF)
    mixed = jnp.dot(attended, output_ref[...], preferred_element_type=F32)
    out_ref[...] = (residual_ref[0:64, :].astype(F32) + mixed + wide(small_ref, 32)).astype(BF)


def call(kernel, out_shape, specs, scratch, flops, *args):
    shapes = out_shape if isinstance(out_shape, tuple) else (out_shape,)
    moved = sum(a.size * a.dtype.itemsize for a in args) + sum(
        s.size * jnp.dtype(s.dtype).itemsize for s in shapes
    )
    return pl.pallas_call(
        kernel,
        out_shape=out_shape,
        in_specs=specs,
        out_specs=tuple(VMEM for _ in shapes) if isinstance(out_shape, tuple) else VMEM,
        scratch_shapes=scratch,
        compiler_params=pltpu.CompilerParams(vmem_limit_bytes=LIMIT),
        cost_estimate=pl.CostEstimate(flops=flops, bytes_accessed=moved, transcendentals=0),
    )(*args)


def ring(count, step):
    return [(i, (i + step) % count) for i in range(count)]


def spread_out(blocks, axis):
    return [blocks[0]] + [
        lax.ppermute(block, axis, [(i, i ^ shift) for i in range(4)]) for block, shift in zip(blocks[1:], SHIFTS[1:])
    ]


def around(block, axis):
    return spread_out([block] * 4, axis)


def relayed(block, axis):
    count = lax.axis_size(axis)
    after = {step: lax.ppermute(block, axis, ring(count, step)) for step in (2, -2, 1, -1)}
    further = [lax.ppermute(after[step], axis, ring(count, move)) for step, move in ((2, 2), (2, 1), (-2, -1))]
    return [block, *after.values(), *further]


def both_sides(outer, inner, axis):
    across = [(i, (i + (1 if i % 2 else -1)) % 8) for i in range(8)]
    return lax.ppermute(outer, axis, across), lax.ppermute(inner, axis, [(i, i ^ 1) for i in range(8)])


def over_tiles(rows):
    return lax.all_to_all(rows, HA + ("z",), split_axis=0, concat_axis=0, tiled=True)


def body(
    latent,
    norm1_gain,
    norm1_shift,
    conv1_kernel,
    conv1_shift,
    norm2_gain,
    norm2_shift,
    conv2_kernel,
    conv2_shift,
    norm3_gain,
    norm3_shift,
    query_weight,
    query_shift,
    key_weight,
    value_weight,
    value_shift,
    output_weight,
    output_shift,
):
    _, height, width, channels = latent.shape
    cells = height * width
    tiles = lax.axis_size(HA) * lax.axis_size("z")
    grid = (lax.axis_size(HA) * height, lax.axis_size("z") * width)
    vectors = [norm1_gain, norm1_shift, norm2_gain, norm2_shift, norm3_gain, norm3_shift]
    vectors += [query_shift, value_shift, output_shift, conv1_shift, conv2_shift]
    small = jnp.concatenate(vectors).reshape(-1, LANES)

    def bf(*shape):
        return jax.ShapeDtypeStruct(shape, BF)

    rows = jax.ShapeDtypeStruct((tiles, 1, LANES), F32)

    slots = around(latent[0].reshape(cells, channels), "ta")
    slots[0] = call(first_kernel, bf(cells, channels), [VMEM], [], 4 * 10**9, slots[0])
    rows1, outer, inner = call(
        frame_moments_kernel, (rows, bf(4, 16, channels), bf(4, 16, channels)), [VMEM] * 4, [], 10**6, *slots
    )
    outer_rows, inner_rows = both_sides(outer, inner, HA)
    rows1 = over_tiles(rows1)
    outer, inner = call(
        columns_kernel,
        (bf(4, 24, channels), bf(4, 24, channels)),
        [VMEM] * 6,
        [pltpu.VMEM((4, 96, LANES), F32), pltpu.VMEM((2, 4, 24, LANES), F32)],
        10**6,
        *slots,
        outer_rows,
        inner_rows,
    )
    outer_columns, inner_columns = both_sides(outer, inner, "z")
    lhs, own = call(
        functools.partial(rimmed_kernel, grid),
        (bf(576, 1536), bf(4, cells, LANES)),
        [VMEM] * 10,
        [pltpu.VMEM((4, cells, channels), BF), pltpu.VMEM((4, 144, LANES), F32), pltpu.VMEM((2, 4, 24, LANES), F32)],
        4 * 10**9,
        *slots,
        outer_rows,
        inner_rows,
        outer_columns,
        inner_columns,
        rows1,
        small,
    )
    hidden, rows2 = call(
        first_conv_kernel,
        (bf(4, 104, LANES), rows),
        [VMEM] * 3,
        [
            pltpu.VMEM((584, 1152), F32),
            pltpu.VMEM((4, 120, LANES), F32),
            pltpu.VMEM((4, 104, LANES), F32),
        ],
        2 * 10**9,
        lhs,
        small,
        conv1_kernel,
    )

    act = call(
        functools.partial(activate_kernel, grid),
        bf(4, 104, LANES),
        [VMEM] * 3,
        [],
        4 * 10**9,
        hidden,
        over_tiles(rows2),
        small,
    )
    blocks = around(act, "ta")
    before = call(
        second_conv_first_kernel,
        jax.ShapeDtypeStruct((448, 1152), F32),
        [VMEM] * 3,
        [pltpu.VMEM((448, 768), BF)],
        10**9,
        *blocks[:2],
        conv2_kernel,
    )
    parts = call(
        second_conv_kernel,
        (bf(cells + 8, LANES),) * 4,
        [VMEM] * 6,
        [
            pltpu.VMEM((448, 768), BF),
            pltpu.VMEM((448, 1152), F32),
            pltpu.VMEM((4, 80, LANES), F32),
            pltpu.VMEM((4, cells, LANES), BF),
        ],
        2 * 10**9,
        *blocks[2:],
        before,
        small,
        own,
        conv2_kernel,
    )

    residual = call(
        residual_kernel,
        bf(cells + 8, channels),
        [VMEM] * 4,
        [pltpu.VMEM((4, cells + 8, LANES), BF)],
        10**6,
        *spread_out(parts, "ta"),
    )
    asked = around(residual, "y")
    told = call(merge_kernel, bf(cells + 8, channels), [VMEM] * 4, [], 10**6, *asked)
    told = call(merge_kernel, bf(8 * cells + 8, channels), [VMEM] * 8, [], 10**6, *relayed(told, "z"))
    packed = call(
        attention_kernel,
        (bf(cells, channels + LANES),) * 4,
        [VMEM] * 9,
        [pltpu.VMEM((1024, channels), BF)],
        10**9,
        *asked,
        told,
        lax.ppermute(told, "core", ring(2, 1)),
        small,
        query_weight,
        key_weight,
    )

    block_out = call(
        finish_kernel,
        bf(cells, channels),
        [VMEM] * 8,
        [],
        10**8,
        *spread_out(packed, "y"),
        residual,
        small,
        value_weight,
        output_weight,
    )
    return block_out.reshape(latent.shape)


def solution(mesh):
    frames, rows, columns = mesh.devices.shape
    split = Mesh(mesh.devices.reshape(frames, rows // 2, 2, columns), ("ta", "y", "core", "z"))
    tile = P("ta", HA, "z", None)
    kernel, shift = P(None, None, "ta"), P("ta")
    in_specs = (tile, P(), P(), kernel, shift, P(), P(), kernel, shift) + (P(),) * 9
    return jax.shard_map(body, mesh=split, in_specs=in_specs, out_specs=tile, check_vma=False)
```

```python
import functools

import jax
import jax.numpy as jnp
from jax import lax
from jax.experimental import pallas as pl
from jax.experimental.pallas import tpu as pltpu
from jax.sharding import Mesh, PartitionSpec as P

GROUPS = 32
EPS = 1e-06
HA = ("y", "core")
BF = jnp.bfloat16
F32 = jnp.float32
LANES = 128
LIMIT = 32 * 1024 * 1024
SHIFTS = (0, 2, 3, 1)
PAIRS = ((0, 1), (2, 3), (4, 5), (6, 7), (8,))
VMEM = pl.BlockSpec(memory_space=pltpu.VMEM)


def lane_in_group(shape):
    return lax.broadcasted_iota(jnp.int32, shape, 1) & 15


def segment_sum(x):
    row = lax.broadcasted_iota(jnp.int32, (LANES, LANES), 0)
    column = lax.broadcasted_iota(jnp.int32, (LANES, LANES), 1)
    ones = jnp.where((row >> 4) == (column >> 4), 1.0, 0.0).astype(BF)
    pieces = jnp.concatenate([*thirds(x), jnp.zeros_like(x)], axis=0).astype(BF)
    sums = jnp.dot(pieces, ones, preferred_element_type=F32)
    return sums[0:8] + sums[8:16] + sums[16:24]


def rows8(x):
    return jnp.broadcast_to(x, (8, LANES))


def cell_rows(rows, pitch):
    index = lax.broadcasted_iota(jnp.int32, (rows, LANES), 0)
    row = (index * {10: 52429, 12: 43691}[pitch]) >> 19
    return row, index - row * pitch


def encode(out_ref, stats):
    lane = lane_in_group((8, LANES))
    row = jnp.zeros((8, LANES), F32)
    for block, mean, spread in stats:
        row = jnp.where(lane == block, mean, row)
        row = jnp.where(lane == block + 4, spread, row)
    out_ref[...] = jnp.broadcast_to(row[0:1][None], out_ref.shape)


def thirds(x):
    high = x.astype(BF).astype(F32)
    middle = (x - high).astype(BF).astype(F32)
    return high, middle, x - high - middle


def pack_stats(mean, spread):
    row = lax.broadcasted_iota(jnp.int32, mean.shape, 0)
    packed = jnp.zeros(mean.shape, F32)
    for k, piece in enumerate(thirds(mean) + thirds(spread)):
        packed = jnp.where(row == k, piece, packed)
    return packed.astype(BF)


def unpack_stats(packed):
    x = packed.astype(F32)
    return x[0:1] + x[1:2] + x[2:3], x[3:4] + x[4:5] + x[5:6]


def merge_stats(stats):
    scale = 1.0 / len(stats)
    middle = sum(mean for mean, _ in stats) * scale
    spread = sum(spread + (mean - middle) * (mean - middle) for mean, spread in stats) * scale
    return middle, spread


def all_rows(x):
    return jnp.broadcast_to(x, (8, x.shape[1]))


def channel_stats(x, keep, count):
    mean = jnp.sum(x, axis=0, keepdims=True) * (1.0 / count)
    deviation = x - mean
    if keep is not None:
        deviation = jnp.where(keep, deviation, 0.0)
    spread = jnp.sum(deviation * deviation, axis=0, keepdims=True) * (1.0 / count)
    return group_stats(mean, spread)


def group_stats(mean, spread):
    mean, spread = rows8(mean), rows8(spread)
    middle = segment_sum(mean) * (1.0 / 16)
    off = mean - middle
    return middle, segment_sum(spread + off * off) * (1.0 / 16)


def tile_stats(rows_ref):
    rows = rows_ref[...].reshape(rows_ref.shape[0], LANES)
    count = rows.shape[0]
    mean = jnp.sum(rows, axis=0, keepdims=True) * (1.0 / count)
    off = rows - mean
    between = jnp.sum(off * off, axis=0, keepdims=True) * (1.0 / count)
    return rows8(mean), rows8(between)


def block_stats(mean, between, block):
    lane = lane_in_group((8, LANES))
    middle = segment_sum(jnp.where(lane == block, mean, 0.0))
    spread = segment_sum(jnp.where(lane == block + 4, mean, jnp.where(lane == block, between, 0.0)))
    return middle[0:1], lax.rsqrt(spread[0:1] + EPS)


def decode(rows_ref, small_ref, at):
    mean, between = tile_stats(rows_ref)
    result = []
    for block in range(4):
        middle, inverse = block_stats(mean, between, block)
        gain, shift = gain_and_shift(small_ref, at, block)
        result.append((middle, inverse * gain, shift))
    return result


def gain_and_shift(small_ref, at, block):
    return small_ref[at + block : at + block + 1, :], small_ref[at + 4 + block : at + 5 + block, :]


def wide(small_ref, at):
    return jnp.concatenate([small_ref[at + b : at + b + 1, :] for b in range(4)], axis=1)


def silu(v):
    half = 0.5 * v
    return half + half * jnp.tanh(half)


def turned(ta, s):
    return ta ^ s


def first_kernel(latent_ref, out_ref):
    out_ref[...] = latent_ref[...]


def frame_moments_kernel(s0, s1, s2, s3, out_ref, outer_ref, inner_ref):
    slots = (s0, s1, s2, s3)
    stats = []
    for block in range(4):
        x = jnp.concatenate(
            [ref[:, block * LANES : (block + 1) * LANES].astype(F32) for ref in slots], axis=0
        )
        stats.append((block,) + channel_stats(x, None, x.shape[0]))
    encode(out_ref, stats)
    for s, ref in zip(SHIFTS, slots):
        start = 48 * lax.axis_index("core")
        outer_ref[s] = ref[pl.ds(pl.multiple_of(start, 16), 16), :]
        inner_ref[s] = ref[pl.ds(pl.multiple_of(48 - start, 16), 16), :]


def above_and_below(outer_ref, inner_ref, s, lanes):
    outer, inner = outer_ref[s, :, lanes].astype(F32), inner_ref[s, :, lanes].astype(F32)
    upper = lax.axis_index("core") == 0
    return jnp.where(upper, outer, inner), jnp.where(upper, inner, outer)


def columns_kernel(s0, s1, s2, s3, outer_rows, inner_rows, outer_ref, inner_ref, tall, sides):
    odd = lax.rem(lax.axis_index("z"), 2) == 1
    for s, ref in zip(SHIFTS, (s0, s1, s2, s3)):
        for b in range(4):
            lanes = slice(b * LANES, (b + 1) * LANES)
            tall[b, 0:16, :], tall[b, 80:96, :] = above_and_below(outer_rows, inner_rows, s, lanes)
            tall[b, 16:80, :] = ref[:, lanes].astype(F32)
            for k in range(2):
                for j in range(2):
                    sides[k, b, 12 * j : 12 * j + 12, :] = tall[b, pl.ds(j + 6 * k, 12, stride=8), :]
            first, last = sides[0, b], sides[1, b]
            outer_ref[s, :, lanes] = jnp.where(odd, last, first).astype(BF)
            inner_ref[s, :, lanes] = jnp.where(odd, first, last).astype(BF)


def activate_kernel(grid, hidden_ref, rows_ref, small_ref, out_ref):
    ta = lax.axis_index("ta")
    middle, inverse = block_stats(*tile_stats(rows_ref), 0)
    scale = inverse * small_ref[pl.ds(8 + ta, 1), :]
    shift = small_ref[pl.ds(12 + ta, 1), :]
    keep = inside(8 * lax.axis_index(HA) - 1, 8 * lax.axis_index("z") - 1, 104, 10, grid)
    for f in range(4):
        v = (hidden_ref[f].astype(F32) - middle) * scale + shift
        out_ref[f] = jnp.where(keep, silu(v), 0.0).astype(BF)


def residual_kernel(s0, s1, s2, s3, out_ref, parts):
    for s, ref in zip(SHIFTS, (s0, s1, s2, s3)):
        parts[turned(lax.axis_index("ta"), s)] = ref[...]
    out_ref[...] = jnp.concatenate([parts[b] for b in range(4)], axis=1)


def merge_kernel(*refs):
    slots, out_ref = refs[:-1], refs[-1]
    room = out_ref.shape[0] - 8
    middle, spread = merge_stats([unpack_stats(ref[64:72, :]) for ref in slots])
    for s in range(room // 64):
        out_ref[64 * s : 64 * s + 64, :] = slots[s][0:64, :]
    out_ref[room : room + 8, :] = pack_stats(all_rows(middle), all_rows(spread))


def convolve(lhs, weights, product, frame_rows, pitch, out_rows):
    for pair in PAIRS:
        rhs = jnp.concatenate(
            [jnp.concatenate([weights[9 * d + s] for s in pair], axis=1) for d in range(3)], axis=0
        )
        lane = pair[0] * LANES
        product[0 : 4 * frame_rows, lane : lane + rhs.shape[1]] = jnp.dot(
            lhs[...], rhs, preferred_element_type=F32
        )
    return shifted_sums(product, frame_rows, pitch, out_rows)


def shifted_sums(product, frame_rows, pitch, out_rows):
    totals = []
    for f in range(4):
        total = None
        for s in range(9):
            at = f * frame_rows + pitch * (s // 3) + s % 3
            piece = product[at : at + out_rows, s * LANES : (s + 1) * LANES]
            total = piece if total is None else total + piece
        totals.append(total)
    return totals


def inside(base_row, base_column, rows, pitch, grid):
    row, column = cell_rows(rows, pitch)
    row, column = row + base_row, column + base_column
    return (row >= 0) & (row < grid[0]) & (column >= 0) & (column < grid[1])


def rimmed_kernel(
    grid,
    s0,
    s1,
    s2,
    s3,
    outer_rows,
    inner_rows,
    outer_columns,
    inner_columns,
    rows_ref,
    small_ref,
    lhs_ref,
    own_ref,
    frames,
    tile,
    sides,
):
    ta = lax.axis_index("ta")
    odd = lax.rem(lax.axis_index("z"), 2) == 1
    coefficients = decode(rows_ref, small_ref, 0)
    keep = inside(8 * lax.axis_index(HA) - 2, 8 * lax.axis_index("z") - 2, 144, 12, grid)
    for s, ref in zip(SHIFTS, (s0, s1, s2, s3)):
        frames[turned(ta, s)] = ref[...]
    for frame in range(4):
        s = turned(ta, frame)
        own = jnp.zeros((64, LANES), F32)
        for b in range(4):
            lanes = slice(b * LANES, (b + 1) * LANES)
            middle = frames[frame, :, lanes].astype(F32)
            own = jnp.where(ta == b, middle, own)
            top, bottom = above_and_below(outer_rows, inner_rows, s, lanes)
            for r in range(12):
                if r < 2:
                    piece = top[8 * r : 8 * r + 8]
                elif r < 10:
                    piece = middle[8 * (r - 2) : 8 * (r - 2) + 8]
                else:
                    piece = bottom[8 * (r - 10) : 8 * (r - 10) + 8]
                tile[b, 12 * r + 2 : 12 * r + 10, :] = piece
            outer, inner = outer_columns[s, :, lanes].astype(F32), inner_columns[s, :, lanes].astype(F32)
            sides[0, b] = jnp.where(odd, inner, outer)
            sides[1, b] = jnp.where(odd, outer, inner)
            for k in range(2):
                for j in range(2):
                    tile[b, pl.ds(j + 10 * k, 12, stride=12), :] = sides[k, b, 12 * j : 12 * j + 12, :]
            mean, scale, shift = coefficients[b]
            v = (tile[b] - mean) * scale + shift
            act = jnp.where(keep, silu(v), 0.0).astype(BF)
            for f in range(4):
                for d in range(3):
                    if max(f + d - 2, 0) == frame:
                        lane = (4 * d + b) * LANES
                        lhs_ref[f * 144 : (f + 1) * 144, lane : lane + LANES] = act
        own_ref[frame] = own.astype(BF)


def first_conv_kernel(lhs, small_ref, kernel_ref, out_ref, moments_ref, product, wide_rows, tight_rows):
    totals = convolve(lhs, kernel_ref, product, 144, 12, 120)
    row, column = cell_rows(104, 10)
    keep = (row >= 1) & (row <= 8) & (column >= 1) & (column <= 8)
    bias = small_ref[36:37, :]
    kept = []
    for f in range(4):
        wide_rows[f] = totals[f] + bias
        for r in range(10):
            tight_rows[f, 10 * r : 10 * r + 10, :] = wide_rows[f, 12 * r : 12 * r + 10, :]
        tight_rows[f, 100:104, :] = jnp.zeros((4, LANES), F32)
        hidden = tight_rows[f].astype(BF)
        out_ref[f] = hidden
        kept.append(jnp.where(keep, hidden.astype(F32), 0.0))
    mean = sum(jnp.sum(x, axis=0, keepdims=True) for x in kept) * (1.0 / 256)
    squares = [jnp.square(jnp.where(keep, x - mean, 0.0)) for x in kept]
    spread = sum(jnp.sum(x, axis=0, keepdims=True) for x in squares) * (1.0 / 256)
    encode(moments_ref, [(0,) + group_stats(mean, spread)])


def add_blocks(refs, shifts, kernel_ref, lhs, product, before=None):
    ta = lax.axis_index("ta")
    for k, ref in enumerate(refs):
        for f in range(4):
            for d in range(3):
                lane = (len(refs) * d + k) * LANES
                lhs[f * 112 : f * 112 + 104, lane : lane + LANES] = ref[max(f + d - 2, 0)]
    for pair in PAIRS:
        rhs = jnp.concatenate(
            [
                jnp.concatenate(
                    [
                        kernel_ref[9 * d + s, pl.ds(pl.multiple_of(turned(ta, shift) * LANES, LANES), LANES), :]
                        for s in pair
                    ],
                    axis=1,
                )
                for d in range(3)
                for shift in shifts
            ],
            axis=0,
        )
        lanes = slice(pair[0] * LANES, pair[0] * LANES + rhs.shape[1])
        part = jnp.dot(lhs[...], rhs, preferred_element_type=F32)
        product[:, lanes] = part if before is None else before[:, lanes] + part


def second_conv_first_kernel(s0, s1, kernel_ref, out_ref, lhs):
    add_blocks((s0, s1), SHIFTS[:2], kernel_ref, lhs, out_ref)


def second_conv_kernel(
    s2,
    s3,
    before_ref,
    small_ref,
    own_ref,
    kernel_ref,
    out0,
    out1,
    out2,
    out3,
    lhs,
    product,
    wide_rows,
    parts,
):
    ta = lax.axis_index("ta")
    add_blocks((s2, s3), SHIFTS[2:], kernel_ref, lhs, product, before_ref)
    totals = shifted_sums(product, 112, 10, 80)
    bias = small_ref[37:38, :]
    tiles = []
    for f in range(4):
        wide_rows[f] = totals[f] + bias
        branch = jnp.concatenate([wide_rows[f, 10 * r : 10 * r + 8, :] for r in range(8)], axis=0)
        branch = branch.astype(BF).astype(F32)
        residual = (own_ref[f].astype(F32) + branch).astype(BF)
        parts[f] = residual
        tiles.append(residual.astype(F32))
    mean, spread = channel_stats(jnp.concatenate(tiles, axis=0), None, 256)
    packed = pack_stats(mean, spread)
    for s, ref in zip(SHIFTS, (out0, out1, out2, out3)):
        ref[0:64, :] = parts[turned(ta, s)]
        ref[64:72, :] = packed


def normalise(x, coefficients):
    parts = []
    for b, (mean, scale, shift) in enumerate(coefficients):
        part = x[:, b * LANES : (b + 1) * LANES].astype(F32)
        parts.append(((part - mean) * scale + shift).astype(BF))
    return jnp.concatenate(parts, axis=1)


def attention_kernel(*refs):
    asked, told = refs[:4], refs[4:6]
    small_ref, query_ref, key_ref = refs[6:9]
    outs, normed = refs[9:13], refs[13]
    middle, spread = merge_stats([unpack_stats(ref[512:520, :]) for ref in told])
    inverse = lax.rsqrt(spread + EPS)
    coefficients = []
    for b in range(4):
        lanes = slice(b * LANES, (b + 1) * LANES)
        gain, shift = gain_and_shift(small_ref, 16, b)
        coefficients.append((middle[:, lanes], inverse[:, lanes] * gain, shift))
    normed_q = normalise(jnp.concatenate([ref[0:64, :] for ref in asked], axis=0), coefficients)
    for k, ref in enumerate(told):
        normed[512 * k : 512 * k + 512, :] = normalise(ref[0:512, :], coefficients)
    queries = jnp.dot(normed_q, query_ref[...], preferred_element_type=F32) + wide(small_ref, 24)
    folded = lax.dot_general(
        queries.astype(BF), key_ref[...], (((1,), (1,)), ((), ())), preferred_element_type=F32
    ) * 512 ** (-0.5)
    scores = lax.dot_general(
        folded.astype(BF), normed[...], (((1,), (1,)), ((), ())), preferred_element_type=F32
    )
    highest = jnp.max(scores, axis=1, keepdims=True)
    weights = jnp.exp(scores - highest)
    total = jnp.sum(weights, axis=1, keepdims=True)
    mixed = jnp.dot(weights.astype(BF), normed[...], preferred_element_type=F32) * (1.0 / total)
    level = highest + jnp.log(total)
    top, middle, low = thirds(level)
    lane = lax.broadcasted_iota(jnp.int32, (256, LANES), 1)
    tail = jnp.where(lane == 0, top, jnp.where(lane == 1, middle, jnp.where(lane == 2, low, 0.0)))
    for s, ref in enumerate(outs):
        ref[:, 0:512] = mixed[64 * s : 64 * s + 64].astype(BF)
        ref[:, 512:640] = tail[64 * s : 64 * s + 64].astype(BF)


def finish_kernel(b0, b1, b2, b3, residual_ref, small_ref, value_ref, output_ref, out_ref):
    backs = [ref[...].astype(F32) for ref in (b0, b1, b2, b3)]
    levels = [jnp.sum(back[:, 512:640], axis=1, keepdims=True) for back in backs]
    highest = functools.reduce(jnp.maximum, levels)
    shares = [jnp.exp(level - highest) for level in levels]
    inverse = 1.0 / sum(shares)
    mean_normed = sum(back[:, 0:512] * (share * inverse) for back, share in zip(backs, shares))
    attended = jnp.dot(mean_normed.astype(BF), value_ref[...], preferred_element_type=F32)
    attended = (attended + wide(small_ref, 28)).astype(BF)
    mixed = jnp.dot(attended, output_ref[...], preferred_element_type=F32)
    out_ref[...] = (residual_ref[0:64, :].astype(F32) + mixed + wide(small_ref, 32)).astype(BF)


def call(kernel, out_shape, specs, scratch, flops, *args):
    shapes = out_shape if isinstance(out_shape, tuple) else (out_shape,)
    moved = sum(a.size * a.dtype.itemsize for a in args) + sum(
        s.size * jnp.dtype(s.dtype).itemsize for s in shapes
    )
    return pl.pallas_call(
        kernel,
        out_shape=out_shape,
        in_specs=specs,
        out_specs=tuple(VMEM for _ in shapes) if isinstance(out_shape, tuple) else VMEM,
        scratch_shapes=scratch,
        compiler_params=pltpu.CompilerParams(vmem_limit_bytes=LIMIT),
        cost_estimate=pl.CostEstimate(flops=flops, bytes_accessed=moved, transcendentals=0),
    )(*args)


def ring(count, step):
    return [(i, (i + step) % count) for i in range(count)]


def spread_out(blocks, axis):
    return [blocks[0]] + [
        lax.ppermute(block, axis, [(i, i ^ shift) for i in range(4)]) for block, shift in zip(blocks[1:], SHIFTS[1:])
    ]


def around(block, axis):
    return spread_out([block] * 4, axis)


def relayed(block, axis):
    count = lax.axis_size(axis)
    after = {step: lax.ppermute(block, axis, ring(count, step)) for step in (2, -2, 1, -1)}
    further = [lax.ppermute(after[step], axis, ring(count, move)) for step, move in ((2, 2), (2, 1), (-2, -1))]
    return [block, *after.values(), *further]


def both_sides(outer, inner, axis):
    across = [(i, (i + (1 if i % 2 else -1)) % 8) for i in range(8)]
    return lax.ppermute(outer, axis, across), lax.ppermute(inner, axis, [(i, i ^ 1) for i in range(8)])


def over_tiles(rows):
    return lax.all_to_all(rows, HA + ("z",), split_axis=0, concat_axis=0, tiled=True)


def body(
    latent,
    norm1_gain,
    norm1_shift,
    conv1_kernel,
    conv1_shift,
    norm2_gain,
    norm2_shift,
    conv2_kernel,
    conv2_shift,
    norm3_gain,
    norm3_shift,
    query_weight,
    query_shift,
    key_weight,
    value_weight,
    value_shift,
    output_weight,
    output_shift,
):
    _, height, width, channels = latent.shape
    cells = height * width
    tiles = lax.axis_size(HA) * lax.axis_size("z")
    grid = (lax.axis_size(HA) * height, lax.axis_size("z") * width)
    vectors = [norm1_gain, norm1_shift, norm2_gain, norm2_shift, norm3_gain, norm3_shift]
    vectors += [query_shift, value_shift, output_shift, conv1_shift, conv2_shift]
    small = jnp.concatenate(vectors).reshape(-1, LANES)

    def bf(*shape):
        return jax.ShapeDtypeStruct(shape, BF)

    rows = jax.ShapeDtypeStruct((tiles, 1, LANES), F32)

    slots = around(latent[0].reshape(cells, channels), "ta")
    slots[0] = call(first_kernel, bf(cells, channels), [VMEM], [], 4 * 10**9, slots[0])
    rows1, outer, inner = call(
        frame_moments_kernel, (rows, bf(4, 16, channels), bf(4, 16, channels)), [VMEM] * 4, [], 10**6, *slots
    )
    outer_rows, inner_rows = both_sides(outer, inner, HA)
    rows1 = over_tiles(rows1)
    outer, inner = call(
        columns_kernel,
        (bf(4, 24, channels), bf(4, 24, channels)),
        [VMEM] * 6,
        [pltpu.VMEM((4, 96, LANES), F32), pltpu.VMEM((2, 4, 24, LANES), F32)],
        10**6,
        *slots,
        outer_rows,
        inner_rows,
    )
    outer_columns, inner_columns = both_sides(outer, inner, "z")
    lhs, own = call(
        functools.partial(rimmed_kernel, grid),
        (bf(576, 1536), bf(4, cells, LANES)),
        [VMEM] * 10,
        [pltpu.VMEM((4, cells, channels), BF), pltpu.VMEM((4, 144, LANES), F32), pltpu.VMEM((2, 4, 24, LANES), F32)],
        4 * 10**9,
        *slots,
        outer_rows,
        inner_rows,
        outer_columns,
        inner_columns,
        rows1,
        small,
    )
    hidden, rows2 = call(
        first_conv_kernel,
        (bf(4, 104, LANES), rows),
        [VMEM] * 3,
        [
            pltpu.VMEM((584, 1152), F32),
            pltpu.VMEM((4, 120, LANES), F32),
            pltpu.VMEM((4, 104, LANES), F32),
        ],
        2 * 10**9,
        lhs,
        small,
        conv1_kernel,
    )

    act = call(
        functools.partial(activate_kernel, grid),
        bf(4, 104, LANES),
        [VMEM] * 3,
        [],
        4 * 10**9,
        hidden,
        over_tiles(rows2),
        small,
    )
    blocks = around(act, "ta")
    before = call(
        second_conv_first_kernel,
        jax.ShapeDtypeStruct((448, 1152), F32),
        [VMEM] * 3,
        [pltpu.VMEM((448, 768), BF)],
        10**9,
        *blocks[:2],
        conv2_kernel,
    )
    parts = call(
        second_conv_kernel,
        (bf(cells + 8, LANES),) * 4,
        [VMEM] * 6,
        [
            pltpu.VMEM((448, 768), BF),
            pltpu.VMEM((448, 1152), F32),
            pltpu.VMEM((4, 80, LANES), F32),
            pltpu.VMEM((4, cells, LANES), BF),
        ],
        2 * 10**9,
        *blocks[2:],
        before,
        small,
        own,
        conv2_kernel,
    )

    residual = call(
        residual_kernel,
        bf(cells + 8, channels),
        [VMEM] * 4,
        [pltpu.VMEM((4, cells + 8, LANES), BF)],
        10**6,
        *spread_out(parts, "ta"),
    )
    asked = around(residual, "y")
    told = call(merge_kernel, bf(cells + 8, channels), [VMEM] * 4, [], 10**6, *asked)
    told = call(merge_kernel, bf(8 * cells + 8, channels), [VMEM] * 8, [], 10**6, *relayed(told, "z"))
    packed = call(
        attention_kernel,
        (bf(cells, channels + LANES),) * 4,
        [VMEM] * 9,
        [pltpu.VMEM((1024, channels), BF)],
        10**9,
        *asked,
        told,
        lax.ppermute(told, "core", ring(2, 1)),
        small,
        query_weight,
        key_weight,
    )

    block_out = call(
        finish_kernel,
        bf(cells, channels),
        [VMEM] * 8,
        [],
        10**8,
        *spread_out(packed, "y"),
        residual,
        small,
        value_weight,
        output_weight,
    )
    return block_out.reshape(latent.shape)


def solution(mesh):
    frames, rows, columns = mesh.devices.shape
    split = Mesh(mesh.devices.reshape(frames, rows // 2, 2, columns), ("ta", "y", "core", "z"))
    tile = P("ta", HA, "z", None)
    kernel, shift = P(None, None, "ta"), P("ta")
    in_specs = (tile, P(), P(), kernel, shift, P(), P(), kernel, shift) + (P(),) * 9
    return jax.shard_map(body, mesh=split, in_specs=in_specs, out_specs=tile, check_vma=False)
```
